32 devices in a mesh: space: 8 (over y, x, core), tm: 4 (over z).
Axes of the slice: x: 2, y: 2, z: 4, core: 2. Of those that a mesh axis runs over, the one named last changes fastest.
Arguments:
- velocity: bfloat16 [3, 3072, 1024], P(None, 'space', 'tm'), may hold values from -6 to 6
- metric: float32 [3072], P('space'), may hold values from 0.5 to 2
Outputs:
- tiles: float32 [1024, 1024], P('tm', 'space')
The draws below stay inside these ranges and needn't reach their ends.
All inputs are finite; a program needn't handle non-finite values.
Results may differ from the reference program's by a relative error of at most 0.0016.
Values may be sent and summed in bfloat16 or wider, within the bound.
No kernel may reach another device: no remote copies, remote signals or barrier semaphores. Data moves between devices by JAX's collectives and lax.ppermute only.
A program may use at most 64 MiB of HBM per device.

```python
import math
import jax
import jax.numpy as jnp
from jax import lax

S = 256
CELLS = 3072
SNAPS = 1024
N_TM = 4


def raised(result, own_key, source, target, shards_of, factor):
    def block_of(axis_at):
        return (jnp.arange(result.shape[axis_at]) // (result.shape[axis_at] // shards_of)).reshape((-1,) + (1,) * (result.ndim - 1 - axis_at))

    first = jax.random.permutation(own_key, shards_of)[block_of(target)]
    second = (block_of(target) + shards_of // 2) % shards_of
    return jnp.where((block_of(source) == first) | (block_of(source) == second), factor * result, result)


def level_of(own_key, extent, cuts, least, high):
    factor_of = 1.0
    for dim, shards_of in cuts:
        draws = jax.random.uniform(jax.random.fold_in(jax.random.fold_in(own_key, 6), dim), (shards_of,), jnp.float32, least / len(cuts), high / len(cuts))
        factor_of = factor_of * jnp.repeat(jnp.exp(draws), extent[dim] // shards_of).reshape((-1,) + (1,) * (len(extent) - 1 - dim))
    return factor_of


def noise_with(rng, dims, spread, reach, pieces, heavy, kind=jnp.bfloat16):
    drawn = spread * jax.random.normal(rng, dims, jnp.float32)
    if pieces:
        drawn = drawn * level_of(rng, dims, pieces, -0.22, 0.18)
    return jnp.clip(raised(drawn, jax.random.fold_in(rng, 3), *heavy), -reach, reach).astype(kind)


def setup_inputs(seed: int = 0) -> dict:
    splits = jax.random.split(jax.random.key(seed), 3)
    return {
        "velocity": noise_with(splits[0], (3, CELLS, SNAPS), 1.0, 6.0, ((1, 8), (2, 4)), (1, 2, 8, 2.0)),
        "metric": jnp.clip(jnp.exp(math.log(2.0) - 1.3862944 * jax.random.uniform(splits[1], (CELLS,), jnp.float32) ** level_of(splits[1], (CELLS,), ((0, 8),), -0.2, 0.2)), 0.5, 2.0),
    }


def features(velocity, metric):
    field = velocity.astype(jnp.float32)
    padded = jnp.pad(field, ((0, 0), (1, 1), (0, 0)))
    gradient = metric[None, :, None] * (padded[:, 2:] - padded[:, :-2]) * 0.5
    helical = gradient[2] + field[0] * gradient[1] - field[1] * gradient[0]
    return jnp.stack([gradient[0], gradient[1], helical]).astype(jnp.bfloat16)

def reference(velocity, metric):
    snapshot_panel = features(velocity, metric)
    flattened = snapshot_panel.reshape(3 * CELLS, SNAPS).astype(jnp.float32)
    shifted = jnp.roll(flattened, -1, axis=1)
    products = jnp.dot(flattened.T.astype(jnp.float32), shifted.astype(jnp.float32), precision=lax.Precision.HIGHEST, preferred_element_type=jnp.float32)
    blocks = flattened.reshape(3 * CELLS, N_TM, S)
    gram_matrix = jnp.einsum('rgs,rgt->gst', blocks, blocks, precision=lax.Precision.HIGHEST)
    factor = jnp.linalg.cholesky(gram_matrix)
    grouped = products.reshape(N_TM, S, SNAPS)
    solved = lax.linalg.triangular_solve(factor, grouped, left_side=True, lower=True)
    return solved.reshape(SNAPS, SNAPS)
```

```python
import functools

import jax
import jax.numpy as jnp
from jax import lax
from jax.experimental import pallas as pl
from jax.experimental.pallas import tpu as pltpu
from jax.sharding import PartitionSpec as P

F32 = jnp.float32
BF16 = jnp.bfloat16
HIGHEST = lax.Precision.HIGHEST
VMEM = pl.BlockSpec(memory_space=pltpu.VMEM)
SMEM = pl.BlockSpec(memory_space=pltpu.SMEM)
LEAF = 64
PIVOTS = 4


def params(mib=40):
    return pltpu.CompilerParams(vmem_limit_bytes=mib * 1024 * 1024)


def cost(flops, moved):
    return pl.CostEstimate(flops=flops, bytes_accessed=moved, transcendentals=0)


def panel_kernel(vel_ref, lo_ref, hi_ref, met_ref, x_ref, xt_ref, g_ref):
    rows, cols = vel_ref.shape[1:]
    row = lax.broadcasted_iota(jnp.int32, (rows, cols), 0)
    metric = met_ref[...]

    def gradient(k):
        field = vel_ref[k].astype(F32)
        up = jnp.where(row == rows - 1, hi_ref[k].astype(F32), pltpu.roll(field, rows - 1, 0))
        down = jnp.where(row == 0, lo_ref[k].astype(F32), pltpu.roll(field, 1, 0))
        return metric * (up - down) * 0.5

    first = gradient(0)
    x_ref[0:rows] = first.astype(BF16)
    second = gradient(1)
    x_ref[rows : 2 * rows] = second.astype(BF16)
    third = gradient(2) + vel_ref[0].astype(F32) * second - vel_ref[1].astype(F32) * first
    x_ref[2 * rows :] = third.astype(BF16)
    xt_ref[...] = x_ref[...].T
    g_ref[...] = jnp.dot(xt_ref[...], x_ref[...], preferred_element_type=F32)


def panel(velocity, lo, hi, metric):
    _, rows, cols = velocity.shape
    return pl.pallas_call(
        panel_kernel,
        out_shape=(
            jax.ShapeDtypeStruct((3 * rows, cols), BF16),
            jax.ShapeDtypeStruct((cols, 3 * rows), BF16),
            jax.ShapeDtypeStruct((cols, cols), F32),
        ),
        in_specs=[VMEM] * 4,
        out_specs=(VMEM,) * 3,
        compiler_params=params(),
        cost_estimate=cost(2 * 3 * rows * cols * cols, 12 * rows * cols),
        name="panel",
    )(velocity, lo, hi, metric.reshape(rows, 1))


def leaf_inverse(block):
    n = block.shape[0]
    row = lax.broadcasted_iota(jnp.int32, (n, 2 * n), 0)
    lane = lax.broadcasted_iota(jnp.int32, (n, 2 * n), 1)
    eye = (row == lane).astype(F32)
    right = (lane == row + n).astype(F32)
    m = jnp.concatenate([block, right[:, n:]], axis=1)
    for j in range(0, n, PIVOTS):
        columns = [jnp.broadcast_to(m[:, j + b : j + b + 1], (n, 2 * n)) for b in range(PIVOTS)]
        pivot_rows = [m[j + a : j + a + 1, :] for a in range(PIVOTS)]
        splat = [[columns[b][j + a : j + a + 1, :] for b in range(PIVOTS)] for a in range(PIVOTS)]
        update = None
        inverses = []
        for a in range(PIVOTS):
            inverse = 1.0 / splat[a][a]
            for b in range(a + 1, PIVOTS):
                ratio = splat[a][b] * inverse
                for c in range(b, PIVOTS):
                    splat[b][c] = splat[b][c] - ratio * splat[a][c]
                pivot_rows[b] = pivot_rows[b] - ratio * pivot_rows[a]
            inverses.append(inverse)
        for a in range(PIVOTS):
            multiplier = jnp.where(row > j + a, columns[a] * inverses[a], 0.0)
            for b in range(a + 1, PIVOTS):
                columns[b] = columns[b] - multiplier * splat[a][b]
            term = multiplier * pivot_rows[a]
            update = term if update is None else update + term
        m = m - update
    diagonal = jnp.sum(m * eye, axis=1, keepdims=True)
    return m[:, n:] * lax.rsqrt(diagonal)


def mm(left, right, dims=((1,), (0,))):
    return lax.dot_general(left, right, (dims, ((), ())), precision=HIGHEST, preferred_element_type=F32)


def factor_kernel(g_ref, w_ref, a_ref, b_ref):
    n = g_ref.shape[0]
    a_ref[...] = g_ref[...]
    row = lax.broadcasted_iota(jnp.int32, (n, n), 0)
    lane = lax.broadcasted_iota(jnp.int32, (n, n), 1)
    b_ref[...] = (row == lane).astype(F32)
    for j in range(0, n, LEAF):
        k = j + LEAF
        own = slice(j, k)
        w = leaf_inverse(a_ref[own, own])
        done = mm(w, b_ref[own, :])
        w_ref[own, :] = done
        if k < n:
            u = mm(w, a_ref[own, :])
            a_ref[k:, :] -= mm(u[:, k:], u, ((0,), (0,)))
            b_ref[k:, :] -= mm(u[:, k:], done, ((0,), (0,)))


def inverse_factor(gram):
    n = gram.shape[0]
    return pl.pallas_call(
        factor_kernel,
        out_shape=jax.ShapeDtypeStruct((n, n), F32),
        in_specs=[VMEM],
        out_specs=VMEM,
        scratch_shapes=[pltpu.VMEM((n, n), F32)] * 2,
        compiler_params=params(),
        cost_estimate=cost(2 * n * n * n, 8 * n * n),
        name="factor",
    )(gram)


def blocks_kernel(count, pos_ref, xt_ref, *refs):
    panels, outs = refs[: count - 1], refs[count - 1 :]
    chip, group, core = pos_ref[0], pos_ref[1], pos_ref[2]
    for r in range(1, count):
        block = jnp.dot(xt_ref[...], panels[r - 1][...], preferred_element_type=F32)
        owner = group + jnp.where(core == 0, -r, r)
        for m in range(count):

            @pl.when(jnp.bitwise_xor(chip, m) == owner)
            def _(m=m, block=block):
                outs[m][...] = block


def blocks(pos, xt, panels):
    n = xt.shape[0]
    count = len(panels) + 1
    return pl.pallas_call(
        functools.partial(blocks_kernel, count),
        out_shape=(jax.ShapeDtypeStruct((n, n), F32),) * count,
        in_specs=[SMEM] + [VMEM] * count,
        out_specs=(VMEM,) * count,
        compiler_params=params(),
        cost_estimate=cost(2 * (count - 1) * n * n * xt.shape[1], 4 * count * n * n),
        name="blocks",
    )(pos, xt, *panels)


def total_kernel(pos_ref, *refs):
    count = len(refs) - 7
    parts = refs[:count]
    own_ref, sib_ref, low_ref, high_ref, top_t_ref, top_ref, st_ref = refs[count:]
    n = parts[0].shape[0]
    half = n // 2
    total = parts[0][...]
    for part in parts[1:]:
        total = total + part[...]
    low_ref[...] = total[: half + 8]
    high_ref[...] = total[half:]
    top_ref[...] = total[:8]
    st_ref[0:n] = total.T
    top_t_ref[...] = st_ref[0:8]
    core = pos_ref[2]
    own_ref[...] = st_ref[pl.ds(pl.multiple_of(core * half, 8), half + 8)]
    sib_ref[...] = st_ref[pl.ds(pl.multiple_of((1 - core) * half, 8), half + 8)]


def total(pos, parts):
    n = parts[0].shape[0]
    half = n // 2
    rows = (half + 8, half + 8, half + 8, half, 8, 8)
    return pl.pallas_call(
        total_kernel,
        out_shape=tuple(jax.ShapeDtypeStruct((r, n), F32) for r in rows),
        in_specs=[SMEM] + [VMEM] * len(parts),
        out_specs=(VMEM,) * 6,
        scratch_shapes=[pltpu.VMEM((n + 8, n), F32)],
        compiler_params=params(),
        name="total",
    )(pos, *parts)


def tiles_kernel(pos_ref, w_ref, g_ref, own_ref, sib_ref, low_ref, high_ref, top_t_ref, top_ref, out_ref, p_ref):
    count = pos_ref[3]
    chip, group, core = pos_ref[0], pos_ref[1], pos_ref[2]
    half = high_ref.shape[0]
    following = jnp.where(chip + 1 == count, 0, chip + 1)
    owner = jnp.where(chip < group, 0, 1)

    @pl.when(chip == group)
    def _():
        p_ref[0:half] = g_ref[pl.ds(pl.multiple_of(core * half, 8), half)]
        p_ref[half:] = g_ref[half : half + 8]

    @pl.when(chip != group)
    def _():
        slab = jnp.where(core == owner, own_ref[...], sib_ref[...])

        @pl.when(core == 0)
        def _():
            p_ref[...] = slab + low_ref[...]

        @pl.when(core != 0)
        def _():
            p_ref[0:half] = slab[:half] + high_ref[...]

    @pl.when(core != 0)
    def _():
        p_ref[half:] = jnp.where(following == group, g_ref[0:8], top_t_ref[...] + top_ref[...])

    shifted = pltpu.roll(p_ref[...], half + 7, 0)[:half]
    out_ref[...] = mm(w_ref[...], shifted, ((1,), (1,)))


def tiles(pos, w, gram, slabs):
    n = w.shape[0]
    half = n // 2
    return pl.pallas_call(
        tiles_kernel,
        out_shape=jax.ShapeDtypeStruct((n, half), F32),
        in_specs=[SMEM] + [VMEM] * 8,
        out_specs=VMEM,
        scratch_shapes=[pltpu.VMEM((half + 8, n), F32)],
        compiler_params=params(),
        name="tiles",
    )(pos, w, gram, *slabs)


def halos(velocity):
    count = lax.axis_size("space")
    head, tail = velocity[:, :1], velocity[:, -1:]
    lo = lax.ppermute(tail, "space", [(i, i + 1) for i in range(count - 1)])
    hi = lax.ppermute(head, "space", [(i + 1, i) for i in range(count - 1)])
    return lo, hi


def paired_body(velocity, metric):
    groups = lax.axis_size("tm")
    axes = ("space", "tm")
    every = range(groups)
    cores = (0, 1)

    def at(chip, group, core):
        return (2 * chip + core) * groups + group

    def send(value, pairs):
        return lax.ppermute(value, axes, pairs)

    space, group = lax.axis_index("space"), lax.axis_index("tm")
    core = space % 2
    pos = jnp.stack([space // 2, group, core, jnp.int32(groups)]).astype(jnp.int32)

    lo, hi = halos(velocity)
    x, xt, gram = panel(velocity, lo, hi, metric)

    n = gram.shape[0]
    half = n // 2
    siblings = [(at(k, z, c), at(k, z, 1 - c)) for k in every for z in every for c in cores]
    away = lax.dynamic_slice_in_dim(gram, (1 - core) * half, half, 0)
    mine = lax.dynamic_slice_in_dim(gram, core * half, half, 0)
    mine = mine + send(away, siblings)
    others = [
        send(mine, [(at(k, z, c), at(k ^ m, z, c)) for k in every for z in every for c in cores])
        for m in range(1, groups)
    ]
    for other in others:
        mine = mine + other
    theirs = send(mine, siblings)
    gram = jnp.where(core == 0, jnp.concatenate([mine, theirs]), jnp.concatenate([theirs, mine]))
    w = inverse_factor(gram)

    panels = []
    for r in range(1, groups):
        pairs = [(at(k, z, 0), at(k, z + r, 0)) for k in every for z in range(groups - r)]
        pairs += [(at(k, z, 1), at(k, z - r, 1)) for k in every for z in range(r, groups)]
        panels.append(send(x, pairs))
    parts = list(blocks(pos, xt, panels))
    for m in range(1, groups):
        pairs = []
        for z in every:
            for j in every:
                k = j ^ m
                if k != z:
                    c = 0 if k < z else 1
                    pairs.append((at(j, z, c), at(k, z, c)))
        parts[m] = send(parts[m], pairs)
    own, sib, low, high, top_t, top = total(pos, parts)

    owners = [(k, z, 0 if k < z else 1) for k in every for z in every if k != z]
    slabs = [
        own,
        send(sib, [(at(k, z, c), at(k, z, 1 - c)) for k, z, c in owners]),
        send(low, [(at(k, z, c), at(z, k, 0)) for k, z, c in owners]),
        send(high, [(at(k, z, c), at(z, k, 1)) for k, z, c in owners]),
        send(top_t, [(at(k, z, c), at((k - 1) % groups, z, 1)) for k, z, c in owners]),
        send(top, [(at(k, z, c), at((z - 1) % groups, k, 1)) for k, z, c in owners]),
    ]
    return tiles(pos, w, gram, slabs)


def general_body(velocity, metric):
    lo, hi = halos(velocity)
    x, xt, gram = panel(velocity, lo, hi, metric)
    w = inverse_factor(lax.psum(gram, "space"))
    count = lax.axis_size("tm")
    following = lax.ppermute(x[:, :1], "tm", [(i, (i - 1) % count) for i in range(count)])
    shifted = jnp.concatenate([x[:, 1:], following], axis=1)
    gathered = lax.all_gather(shifted, "tm", axis=1, tiled=True)
    partial = jnp.dot(xt, gathered, preferred_element_type=F32)
    summed = lax.psum_scatter(partial, "space", scatter_dimension=1, tiled=True)
    return mm(w, summed)


def solution(mesh):
    groups = mesh.shape["tm"]
    paired = mesh.shape["space"] == 2 * groups and groups & (groups - 1) == 0
    return jax.shard_map(
        paired_body if paired else general_body,
        mesh=mesh,
        in_specs=(P(None, "space", "tm"), P("space")),
        out_specs=P("tm", "space"),
        check_vma=False,
    )
```

```python
import functools

import jax
import jax.numpy as jnp
from jax import lax
from jax.experimental import pallas as pl
from jax.experimental.pallas import tpu as pltpu
from jax.sharding import PartitionSpec as P

F32 = jnp.float32
BF16 = jnp.bfloat16
HIGHEST = lax.Precision.HIGHEST
VMEM = pl.BlockSpec(memory_space=pltpu.VMEM)
SMEM = pl.BlockSpec(memory_space=pltpu.SMEM)
LEAF = 64
PIVOTS = 4


def params(mib=40):
    return pltpu.CompilerParams(vmem_limit_bytes=mib * 1024 * 1024)


def cost(flops, moved):
    return pl.CostEstimate(flops=flops, bytes_accessed=moved, transcendentals=0)


def panel_kernel(vel_ref, lo_ref, hi_ref, met_ref, x_ref, xt_ref, g_ref):
    rows, cols = vel_ref.shape[1:]
    row = lax.broadcasted_iota(jnp.int32, (rows, cols), 0)
    metric = met_ref[...]

    def gradient(k):
        field = vel_ref[k].astype(F32)
        up = jnp.where(row == rows - 1, hi_ref[k].astype(F32), pltpu.roll(field, rows - 1, 0))
        down = jnp.where(row == 0, lo_ref[k].astype(F32), pltpu.roll(field, 1, 0))
        return metric * (up - down) * 0.5

    first = gradient(0)
    x_ref[0:rows] = first.astype(BF16)
    second = gradient(1)
    x_ref[rows : 2 * rows] = second.astype(BF16)
    third = gradient(2) + vel_ref[0].astype(F32) * second - vel_ref[1].astype(F32) * first
    x_ref[2 * rows :] = third.astype(BF16)
    xt_ref[...] = x_ref[...].T
    g_ref[...] = jnp.dot(xt_ref[...], x_ref[...], preferred_element_type=F32)


def panel(velocity, lo, hi, metric):
    _, rows, cols = velocity.shape
    return pl.pallas_call(
        panel_kernel,
        out_shape=(
            jax.ShapeDtypeStruct((3 * rows, cols), BF16),
            jax.ShapeDtypeStruct((cols, 3 * rows), BF16),
            jax.ShapeDtypeStruct((cols, cols), F32),
        ),
        in_specs=[VMEM] * 4,
        out_specs=(VMEM,) * 3,
        compiler_params=params(),
        cost_estimate=cost(2 * 3 * rows * cols * cols, 12 * rows * cols),
        name="panel",
    )(velocity, lo, hi, metric.reshape(rows, 1))


def leaf_inverse(block):
    n = block.shape[0]
    row = lax.broadcasted_iota(jnp.int32, (n, 2 * n), 0)
    lane = lax.broadcasted_iota(jnp.int32, (n, 2 * n), 1)
    eye = (row == lane).astype(F32)
    right = (lane == row + n).astype(F32)
    m = jnp.concatenate([block, right[:, n:]], axis=1)
    for j in range(0, n, PIVOTS):
        columns = [jnp.broadcast_to(m[:, j + b : j + b + 1], (n, 2 * n)) for b in range(PIVOTS)]
        pivot_rows = [m[j + a : j + a + 1, :] for a in range(PIVOTS)]
        splat = [[columns[b][j + a : j + a + 1, :] for b in range(PIVOTS)] for a in range(PIVOTS)]
        update = None
        inverses = []
        for a in range(PIVOTS):
            inverse = 1.0 / splat[a][a]
            for b in range(a + 1, PIVOTS):
                ratio = splat[a][b] * inverse
                for c in range(b, PIVOTS):
                    splat[b][c] = splat[b][c] - ratio * splat[a][c]
                pivot_rows[b] = pivot_rows[b] - ratio * pivot_rows[a]
            inverses.append(inverse)
        for a in range(PIVOTS):
            multiplier = jnp.where(row > j + a, columns[a] * inverses[a], 0.0)
            for b in range(a + 1, PIVOTS):
                columns[b] = columns[b] - multiplier * splat[a][b]
            term = multiplier * pivot_rows[a]
            update = term if update is None else update + term
        m = m - update
    diagonal = jnp.sum(m * eye, axis=1, keepdims=True)
    return m[:, n:] * lax.rsqrt(diagonal)


def mm(left, right, dims=((1,), (0,))):
    return lax.dot_general(left, right, (dims, ((), ())), precision=HIGHEST, preferred_element_type=F32)


def factor_kernel(g_ref, w_ref, a_ref, b_ref):
    n = g_ref.shape[0]
    a_ref[...] = g_ref[...]
    row = lax.broadcasted_iota(jnp.int32, (n, n), 0)
    lane = lax.broadcasted_iota(jnp.int32, (n, n), 1)
    b_ref[...] = (row == lane).astype(F32)
    for j in range(0, n, LEAF):
        k = j + LEAF
        own = slice(j, k)
        w = leaf_inverse(a_ref[own, own])
        done = mm(w, b_ref[own, :])
        w_ref[own, :] = done
        if k < n:
            u = mm(w, a_ref[own, :])
            a_ref[k:, :] -= mm(u[:, k:], u, ((0,), (0,)))
            b_ref[k:, :] -= mm(u[:, k:], done, ((0,), (0,)))


def inverse_factor(gram):
    n = gram.shape[0]
    return pl.pallas_call(
        factor_kernel,
        out_shape=jax.ShapeDtypeStruct((n, n), F32),
        in_specs=[VMEM],
        out_specs=VMEM,
        scratch_shapes=[pltpu.VMEM((n, n), F32)] * 2,
        compiler_params=params(),
        cost_estimate=cost(2 * n * n * n, 8 * n * n),
        name="factor",
    )(gram)


def blocks_kernel(count, pos_ref, after_ref, xt_ref, *refs):
    del after_ref
    panels, outs = refs[: count - 1], refs[count - 1 :]
    chip, group, core = pos_ref[0], pos_ref[1], pos_ref[2]
    for r in range(1, count):
        block = jnp.dot(xt_ref[...], panels[r - 1][...], preferred_element_type=F32)
        owner = group + jnp.where(core == 0, -r, r)
        for m in range(count):

            @pl.when(jnp.bitwise_xor(chip, m) == owner)
            def _(m=m, block=block):
                outs[m][...] = block


def blocks(pos, after, xt, panels):
    n = xt.shape[0]
    count = len(panels) + 1
    return pl.pallas_call(
        functools.partial(blocks_kernel, count),
        out_shape=(jax.ShapeDtypeStruct((n, n), F32),) * count,
        in_specs=[SMEM, pl.BlockSpec(memory_space=pl.ANY)] + [VMEM] * count,
        out_specs=(VMEM,) * count,
        compiler_params=params(),
        cost_estimate=cost(2 * (count - 1) * n * n * xt.shape[1], 4 * count * n * n),
        name="blocks",
    )(pos, after, xt, *panels)


def total_kernel(pos_ref, *refs):
    count = len(refs) - 7
    parts = refs[:count]
    own_ref, sib_ref, low_ref, high_ref, top_t_ref, top_ref, st_ref = refs[count:]
    n = parts[0].shape[0]
    half = n // 2
    total = parts[0][...]
    for part in parts[1:]:
        total = total + part[...]
    low_ref[...] = total[: half + 8]
    high_ref[...] = total[half:]
    top_ref[...] = total[:8]
    st_ref[0:n] = total.T
    top_t_ref[...] = st_ref[0:8]
    core = pos_ref[2]
    own_ref[...] = st_ref[pl.ds(pl.multiple_of(core * half, 8), half + 8)]
    sib_ref[...] = st_ref[pl.ds(pl.multiple_of((1 - core) * half, 8), half + 8)]


def total(pos, parts):
    n = parts[0].shape[0]
    half = n // 2
    rows = (half + 8, half + 8, half + 8, half, 8, 8)
    return pl.pallas_call(
        total_kernel,
        out_shape=tuple(jax.ShapeDtypeStruct((r, n), F32) for r in rows),
        in_specs=[SMEM] + [VMEM] * len(parts),
        out_specs=(VMEM,) * 6,
        scratch_shapes=[pltpu.VMEM((n + 8, n), F32)],
        compiler_params=params(),
        name="total",
    )(pos, *parts)


def tiles_kernel(pos_ref, w_ref, g_ref, own_ref, sib_ref, low_ref, high_ref, top_t_ref, top_ref, out_ref, p_ref):
    count = pos_ref[3]
    chip, group, core = pos_ref[0], pos_ref[1], pos_ref[2]
    half = high_ref.shape[0]
    following = jnp.where(chip + 1 == count, 0, chip + 1)
    owner = jnp.where(chip < group, 0, 1)

    @pl.when(chip == group)
    def _():
        p_ref[0:half] = g_ref[pl.ds(pl.multiple_of(core * half, 8), half)]
        p_ref[half:] = g_ref[half : half + 8]

    @pl.when(chip != group)
    def _():
        slab = jnp.where(core == owner, own_ref[...], sib_ref[...])

        @pl.when(core == 0)
        def _():
            p_ref[...] = slab + low_ref[...]

        @pl.when(core != 0)
        def _():
            p_ref[0:half] = slab[:half] + high_ref[...]

    @pl.when(core != 0)
    def _():
        p_ref[half:] = jnp.where(following == group, g_ref[0:8], top_t_ref[...] + top_ref[...])

    shifted = pltpu.roll(p_ref[...], half + 7, 0)[:half]
    out_ref[...] = mm(w_ref[...], shifted, ((1,), (1,)))


def tiles(pos, w, gram, slabs):
    n = w.shape[0]
    half = n // 2
    return pl.pallas_call(
        tiles_kernel,
        out_shape=jax.ShapeDtypeStruct((n, half), F32),
        in_specs=[SMEM] + [VMEM] * 8,
        out_specs=VMEM,
        scratch_shapes=[pltpu.VMEM((half + 8, n), F32)],
        compiler_params=params(),
        name="tiles",
    )(pos, w, gram, *slabs)


def halos(velocity):
    count = lax.axis_size("space")
    head, tail = velocity[:, :1], velocity[:, -1:]
    lo = lax.ppermute(tail, "space", [(i, i + 1) for i in range(count - 1)])
    hi = lax.ppermute(head, "space", [(i + 1, i) for i in range(count - 1)])
    return lo, hi


def paired_body(velocity, metric):
    groups = lax.axis_size("tm")
    axes = ("space", "tm")
    every = range(groups)
    cores = (0, 1)

    def at(chip, group, core):
        return (2 * chip + core) * groups + group

    def send(value, pairs):
        return lax.ppermute(value, axes, pairs)

    space, group = lax.axis_index("space"), lax.axis_index("tm")
    core = space % 2
    pos = jnp.stack([space // 2, group, core, jnp.int32(groups)]).astype(jnp.int32)

    lo, hi = halos(velocity)
    x, xt, gram = panel(velocity, lo, hi, metric)

    n = gram.shape[0]
    half = n // 2
    siblings = [(at(k, z, c), at(k, z, 1 - c)) for k in every for z in every for c in cores]
    away = lax.dynamic_slice_in_dim(gram, (1 - core) * half, half, 0)
    mine = lax.dynamic_slice_in_dim(gram, core * half, half, 0)
    mine = mine + send(away, siblings)
    others = [
        send(mine, [(at(k, z, c), at(k ^ m, z, c)) for k in every for z in every for c in cores])
        for m in range(1, groups)
    ]
    for other in others:
        mine = mine + other
    theirs = send(mine, siblings)
    gram = jnp.where(core == 0, jnp.concatenate([mine, theirs]), jnp.concatenate([theirs, mine]))
    w = inverse_factor(gram)

    panels = []
    for r in range(1, groups):
        pairs = [(at(k, z, 0), at(k, z + r, 0)) for k in every for z in range(groups - r)]
        pairs += [(at(k, z, 1), at(k, z - r, 1)) for k in every for z in range(r, groups)]
        panels.append(send(x, pairs))
    parts = list(blocks(pos, w, xt, panels))
    for m in range(1, groups):
        pairs = []
        for z in every:
            for j in every:
                k = j ^ m
                if k != z:
                    c = 0 if k < z else 1
                    pairs.append((at(j, z, c), at(k, z, c)))
        parts[m] = send(parts[m], pairs)
    own, sib, low, high, top_t, top = total(pos, parts)

    owners = [(k, z, 0 if k < z else 1) for k in every for z in every if k != z]
    slabs = [
        own,
        send(sib, [(at(k, z, c), at(k, z, 1 - c)) for k, z, c in owners]),
        send(low, [(at(k, z, c), at(z, k, 0)) for k, z, c in owners]),
        send(high, [(at(k, z, c), at(z, k, 1)) for k, z, c in owners]),
        send(top_t, [(at(k, z, c), at((k - 1) % groups, z, 1)) for k, z, c in owners]),
        send(top, [(at(k, z, c), at((z - 1) % groups, k, 1)) for k, z, c in owners]),
    ]
    return tiles(pos, w, gram, slabs)


def general_body(velocity, metric):
    lo, hi = halos(velocity)
    x, xt, gram = panel(velocity, lo, hi, metric)
    w = inverse_factor(lax.psum(gram, "space"))
    count = lax.axis_size("tm")
    following = lax.ppermute(x[:, :1], "tm", [(i, (i - 1) % count) for i in range(count)])
    shifted = jnp.concatenate([x[:, 1:], following], axis=1)
    gathered = lax.all_gather(shifted, "tm", axis=1, tiled=True)
    partial = jnp.dot(xt, gathered, preferred_element_type=F32)
    summed = lax.psum_scatter(partial, "space", scatter_dimension=1, tiled=True)
    return mm(w, summed)


def solution(mesh):
    groups = mesh.shape["tm"]
    paired = mesh.shape["space"] == 2 * groups and groups & (groups - 1) == 0
    return jax.shard_map(
        paired_body if paired else general_body,
        mesh=mesh,
        in_specs=(P(None, "space", "tm"), P("space")),
        out_specs=P("tm", "space"),
        check_vma=False,
    )
```

```python
import functools

import jax
import jax.numpy as jnp
from jax import lax
from jax.experimental import pallas as pl
from jax.experimental.pallas import tpu as pltpu
from jax.sharding import PartitionSpec as P

F32 = jnp.float32
BF16 = jnp.bfloat16
HIGHEST = lax.Precision.HIGHEST
VMEM = pl.BlockSpec(memory_space=pltpu.VMEM)
SMEM = pl.BlockSpec(memory_space=pltpu.SMEM)
LEAF = 64
PIVOTS = 4


def params(mib=40):
    return pltpu.CompilerParams(vmem_limit_bytes=mib * 1024 * 1024)


def cost(flops, moved):
    return pl.CostEstimate(flops=flops, bytes_accessed=moved, transcendentals=0)


def panel_kernel(vel_ref, lo_ref, hi_ref, met_ref, x_ref, xt_ref, g_ref):
    rows, cols = vel_ref.shape[1:]
    row = lax.broadcasted_iota(jnp.int32, (rows, cols), 0)
    metric = met_ref[...]

    def gradient(k):
        field = vel_ref[k].astype(F32)
        up = jnp.where(row == rows - 1, hi_ref[k].astype(F32), pltpu.roll(field, rows - 1, 0))
        down = jnp.where(row == 0, lo_ref[k].astype(F32), pltpu.roll(field, 1, 0))
        return metric * (up - down) * 0.5

    first = gradient(0)
    x_ref[0:rows] = first.astype(BF16)
    second = gradient(1)
    x_ref[rows : 2 * rows] = second.astype(BF16)
    third = gradient(2) + vel_ref[0].astype(F32) * second - vel_ref[1].astype(F32) * first
    x_ref[2 * rows :] = third.astype(BF16)
    xt_ref[...] = x_ref[...].T
    g_ref[...] = jnp.dot(xt_ref[...], x_ref[...], preferred_element_type=F32)


def panel(velocity, lo, hi, metric):
    _, rows, cols = velocity.shape
    return pl.pallas_call(
        panel_kernel,
        out_shape=(
            jax.ShapeDtypeStruct((3 * rows, cols), BF16),
            jax.ShapeDtypeStruct((cols, 3 * rows), BF16),
            jax.ShapeDtypeStruct((cols, cols), F32),
        ),
        in_specs=[VMEM] * 4,
        out_specs=(VMEM,) * 3,
        compiler_params=params(),
        cost_estimate=cost(2 * 3 * rows * cols * cols, 12 * rows * cols),
        name="panel",
    )(velocity, lo, hi, metric.reshape(rows, 1))


def leaf_inverse(block):
    n = block.shape[0]
    row = lax.broadcasted_iota(jnp.int32, (n, 2 * n), 0)
    lane = lax.broadcasted_iota(jnp.int32, (n, 2 * n), 1)
    eye = (row == lane).astype(F32)
    right = (lane == row + n).astype(F32)
    m = jnp.concatenate([block, right[:, n:]], axis=1)
    for j in range(0, n, PIVOTS):
        columns = [jnp.broadcast_to(m[:, j + b : j + b + 1], (n, 2 * n)) for b in range(PIVOTS)]
        pivot_rows = [m[j + a : j + a + 1, :] for a in range(PIVOTS)]
        splat = [[columns[b][j + a : j + a + 1, :] for b in range(PIVOTS)] for a in range(PIVOTS)]
        update = None
        inverses = []
        for a in range(PIVOTS):
            inverse = 1.0 / splat[a][a]
            for b in range(a + 1, PIVOTS):
                ratio = splat[a][b] * inverse
                for c in range(b, PIVOTS):
                    splat[b][c] = splat[b][c] - ratio * splat[a][c]
                pivot_rows[b] = pivot_rows[b] - ratio * pivot_rows[a]
            inverses.append(inverse)
        for a in range(PIVOTS):
            multiplier = jnp.where(row > j + a, columns[a] * inverses[a], 0.0)
            for b in range(a + 1, PIVOTS):
                columns[b] = columns[b] - multiplier * splat[a][b]
            term = multiplier * pivot_rows[a]
            update = term if update is None else update + term
        m = m - update
    diagonal = jnp.sum(m * eye, axis=1, keepdims=True)
    return m[:, n:] * lax.rsqrt(diagonal)


def mm(left, right, dims=((1,), (0,))):
    return lax.dot_general(left, right, (dims, ((), ())), precision=HIGHEST, preferred_element_type=F32)


def factor_kernel(first, leaves, *refs):
    g_ref, w_in_ref = (refs[0], None) if first == 0 else refs[:2]
    a_ref, w_ref = refs[-2:]
    n = g_ref.shape[0]
    a_ref[...] = g_ref[...]
    if first == 0:
        row = lax.broadcasted_iota(jnp.int32, (n, n), 0)
        lane = lax.broadcasted_iota(jnp.int32, (n, n), 1)
        w_ref[...] = (row == lane).astype(F32)
    else:
        w_ref[...] = w_in_ref[...]
    for leaf in range(first, first + leaves):
        j = leaf * LEAF
        k = j + LEAF
        own = slice(j, k)
        w = leaf_inverse(a_ref[own, own])
        done = mm(w, w_ref[own, :])
        w_ref[own, :] = done
        if k < n:
            u = mm(w, a_ref[own, :])
            a_ref[k:, :] -= mm(u[:, k:], u, ((0,), (0,)))
            w_ref[k:, :] -= mm(u[:, k:], done, ((0,), (0,)))


def factor_part(first, leaves, state, after=()):
    n = state[0].shape[0]
    skip = len(after)

    def kernel(*refs):
        factor_kernel(first, leaves, *refs[: len(state)], *refs[len(state) + skip :])

    return pl.pallas_call(
        kernel,
        out_shape=(jax.ShapeDtypeStruct((n, n), F32),) * 2,
        in_specs=[VMEM] * len(state) + [pl.BlockSpec(memory_space=pl.ANY)] * skip,
        out_specs=(VMEM,) * 2,
        compiler_params=params(),
        cost_estimate=cost(2 * n * n * n, 8 * n * n),
        name="factor",
    )(*state, *after)


def inverse_factor(gram):
    return factor_part(0, gram.shape[0] // LEAF, (gram,))[1]


def blocks_kernel(pos_ref, after_ref, xt_ref, near_ref, far_ref, swap_ref, *outs):
    del after_ref
    chip, group, core = pos_ref[0], pos_ref[1], pos_ref[2]
    count = len(outs)

    def store(block, owner):
        for m in range(count):

            @pl.when(jnp.bitwise_xor(chip, m) == owner)
            def _(m=m):
                outs[m][...] = block

    for r, panel_ref in ((1, near_ref), (2, far_ref)):
        owner = group + jnp.where(core == 0, -r, r)

        @pl.when((owner >= 0) & (owner < count))
        def _(panel_ref=panel_ref, owner=owner):
            store(jnp.dot(xt_ref[...], panel_ref[...], preferred_element_type=F32), owner)

    @pl.when(group == jnp.where(core == 0, 2, 1))
    def _():
        dims = (((0,), (0,)), ((), ()))
        store(lax.dot_general(swap_ref[...], far_ref[...], dims, preferred_element_type=F32), group)


def blocks(pos, after, xt, near, far, swap, count):
    n = xt.shape[0]
    return pl.pallas_call(
        blocks_kernel,
        out_shape=(jax.ShapeDtypeStruct((n, n), F32),) * count,
        in_specs=[SMEM, pl.BlockSpec(memory_space=pl.ANY)] + [VMEM] * 4,
        out_specs=(VMEM,) * count,
        compiler_params=params(),
        cost_estimate=cost(2 * 3 * n * n * xt.shape[1], 4 * count * n * n),
        name="blocks",
    )(pos, after, xt, near, far, swap)


def total_kernel(pos_ref, after_ref, *refs):
    del after_ref
    count = len(refs) - 7
    parts = refs[:count]
    own_ref, sib_ref, low_ref, high_ref, top_t_ref, top_ref, st_ref = refs[count:]
    n = parts[0].shape[0]
    half = n // 2
    total = parts[0][...]
    for part in parts[1:]:
        total = total + part[...]
    low_ref[...] = total[: half + 8]
    high_ref[...] = total[half:]
    top_ref[...] = total[:8]
    st_ref[0:n] = total.T
    top_t_ref[...] = st_ref[0:8]
    core = pos_ref[2]
    own_ref[...] = st_ref[pl.ds(pl.multiple_of(core * half, 8), half + 8)]
    sib_ref[...] = st_ref[pl.ds(pl.multiple_of((1 - core) * half, 8), half + 8)]


def total(pos, after, parts):
    n = parts[0].shape[0]
    half = n // 2
    rows = (half + 8, half + 8, half + 8, half, 8, 8)
    return pl.pallas_call(
        total_kernel,
        out_shape=tuple(jax.ShapeDtypeStruct((r, n), F32) for r in rows),
        in_specs=[SMEM, pl.BlockSpec(memory_space=pl.ANY)] + [VMEM] * len(parts),
        out_specs=(VMEM,) * 6,
        scratch_shapes=[pltpu.VMEM((n + 8, n), F32)],
        compiler_params=params(),
        name="total",
    )(pos, after, *parts)


def tiles_kernel(pos_ref, w_ref, g_ref, own_ref, moved_ref, sib_ref, low_ref, high_ref, top_t_ref, top_ref, out_ref, p_ref):
    count = pos_ref[3]
    chip, group, core = pos_ref[0], pos_ref[1], pos_ref[2]
    half = high_ref.shape[0]
    following = jnp.where(chip + 1 == count, 0, chip + 1)
    owner = jnp.where(chip < group, 0, 1)

    @pl.when(chip == group)
    def _():
        p_ref[0:half] = g_ref[pl.ds(pl.multiple_of(core * half, 8), half)]
        p_ref[half:] = g_ref[half : half + 8]

    @pl.when(chip != group)
    def _():
        direct = jnp.where(jnp.abs(chip - group) == 3, moved_ref[...], own_ref[...])
        slab = jnp.where(core == owner, direct, sib_ref[...])

        @pl.when(core == 0)
        def _():
            p_ref[...] = slab + low_ref[...]

        @pl.when(core != 0)
        def _():
            p_ref[0:half] = slab[:half] + high_ref[...]

    @pl.when(core != 0)
    def _():
        p_ref[half:] = jnp.where(following == group, g_ref[0:8], top_t_ref[...] + top_ref[...])

    shifted = pltpu.roll(p_ref[...], half + 7, 0)[:half]
    out_ref[...] = mm(w_ref[...], shifted, ((1,), (1,)))


def tiles(pos, w, gram, slabs):
    n = w.shape[0]
    half = n // 2
    return pl.pallas_call(
        tiles_kernel,
        out_shape=jax.ShapeDtypeStruct((n, half), F32),
        in_specs=[SMEM] + [VMEM] * 9,
        out_specs=VMEM,
        scratch_shapes=[pltpu.VMEM((half + 8, n), F32)],
        compiler_params=params(),
        name="tiles",
    )(pos, w, gram, *slabs)


def halos(velocity):
    count = lax.axis_size("space")
    head, tail = velocity[:, :1], velocity[:, -1:]
    lo = lax.ppermute(tail, "space", [(i, i + 1) for i in range(count - 1)])
    hi = lax.ppermute(head, "space", [(i + 1, i) for i in range(count - 1)])
    return lo, hi


def paired_body(velocity, metric):
    groups = lax.axis_size("tm")
    axes = ("space", "tm")
    every = range(groups)
    cores = (0, 1)

    def at(chip, group, core):
        return (2 * chip + core) * groups + group

    def send(value, pairs):
        return lax.ppermute(value, axes, pairs)

    space, group = lax.axis_index("space"), lax.axis_index("tm")
    core = space % 2
    pos = jnp.stack([space // 2, group, core, jnp.int32(groups)]).astype(jnp.int32)

    lo, hi = halos(velocity)
    x, xt, gram = panel(velocity, lo, hi, metric)

    n = gram.shape[0]
    half = n // 2
    siblings = [(at(k, z, c), at(k, z, 1 - c)) for k in every for z in every for c in cores]
    away = lax.dynamic_slice_in_dim(gram, (1 - core) * half, half, 0)
    mine = lax.dynamic_slice_in_dim(gram, core * half, half, 0)
    mine = mine + send(away, siblings)
    others = [
        send(mine, [(at(k, z, c), at(k ^ m, z, c)) for k in every for z in every for c in cores])
        for m in range(1, groups)
    ]
    for other in others:
        mine = mine + other
    theirs = send(mine, siblings)
    gram = jnp.where(core == 0, jnp.concatenate([mine, theirs]), jnp.concatenate([theirs, mine]))
    state = factor_part(0, n // LEAF // 2, (gram,))

    def hops(group_pairs):
        pairs = [(at(k, z, 0), at(k, t, 0)) for k in every for z, t in group_pairs]
        return pairs + [(at(k, 3 - z, 1), at(k, 3 - t, 1)) for k in every for z, t in group_pairs]

    near = send(x, hops([(0, 1), (1, 2), (2, 3)]))
    far = send(near, hops([(1, 2), (2, 3)]))
    swap = send(x, hops([(3, 2)]))
    parts = list(blocks(pos, state[0], xt, near, far, swap, groups))
    w = factor_part(n // LEAF // 2, n // LEAF - n // LEAF // 2, state, (parts[0],))[1]

    owners = {(k, z): (k, z, 0 if k < z else 1) for k in every for z in every if k != z}
    owners[0, 3] = (2, 2, 0)
    owners[3, 0] = (1, 1, 1)
    for m in range(1, groups):
        parts[m] = send(parts[m], [(at(k ^ m, z, c), at(k, z, c)) for k, z, c in owners.values()])
    own, sib, low, high, top_t, top = total(pos, w, parts)

    def deliver(value, target):
        return send(value, [(at(*o), at(*target(k, z))) for (k, z), o in owners.items()])

    def first_core(k, z):
        return 0 if k < z else 1

    slabs = [
        own,
        send(own, [(at(*owners[p]), at(*p, first_core(*p))) for p in ((0, 3), (3, 0))]),
        deliver(sib, lambda k, z: (k, z, 1 - first_core(k, z))),
        deliver(low, lambda k, z: (z, k, 0)),
        deliver(high, lambda k, z: (z, k, 1)),
        deliver(top_t, lambda k, z: ((k - 1) % groups, z, 1)),
        deliver(top, lambda k, z: ((z - 1) % groups, k, 1)),
    ]
    return tiles(pos, w, gram, slabs)


def general_body(velocity, metric):
    lo, hi = halos(velocity)
    x, xt, gram = panel(velocity, lo, hi, metric)
    w = inverse_factor(lax.psum(gram, "space"))
    count = lax.axis_size("tm")
    following = lax.ppermute(x[:, :1], "tm", [(i, (i - 1) % count) for i in range(count)])
    shifted = jnp.concatenate([x[:, 1:], following], axis=1)
    gathered = lax.all_gather(shifted, "tm", axis=1, tiled=True)
    partial = jnp.dot(xt, gathered, preferred_element_type=F32)
    summed = lax.psum_scatter(partial, "space", scatter_dimension=1, tiled=True)
    return mm(w, summed)


def solution(mesh):
    groups = mesh.shape["tm"]
    paired = groups == 4 and mesh.shape["space"] == 8
    return jax.shard_map(
        paired_body if paired else general_body,
        mesh=mesh,
        in_specs=(P(None, "space", "tm"), P("space")),
        out_specs=P("tm", "space"),
        check_vma=False,
    )
```

```python
import functools

import jax
import jax.numpy as jnp
from jax import lax
from jax.experimental import pallas as pl
from jax.experimental.pallas import tpu as pltpu
from jax.sharding import PartitionSpec as P

F32 = jnp.float32
BF16 = jnp.bfloat16
HIGHEST = lax.Precision.HIGHEST
VMEM = pl.BlockSpec(memory_space=pltpu.VMEM)
SMEM = pl.BlockSpec(memory_space=pltpu.SMEM)
LEAF = 64
PIVOTS = 4


def params(mib=40):
    return pltpu.CompilerParams(vmem_limit_bytes=mib * 1024 * 1024)


def cost(flops, moved):
    return pl.CostEstimate(flops=flops, bytes_accessed=moved, transcendentals=0)


def panel_kernel(vel_ref, lo_ref, hi_ref, met_ref, x_ref, xt_ref, g_ref):
    rows, cols = vel_ref.shape[1:]
    row = lax.broadcasted_iota(jnp.int32, (rows, cols), 0)
    metric = met_ref[...]

    def gradient(k):
        field = vel_ref[k].astype(F32)
        up = jnp.where(row == rows - 1, hi_ref[k].astype(F32), pltpu.roll(field, rows - 1, 0))
        down = jnp.where(row == 0, lo_ref[k].astype(F32), pltpu.roll(field, 1, 0))
        return metric * (up - down) * 0.5

    first = gradient(0)
    x_ref[0:rows] = first.astype(BF16)
    second = gradient(1)
    x_ref[rows : 2 * rows] = second.astype(BF16)
    third = gradient(2) + vel_ref[0].astype(F32) * second - vel_ref[1].astype(F32) * first
    x_ref[2 * rows :] = third.astype(BF16)
    xt_ref[...] = x_ref[...].T
    g_ref[...] = jnp.dot(xt_ref[...], x_ref[...], preferred_element_type=F32)


def panel(velocity, lo, hi, metric):
    _, rows, cols = velocity.shape
    return pl.pallas_call(
        panel_kernel,
        out_shape=(
            jax.ShapeDtypeStruct((3 * rows, cols), BF16),
            jax.ShapeDtypeStruct((cols, 3 * rows), BF16),
            jax.ShapeDtypeStruct((cols, cols), F32),
        ),
        in_specs=[VMEM] * 4,
        out_specs=(VMEM,) * 3,
        compiler_params=params(),
        cost_estimate=cost(2 * 3 * rows * cols * cols, 12 * rows * cols),
        name="panel",
    )(velocity, lo, hi, metric.reshape(rows, 1))


def leaf_inverse(block):
    n = block.shape[0]
    row = lax.broadcasted_iota(jnp.int32, (n, 2 * n), 0)
    lane = lax.broadcasted_iota(jnp.int32, (n, 2 * n), 1)
    eye = (row == lane).astype(F32)
    right = (lane == row + n).astype(F32)
    m = jnp.concatenate([block, right[:, n:]], axis=1)
    for j in range(0, n, PIVOTS):
        columns = [jnp.broadcast_to(m[:, j + b : j + b + 1], (n, 2 * n)) for b in range(PIVOTS)]
        pivot_rows = [m[j + a : j + a + 1, :] for a in range(PIVOTS)]
        splat = [[columns[b][j + a : j + a + 1, :] for b in range(PIVOTS)] for a in range(PIVOTS)]
        update = None
        inverses = []
        for a in range(PIVOTS):
            inverse = 1.0 / splat[a][a]
            for b in range(a + 1, PIVOTS):
                ratio = splat[a][b] * inverse
                for c in range(b, PIVOTS):
                    splat[b][c] = splat[b][c] - ratio * splat[a][c]
                pivot_rows[b] = pivot_rows[b] - ratio * pivot_rows[a]
            inverses.append(inverse)
        for a in range(PIVOTS):
            multiplier = jnp.where(row > j + a, columns[a] * inverses[a], 0.0)
            for b in range(a + 1, PIVOTS):
                columns[b] = columns[b] - multiplier * splat[a][b]
            term = multiplier * pivot_rows[a]
            update = term if update is None else update + term
        m = m - update
    diagonal = jnp.sum(m * eye, axis=1, keepdims=True)
    return m[:, n:] * lax.rsqrt(diagonal)


def mm(left, right, dims=((1,), (0,))):
    return lax.dot_general(left, right, (dims, ((), ())), precision=HIGHEST, preferred_element_type=F32)


def factor_kernel(first, leaves, *refs):
    g_ref, w_in_ref = (refs[0], None) if first == 0 else refs[:2]
    a_ref, w_ref = refs[-2:]
    n = g_ref.shape[0]
    a_ref[...] = g_ref[...]
    if first == 0:
        row = lax.broadcasted_iota(jnp.int32, (n, n), 0)
        lane = lax.broadcasted_iota(jnp.int32, (n, n), 1)
        w_ref[...] = (row == lane).astype(F32)
    else:
        w_ref[...] = w_in_ref[...]
    for leaf in range(first, first + leaves):
        j = leaf * LEAF
        k = j + LEAF
        own = slice(j, k)
        w = leaf_inverse(a_ref[own, own])
        done = mm(w, w_ref[own, :])
        w_ref[own, :] = done
        if k < n:
            u = mm(w, a_ref[own, :])
            a_ref[k:, :] -= mm(u[:, k:], u, ((0,), (0,)))
            w_ref[k:, :] -= mm(u[:, k:], done, ((0,), (0,)))


def factor_part(first, leaves, state, after=()):
    n = state[0].shape[0]
    skip = len(after)

    def kernel(*refs):
        factor_kernel(first, leaves, *refs[: len(state)], *refs[len(state) + skip :])

    return pl.pallas_call(
        kernel,
        out_shape=(jax.ShapeDtypeStruct((n, n), F32),) * 2,
        in_specs=[VMEM] * len(state) + [pl.BlockSpec(memory_space=pl.ANY)] * skip,
        out_specs=(VMEM,) * 2,
        compiler_params=params(),
        cost_estimate=cost(2 * n * n * n, 8 * n * n),
        name="factor",
    )(*state, *after)


def inverse_factor(gram):
    return factor_part(0, gram.shape[0] // LEAF, (gram,))[1]


def blocks_kernel(pos_ref, after_ref, xt_ref, near_ref, far_ref, swap_ref, *outs):
    del after_ref
    chip, group, core = pos_ref[0], pos_ref[1], pos_ref[2]
    count = len(outs)

    def store(block, owner):
        for m in range(count):

            @pl.when(jnp.bitwise_xor(chip, m) == owner)
            def _(m=m):
                outs[m][...] = block

    for r, panel_ref in ((1, near_ref), (2, far_ref)):
        owner = group + jnp.where(core == 0, -r, r)

        @pl.when((owner >= 0) & (owner < count))
        def _(panel_ref=panel_ref, owner=owner):
            store(jnp.dot(xt_ref[...], panel_ref[...], preferred_element_type=F32), owner)

    @pl.when(group == jnp.where(core == 0, 2, 1))
    def _():
        dims = (((0,), (0,)), ((), ()))
        store(lax.dot_general(swap_ref[...], far_ref[...], dims, preferred_element_type=F32), group)


def blocks(pos, after, xt, near, far, swap, count):
    n = xt.shape[0]
    return pl.pallas_call(
        blocks_kernel,
        out_shape=(jax.ShapeDtypeStruct((n, n), F32),) * count,
        in_specs=[SMEM, pl.BlockSpec(memory_space=pl.ANY)] + [VMEM] * 4,
        out_specs=(VMEM,) * count,
        compiler_params=params(),
        cost_estimate=cost(2 * 3 * n * n * xt.shape[1], 4 * count * n * n),
        name="blocks",
    )(pos, after, xt, near, far, swap)


def total_kernel(pos_ref, after_ref, *refs):
    del after_ref
    count = len(refs) - 7
    parts = refs[:count]
    own_ref, sib_ref, low_ref, high_ref, top_t_ref, top_ref, st_ref = refs[count:]
    n = parts[0].shape[0]
    half = n // 2
    total = parts[0][...]
    for part in parts[1:]:
        total = total + part[...]
    low_ref[...] = total[: half + 8]
    high_ref[...] = total[half:]
    top_ref[...] = total[:8]
    st_ref[0:n] = total.T
    top_t_ref[...] = st_ref[0:8]
    core = pos_ref[2]
    own_ref[...] = st_ref[pl.ds(pl.multiple_of(core * half, 8), half + 8)]
    sib_ref[...] = st_ref[pl.ds(pl.multiple_of((1 - core) * half, 8), half + 8)]


def total(pos, after, parts):
    n = parts[0].shape[0]
    half = n // 2
    rows = (half + 8, half + 8, half + 8, half, 8, 8)
    return pl.pallas_call(
        total_kernel,
        out_shape=tuple(jax.ShapeDtypeStruct((r, n), F32) for r in rows),
        in_specs=[SMEM, pl.BlockSpec(memory_space=pl.ANY)] + [VMEM] * len(parts),
        out_specs=(VMEM,) * 6,
        scratch_shapes=[pltpu.VMEM((n + 8, n), F32)],
        compiler_params=params(),
        name="total",
    )(pos, after, *parts)


def tiles_kernel(pos_ref, w_ref, g_ref, own_ref, moved_ref, sib_ref, low_ref, high_ref, top_t_ref, top_ref, out_ref, p_ref):
    count = pos_ref[3]
    chip, group, core = pos_ref[0], pos_ref[1], pos_ref[2]
    half = high_ref.shape[0]
    following = jnp.where(chip + 1 == count, 0, chip + 1)
    owner = jnp.where(chip < group, 0, 1)

    @pl.when(chip == group)
    def _():
        p_ref[0:half] = g_ref[pl.ds(pl.multiple_of(core * half, 8), half)]
        p_ref[half:] = g_ref[half : half + 8]

    @pl.when(chip != group)
    def _():
        direct = jnp.where(jnp.abs(chip - group) == 3, moved_ref[...], own_ref[...])
        slab = jnp.where(core == owner, direct, sib_ref[...])

        @pl.when(core == 0)
        def _():
            p_ref[...] = slab + low_ref[...]

        @pl.when(core != 0)
        def _():
            p_ref[0:half] = slab[:half] + high_ref[...]

    @pl.when(core != 0)
    def _():
        p_ref[half:] = jnp.where(following == group, g_ref[0:8], top_t_ref[...] + top_ref[...])

    shifted = pltpu.roll(p_ref[...], half + 7, 0)[:half]
    out_ref[...] = mm(w_ref[...], shifted, ((1,), (1,)))


def tiles(pos, w, gram, slabs):
    n = w.shape[0]
    half = n // 2
    return pl.pallas_call(
        tiles_kernel,
        out_shape=jax.ShapeDtypeStruct((n, half), F32),
        in_specs=[SMEM] + [VMEM] * 9,
        out_specs=VMEM,
        scratch_shapes=[pltpu.VMEM((half + 8, n), F32)],
        compiler_params=params(),
        name="tiles",
    )(pos, w, gram, *slabs)


def halos(velocity):
    count = lax.axis_size("space")
    head, tail = velocity[:, :1], velocity[:, -1:]
    lo = lax.ppermute(tail, "space", [(i, i + 1) for i in range(count - 1)])
    hi = lax.ppermute(head, "space", [(i + 1, i) for i in range(count - 1)])
    return lo, hi


def paired_body(velocity, metric):
    groups = lax.axis_size("tm")
    axes = ("space", "tm")
    every = range(groups)
    cores = (0, 1)

    def at(chip, group, core):
        return (2 * chip + core) * groups + group

    def send(value, pairs):
        return lax.ppermute(value, axes, pairs)

    space, group = lax.axis_index("space"), lax.axis_index("tm")
    core = space % 2
    pos = jnp.stack([space // 2, group, core, jnp.int32(groups)]).astype(jnp.int32)

    lo, hi = halos(velocity)
    x, xt, gram = panel(velocity, lo, hi, metric)

    n = gram.shape[0]
    devices = 2 * groups
    shares = lax.all_to_all(gram, "space", 0, 0, tiled=True)
    mine = jnp.sum(shares.reshape(devices, n // devices, n), axis=0)
    gram = lax.all_to_all(jnp.tile(mine, (devices, 1)), "space", 0, 0, tiled=True)
    state = factor_part(0, n // LEAF // 2, (gram,))

    def hops(group_pairs):
        pairs = [(at(k, z, 0), at(k, t, 0)) for k in every for z, t in group_pairs]
        return pairs + [(at(k, 3 - z, 1), at(k, 3 - t, 1)) for k in every for z, t in group_pairs]

    near = send(x, hops([(0, 1), (1, 2), (2, 3)]))
    far = send(near, hops([(1, 2), (2, 3)]))
    swap = send(x, hops([(3, 2)]))
    parts = list(blocks(pos, state[0], xt, near, far, swap, groups))
    w = factor_part(n // LEAF // 2, n // LEAF - n // LEAF // 2, state, (parts[0],))[1]

    owners = {(k, z): (k, z, 0 if k < z else 1) for k in every for z in every if k != z}
    owners[0, 3] = (2, 2, 0)
    owners[3, 0] = (1, 1, 1)
    for m in range(1, groups):
        parts[m] = send(parts[m], [(at(k ^ m, z, c), at(k, z, c)) for k, z, c in owners.values()])
    own, sib, low, high, top_t, top = total(pos, w, parts)

    def deliver(value, target):
        return send(value, [(at(*o), at(*target(k, z))) for (k, z), o in owners.items()])

    def first_core(k, z):
        return 0 if k < z else 1

    slabs = [
        own,
        send(own, [(at(*owners[p]), at(*p, first_core(*p))) for p in ((0, 3), (3, 0))]),
        deliver(sib, lambda k, z: (k, z, 1 - first_core(k, z))),
        deliver(low, lambda k, z: (z, k, 0)),
        deliver(high, lambda k, z: (z, k, 1)),
        deliver(top_t, lambda k, z: ((k - 1) % groups, z, 1)),
        deliver(top, lambda k, z: ((z - 1) % groups, k, 1)),
    ]
    return tiles(pos, w, gram, slabs)


def general_body(velocity, metric):
    lo, hi = halos(velocity)
    x, xt, gram = panel(velocity, lo, hi, metric)
    w = inverse_factor(lax.psum(gram, "space"))
    count = lax.axis_size("tm")
    following = lax.ppermute(x[:, :1], "tm", [(i, (i - 1) % count) for i in range(count)])
    shifted = jnp.concatenate([x[:, 1:], following], axis=1)
    gathered = lax.all_gather(shifted, "tm", axis=1, tiled=True)
    partial = jnp.dot(xt, gathered, preferred_element_type=F32)
    summed = lax.psum_scatter(partial, "space", scatter_dimension=1, tiled=True)
    return mm(w, summed)


def solution(mesh):
    groups = mesh.shape["tm"]
    paired = groups == 4 and mesh.shape["space"] == 8
    return jax.shard_map(
        paired_body if paired else general_body,
        mesh=mesh,
        in_specs=(P(None, "space", "tm"), P("space")),
        out_specs=P("tm", "space"),
        check_vma=False,
    )
```

```python
import functools

import jax
import jax.numpy as jnp
from jax import lax
from jax.experimental import pallas as pl
from jax.experimental.pallas import tpu as pltpu
from jax.sharding import PartitionSpec as P

F32 = jnp.float32
BF16 = jnp.bfloat16
HIGHEST = lax.Precision.HIGHEST
VMEM = pl.BlockSpec(memory_space=pltpu.VMEM)
SMEM = pl.BlockSpec(memory_space=pltpu.SMEM)
LEAF = 64
PIVOTS = 4


def params(mib=40):
    return pltpu.CompilerParams(vmem_limit_bytes=mib * 1024 * 1024)


def cost(flops, moved):
    return pl.CostEstimate(flops=flops, bytes_accessed=moved, transcendentals=0)


EDGE = 16


def combine(first, second, third, center0, center1):
    return third + center0 * second - center1 * first


def interior_kernel(vel_ref, met_ref, x_ref, head_ref, tail_ref):
    rows, cols = vel_ref.shape[1:]
    row = lax.broadcasted_iota(jnp.int32, (rows, cols), 0)
    metric = met_ref[...]

    def gradient(k):
        field = vel_ref[k].astype(F32)
        head_ref[k] = field[:8]
        tail_ref[k] = field[rows - 8 :]
        up = jnp.where(row == rows - 1, 0.0, pltpu.roll(field, rows - 1, 0))
        down = jnp.where(row == 0, 0.0, pltpu.roll(field, 1, 0))
        return metric * (up - down) * 0.5

    first = gradient(0)
    x_ref[0:rows] = first.astype(BF16)
    second = gradient(1)
    x_ref[rows : 2 * rows] = second.astype(BF16)
    third = combine(first, second, gradient(2), vel_ref[0].astype(F32), vel_ref[1].astype(F32))
    x_ref[2 * rows :] = third.astype(BF16)


def interior(velocity, metric):
    _, rows, cols = velocity.shape
    return pl.pallas_call(
        interior_kernel,
        out_shape=(
            jax.ShapeDtypeStruct((3 * rows, cols), BF16),
            jax.ShapeDtypeStruct((3, 8, cols), F32),
            jax.ShapeDtypeStruct((3, 8, cols), F32),
        ),
        in_specs=[VMEM] * 2,
        out_specs=(VMEM,) * 3,
        compiler_params=params(),
        cost_estimate=cost(30 * rows * cols, 12 * rows * cols),
        name="interior",
    )(velocity, metric)


def panel_kernel(pos_ref, x_in_ref, head_ref, tail_ref, near_ref, far_ref, met_ref, x_ref, xt_ref, *g_refs):
    cols = x_ref.shape[1]
    rows = x_ref.shape[0] // 3
    even = pos_ref[2] == 0
    row = lax.broadcasted_iota(jnp.int32, (EDGE, cols), 0)

    def edge(start, gradient, heads, at):
        first, second, third = [gradient(k) for k in range(3)]
        third = combine(first, second, third, heads[0], heads[1])
        for k, value in enumerate((first, second, third)):
            span = slice(k * rows + start, k * rows + start + EDGE)
            kept = x_in_ref[span].astype(F32)
            x_ref[span] = jnp.where(row == at, value, kept).astype(BF16)

    x_ref[...] = x_in_ref[...]
    lo = [jnp.where(even, far_ref[k].astype(F32), near_ref[k].astype(F32)) for k in range(3)]
    hi = [jnp.where(even, near_ref[k].astype(F32), far_ref[k].astype(F32)) for k in range(3)]
    low = met_ref[0:1]
    edge(0, lambda k: low * (head_ref[k, 1:2] - lo[k]) * 0.5, [head_ref[k, 0:1] for k in range(2)], 0)
    high = met_ref[rows - 1 : rows]
    edge(rows - EDGE, lambda k: high * (hi[k] - tail_ref[k, 6:7]) * 0.5, [tail_ref[k, 7:8] for k in range(2)], EDGE - 1)
    xt_ref[...] = x_ref[...].T
    gram = jnp.dot(xt_ref[...], x_ref[...], preferred_element_type=F32)
    if len(g_refs) == 1:
        g_refs[0][...] = gram
        return
    away_ref, mine_ref, g_ref = g_refs
    g_ref[...] = gram
    half = cols // 2
    for ref, core in ((mine_ref, pos_ref[2]), (away_ref, 1 - pos_ref[2])):
        ref[0:half] = jnp.where(core == 0, g_ref[0:half, 0:half], g_ref[half:, half:])
        ref[half:] = jnp.where(core == 0, g_ref[half : half + half // 2, 0:half], g_ref[half + half // 2 :, 0:half])


def panel(pos, inner, near, far, metric, packed):
    x, head, tail = inner
    height, cols = x.shape
    share = jax.ShapeDtypeStruct((3 * cols // 4, cols // 2), F32)
    whole = jax.ShapeDtypeStruct((cols, cols), F32)
    grams = (share, share) if packed else (whole,)
    return pl.pallas_call(
        panel_kernel,
        out_shape=(jax.ShapeDtypeStruct((height, cols), BF16), jax.ShapeDtypeStruct((cols, height), BF16)) + grams,
        in_specs=[SMEM] + [VMEM] * 6,
        out_specs=(VMEM,) * (2 + len(grams)),
        scratch_shapes=[pltpu.VMEM((cols, cols), F32)] if packed else [],
        compiler_params=params(),
        cost_estimate=cost(2 * height * cols * cols, 6 * height * cols),
        name="panel",
    )(pos, x, head, tail, near, far, metric)


def gather_kernel(pos_ref, mine_ref, theirs_ref, x_in_ref, near_in_ref, g_ref, x_ref, near_ref):
    del x_in_ref, near_in_ref, x_ref, near_ref
    half = mine_ref.shape[1]
    even = pos_ref[2] == 0
    first = jnp.where(even, mine_ref[...], theirs_ref[...])
    second = jnp.where(even, theirs_ref[...], mine_ref[...])
    g_ref[0:half, 0:half] = first[:half]
    g_ref[half:, half:] = second[:half]
    across = jnp.concatenate([first[half:], second[half:]], axis=0)
    g_ref[half:, 0:half] = across
    g_ref[0:half, half:] = across.T


def gather_gram(pos, mine, theirs, x, near):
    n = 2 * mine.shape[1]
    anywhere = pl.BlockSpec(memory_space=pl.ANY)
    return pl.pallas_call(
        gather_kernel,
        out_shape=(
            jax.ShapeDtypeStruct((n, n), F32),
            jax.ShapeDtypeStruct(x.shape, x.dtype),
            jax.ShapeDtypeStruct(near.shape, near.dtype),
        ),
        in_specs=[SMEM, VMEM, VMEM, anywhere, anywhere],
        out_specs=(VMEM, anywhere, anywhere),
        input_output_aliases={3: 1, 4: 2},
        compiler_params=params(),
        name="gather",
    )(pos, mine, theirs, x, near)


def leaf_inverse(block):
    n = block.shape[0]
    row = lax.broadcasted_iota(jnp.int32, (n, 2 * n), 0)
    lane = lax.broadcasted_iota(jnp.int32, (n, 2 * n), 1)
    eye = (row == lane).astype(F32)
    right = (lane == row + n).astype(F32)
    m = jnp.concatenate([block, right[:, n:]], axis=1)
    for j in range(0, n, PIVOTS):
        columns = [jnp.broadcast_to(m[:, j + b : j + b + 1], (n, 2 * n)) for b in range(PIVOTS)]
        pivot_rows = [m[j + a : j + a + 1, :] for a in range(PIVOTS)]
        splat = [[columns[b][j + a : j + a + 1, :] for b in range(PIVOTS)] for a in range(PIVOTS)]
        update = None
        inverses = []
        for a in range(PIVOTS):
            inverse = 1.0 / splat[a][a]
            for b in range(a + 1, PIVOTS):
                ratio = splat[a][b] * inverse
                for c in range(b, PIVOTS):
                    splat[b][c] = splat[b][c] - ratio * splat[a][c]
                pivot_rows[b] = pivot_rows[b] - ratio * pivot_rows[a]
            inverses.append(inverse)
        for a in range(PIVOTS):
            multiplier = jnp.where(row > j + a, columns[a] * inverses[a], 0.0)
            for b in range(a + 1, PIVOTS):
                columns[b] = columns[b] - multiplier * splat[a][b]
            term = multiplier * pivot_rows[a]
            update = term if update is None else update + term
        m = m - update
    diagonal = jnp.sum(m * eye, axis=1, keepdims=True)
    return m[:, n:] * lax.rsqrt(diagonal)


def mm(left, right, dims=((1,), (0,))):
    return lax.dot_general(left, right, (dims, ((), ())), precision=HIGHEST, preferred_element_type=F32)


def factor_kernel(first, leaves, *refs):
    g_ref, w_in_ref = (refs[0], None) if first == 0 else refs[:2]
    a_ref, w_ref = refs[-2:]
    n = g_ref.shape[0]
    a_ref[...] = g_ref[...]
    if first == 0:
        row = lax.broadcasted_iota(jnp.int32, (n, n), 0)
        lane = lax.broadcasted_iota(jnp.int32, (n, n), 1)
        w_ref[...] = (row == lane).astype(F32)
    else:
        w_ref[...] = w_in_ref[...]
    for leaf in range(first, first + leaves):
        j = leaf * LEAF
        k = j + LEAF
        own = slice(j, k)
        w = leaf_inverse(a_ref[own, own])
        done = mm(w, w_ref[own, :])
        w_ref[own, :] = done
        if k < n:
            u = mm(w, a_ref[own, :])
            a_ref[k:, :] -= mm(u[:, k:], u, ((0,), (0,)))
            w_ref[k:, :] -= mm(u[:, k:], done, ((0,), (0,)))


def factor_part(first, leaves, state, after=()):
    n = state[0].shape[0]
    skip = len(after)

    def kernel(*refs):
        factor_kernel(first, leaves, *refs[: len(state)], *refs[len(state) + skip :])

    return pl.pallas_call(
        kernel,
        out_shape=(jax.ShapeDtypeStruct((n, n), F32),) * 2,
        in_specs=[VMEM] * len(state) + [pl.BlockSpec(memory_space=pl.ANY)] * skip,
        out_specs=(VMEM,) * 2,
        compiler_params=params(),
        cost_estimate=cost(2 * n * n * n, 8 * n * n),
        name="factor",
    )(*state, *after)


def inverse_factor(gram):
    return factor_part(0, gram.shape[0] // LEAF, (gram,))[1]


def blocks_kernel(pos_ref, after_ref, xt_ref, near_ref, far_ref, swap_ref, *outs):
    del after_ref
    chip, group, core = pos_ref[0], pos_ref[1], pos_ref[2]
    count = len(outs)

    def store(block, owner):
        for m in range(count):

            @pl.when(jnp.bitwise_xor(chip, m) == owner)
            def _(m=m):
                outs[m][...] = block

    for r, panel_ref in ((1, near_ref), (2, far_ref)):
        owner = group + jnp.where(core == 0, -r, r)

        @pl.when((owner >= 0) & (owner < count))
        def _(panel_ref=panel_ref, owner=owner):
            store(jnp.dot(xt_ref[...], panel_ref[...], preferred_element_type=F32), owner)

    @pl.when(group == jnp.where(core == 0, 2, 1))
    def _():
        dims = (((0,), (0,)), ((), ()))
        store(lax.dot_general(swap_ref[...], far_ref[...], dims, preferred_element_type=F32), group)


def blocks(pos, after, xt, near, far, swap, count):
    n = xt.shape[0]
    return pl.pallas_call(
        blocks_kernel,
        out_shape=(jax.ShapeDtypeStruct((n, n), F32),) * count,
        in_specs=[SMEM, pl.BlockSpec(memory_space=pl.ANY)] + [VMEM] * 4,
        out_specs=(VMEM,) * count,
        compiler_params=params(),
        cost_estimate=cost(2 * 3 * n * n * xt.shape[1], 4 * count * n * n),
        name="blocks",
    )(pos, after, xt, near, far, swap)


def total_kernel(after_ref, *refs):
    del after_ref
    value = refs[0][...]
    for ref in refs[1:-1]:
        value = value + ref[...]
    refs[-1][...] = value


def total(after, parts):
    n = parts[0].shape[0]
    return pl.pallas_call(
        total_kernel,
        out_shape=jax.ShapeDtypeStruct((n, n), F32),
        in_specs=[pl.BlockSpec(memory_space=pl.ANY)] + [VMEM] * len(parts),
        out_specs=VMEM,
        compiler_params=params(),
        name="total",
    )(after, *parts)


def merge_kernel(pos_ref, after_ref, own_ref, moved_ref, cross_ref, mine_ref, sib_ref, top_ref, t_ref):
    del after_ref
    n = own_ref.shape[0]
    half = n // 2
    moved = jnp.abs(pos_ref[0] - pos_ref[1]) == 3
    own = jnp.where(moved, moved_ref[...], own_ref[...])
    t_ref[0:n] = own.T + cross_ref[...]
    core = pos_ref[2]
    top_ref[...] = t_ref[0:8]
    mine_ref[...] = t_ref[pl.ds(pl.multiple_of(core * half, 8), half + 8)]
    sib_ref[...] = t_ref[pl.ds(pl.multiple_of((1 - core) * half, 8), half + 8)]


def merge(pos, after, own, moved, cross):
    n = own.shape[0]
    half = n // 2
    return pl.pallas_call(
        merge_kernel,
        out_shape=tuple(jax.ShapeDtypeStruct((r, n), F32) for r in (half + 8, half + 8, 8)),
        in_specs=[SMEM, pl.BlockSpec(memory_space=pl.ANY)] + [VMEM] * 3,
        out_specs=(VMEM,) * 3,
        scratch_shapes=[pltpu.VMEM((n + 8, n), F32)],
        compiler_params=params(),
        name="merge",
    )(pos, after, own, moved, cross)


def tiles_kernel(pos_ref, w_ref, g_ref, own_ref, sib_ref, top_ref, out_ref, p_ref):
    chip, group, core, count = pos_ref[0], pos_ref[1], pos_ref[2], pos_ref[3]
    half = out_ref.shape[1]
    following = jnp.where(chip + 1 == count, 0, chip + 1)
    owner = jnp.where(chip < group, 0, 1)

    @pl.when(chip == group)
    def _():
        p_ref[0:half] = g_ref[pl.ds(pl.multiple_of(core * half, 8), half)]
        p_ref[half:] = g_ref[half : half + 8]

    @pl.when(chip != group)
    def _():
        p_ref[...] = jnp.where(core == owner, own_ref[...], sib_ref[...])

    @pl.when(core != 0)
    def _():
        p_ref[half:] = jnp.where(following == group, g_ref[0:8], top_ref[...])

    shifted = pltpu.roll(p_ref[...], half + 7, 0)[:half]
    out_ref[...] = mm(w_ref[...], shifted, ((1,), (1,)))


def tiles(pos, w, gram, slabs):
    n = w.shape[0]
    half = n // 2
    return pl.pallas_call(
        tiles_kernel,
        out_shape=jax.ShapeDtypeStruct((n, half), F32),
        in_specs=[SMEM] + [VMEM] * 5,
        out_specs=VMEM,
        scratch_shapes=[pltpu.VMEM((half + 8, n), F32)],
        compiler_params=params(),
        name="tiles",
    )(pos, w, gram, *slabs)


def start(velocity, metric, packed):
    count = lax.axis_size("space")
    space, group = lax.axis_index("space"), lax.axis_index("tm")
    odd = space % 2
    pos = jnp.stack([space // 2, group, odd, lax.axis_size("tm")]).astype(jnp.int32)
    head, tail = velocity[:, :1], velocity[:, -1:]
    inside = [(i, i ^ 1) for i in range(count)]
    outside = [(i, i + 1) for i in range(1, count - 1, 2)]
    outside += [(j, i) for i, j in outside]
    far = lax.ppermute(jnp.where(odd == 0, head, tail), "space", outside)
    near = lax.ppermute(jnp.where(odd == 0, tail, head), "space", inside)
    column = metric.reshape(-1, 1)
    return pos, panel(pos, interior(velocity, column), near, far, column, packed)


def paired_body(velocity, metric):
    groups = lax.axis_size("tm")
    axes = ("space", "tm")
    every = range(groups)
    cores = (0, 1)

    def at(chip, group, core):
        return (2 * chip + core) * groups + group

    def send(value, pairs):
        return lax.ppermute(value, axes, pairs)

    pos, (x, xt, away, mine) = start(velocity, metric, True)

    def hops(group_pairs):
        pairs = [(at(k, z, 0), at(k, t, 0)) for k in every for z, t in group_pairs]
        return pairs + [(at(k, 3 - z, 1), at(k, 3 - t, 1)) for k in every for z, t in group_pairs]

    near = send(x, hops([(0, 1), (1, 2), (2, 3)]))

    siblings = [(at(k, z, c), at(k, z, 1 - c)) for k in every for z in every for c in cores]
    mine = mine + send(away, siblings)
    others = [
        send(mine, [(at(k, z, c), at(k ^ m, z, c)) for k in every for z in every for c in cores])
        for m in range(1, groups)
    ]
    for other in others:
        mine = mine + other
    gram, x, near = gather_gram(pos, mine, send(mine, siblings), x, near)
    state = factor_part(0, 2, (gram,))

    far = send(near, hops([(1, 2), (2, 3)]))
    swap = send(x, hops([(3, 2)]))
    parts = list(blocks(pos, state[0], xt, near, far, swap, groups))
    state = factor_part(2, 1, state, (parts[0],))

    owners = {(k, z): (k, z, 0 if k < z else 1) for k in every for z in every if k != z}
    owners[0, 3] = (2, 2, 0)
    owners[3, 0] = (1, 1, 1)
    for m in range(1, groups):
        parts[m] = send(parts[m], [(at(k ^ m, z, c), at(k, z, c)) for k, z, c in owners.values()])
    own = total(state[0], parts)
    w = factor_part(3, 1, state, (own,))[1]

    homes = {(k, z): (k, z, 0 if k < z else 1) for k, z in owners}
    cross = send(own, [(at(*o), at(*homes[z, k])) for (k, z), o in owners.items()])
    moved = send(own, [(at(*owners[p]), at(*homes[p])) for p in ((0, 3), (3, 0))])
    mine, sib, top = merge(pos, w, own, moved, cross)
    sib = send(sib, [(at(k, z, c), at(k, z, 1 - c)) for k, z, c in homes.values()])
    top = send(top, [(at(k, z, c), at((k - 1) % groups, z, 1)) for k, z, c in homes.values()])
    return tiles(pos, w, gram, (mine, sib, top))


def general_body(velocity, metric):
    _, (x, xt, gram) = start(velocity, metric, False)
    w = inverse_factor(lax.psum(gram, "space"))
    count = lax.axis_size("tm")
    following = lax.ppermute(x[:, :1], "tm", [(i, (i - 1) % count) for i in range(count)])
    shifted = jnp.concatenate([x[:, 1:], following], axis=1)
    gathered = lax.all_gather(shifted, "tm", axis=1, tiled=True)
    partial = jnp.dot(xt, gathered, preferred_element_type=F32)
    summed = lax.psum_scatter(partial, "space", scatter_dimension=1, tiled=True)
    return mm(w, summed)


def solution(mesh):
    groups = mesh.shape["tm"]
    paired = groups == 4 and mesh.shape["space"] == 8
    return jax.shard_map(
        paired_body if paired else general_body,
        mesh=mesh,
        in_specs=(P(None, "space", "tm"), P("space")),
        out_specs=P("tm", "space"),
        check_vma=False,
    )
```

```python
import functools

import jax
import jax.numpy as jnp
from jax import lax
from jax.experimental import pallas as pl
from jax.experimental.pallas import tpu as pltpu
from jax.sharding import PartitionSpec as P

F32 = jnp.float32
BF16 = jnp.bfloat16
HIGHEST = lax.Precision.HIGHEST
VMEM = pl.BlockSpec(memory_space=pltpu.VMEM)
SMEM = pl.BlockSpec(memory_space=pltpu.SMEM)
LEAF = 64
PIVOTS = 4


def params(mib=40):
    return pltpu.CompilerParams(vmem_limit_bytes=mib * 1024 * 1024)


def cost(flops, moved):
    return pl.CostEstimate(flops=flops, bytes_accessed=moved, transcendentals=0)


EDGE = 16


def combine(first, second, third, center0, center1):
    return third + center0 * second - center1 * first


def interior_kernel(pos_ref, vel_hbm, met_hbm, x_ref, met_ref, inside_ref, outside_ref, head_ref, tail_ref, vel_ref, row_ref, sems):
    rows, cols = vel_ref.shape[1:]
    copies = [pltpu.make_async_copy(met_hbm, row_ref, sems.at[3])]
    copies += [pltpu.make_async_copy(vel_hbm.at[k], vel_ref.at[k], sems.at[k]) for k in range(3)]
    for copy in copies:
        copy.start()
    even = pos_ref[2] == 0
    row = lax.broadcasted_iota(jnp.int32, (rows, cols), 0)
    copies[0].wait()
    metric = jnp.broadcast_to(row_ref[...][None, :], (8, rows)).T[:, 0:1]
    met_ref[...] = metric

    def gradient(k):
        copies[k + 1].wait()
        field = vel_ref[k].astype(F32)
        head, tail = field[0:1], field[rows - 1 : rows]
        inside_ref[k : k + 1] = jnp.where(even, tail, head)
        outside_ref[k : k + 1] = jnp.where(even, head, tail)
        head_ref[k] = field[:8]
        tail_ref[k] = field[rows - 8 :]
        up = jnp.where(row == rows - 1, 0.0, pltpu.roll(field, rows - 1, 0))
        down = jnp.where(row == 0, 0.0, pltpu.roll(field, 1, 0))
        return metric * (up - down) * 0.5

    first = gradient(0)
    x_ref[0:rows] = first.astype(BF16)
    second = gradient(1)
    x_ref[rows : 2 * rows] = second.astype(BF16)
    third = combine(first, second, gradient(2), vel_ref[0].astype(F32), vel_ref[1].astype(F32))
    x_ref[2 * rows :] = third.astype(BF16)


def interior(pos, velocity, metric):
    _, rows, cols = velocity.shape
    hbm = pl.BlockSpec(memory_space=pltpu.HBM)
    return pl.pallas_call(
        interior_kernel,
        out_shape=(
            jax.ShapeDtypeStruct((3 * rows, cols), BF16),
            jax.ShapeDtypeStruct((rows, 1), F32),
            jax.ShapeDtypeStruct((8, cols), F32),
            jax.ShapeDtypeStruct((8, cols), F32),
            jax.ShapeDtypeStruct((3, 8, cols), F32),
            jax.ShapeDtypeStruct((3, 8, cols), F32),
        ),
        in_specs=[SMEM, hbm, hbm],
        out_specs=(VMEM,) * 6,
        scratch_shapes=[
            pltpu.VMEM((3, rows, cols), BF16),
            pltpu.VMEM((rows,), F32),
            pltpu.SemaphoreType.DMA((4,)),
        ],
        compiler_params=params(60),
        cost_estimate=cost(30 * rows * cols, 12 * rows * cols),
        name="interior",
    )(pos, velocity, metric)


def panel_kernel(pos_ref, x_in_ref, head_ref, tail_ref, near_ref, far_ref, met_ref, x_ref, xt_ref, *g_refs):
    cols = x_ref.shape[1]
    rows = x_ref.shape[0] // 3
    even = pos_ref[2] == 0
    row = lax.broadcasted_iota(jnp.int32, (EDGE, cols), 0)

    def edge(start, gradient, heads, at):
        first, second, third = [gradient(k) for k in range(3)]
        third = combine(first, second, third, heads[0], heads[1])
        for k, value in enumerate((first, second, third)):
            span = slice(k * rows + start, k * rows + start + EDGE)
            kept = x_in_ref[span].astype(F32)
            x_ref[span] = jnp.where(row == at, value, kept).astype(BF16)

    x_ref[...] = x_in_ref[...]
    lo = [jnp.where(even, far_ref[k : k + 1], near_ref[k : k + 1]) for k in range(3)]
    hi = [jnp.where(even, near_ref[k : k + 1], far_ref[k : k + 1]) for k in range(3)]
    low = met_ref[0:1]
    edge(0, lambda k: low * (head_ref[k, 1:2] - lo[k]) * 0.5, [head_ref[k, 0:1] for k in range(2)], 0)
    high = met_ref[rows - 1 : rows]
    edge(rows - EDGE, lambda k: high * (hi[k] - tail_ref[k, 6:7]) * 0.5, [tail_ref[k, 7:8] for k in range(2)], EDGE - 1)
    xt_ref[...] = x_ref[...].T
    gram = jnp.dot(xt_ref[...], x_ref[...], preferred_element_type=F32)
    if len(g_refs) == 1:
        g_refs[0][...] = gram
        return
    away_ref, mine_ref, g_ref = g_refs
    g_ref[...] = gram
    half = cols // 2
    for ref, core in ((mine_ref, pos_ref[2]), (away_ref, 1 - pos_ref[2])):
        ref[0:half] = jnp.where(core == 0, g_ref[0:half, 0:half], g_ref[half:, half:])
        ref[half:] = jnp.where(core == 0, g_ref[half : half + half // 2, 0:half], g_ref[half + half // 2 :, 0:half])


def panel(pos, inner, near, far, metric, packed):
    x, head, tail = inner
    height, cols = x.shape
    share = jax.ShapeDtypeStruct((3 * cols // 4, cols // 2), F32)
    whole = jax.ShapeDtypeStruct((cols, cols), F32)
    grams = (share, share) if packed else (whole,)
    return pl.pallas_call(
        panel_kernel,
        out_shape=(jax.ShapeDtypeStruct((height, cols), BF16), jax.ShapeDtypeStruct((cols, height), BF16)) + grams,
        in_specs=[SMEM] + [VMEM] * 6,
        out_specs=(VMEM,) * (2 + len(grams)),
        scratch_shapes=[pltpu.VMEM((cols, cols), F32)] if packed else [],
        compiler_params=params(),
        cost_estimate=cost(2 * height * cols * cols, 6 * height * cols),
        name="panel",
    )(pos, x, head, tail, near, far, metric)


def gather_kernel(pos_ref, mine_ref, theirs_ref, g_ref):
    half = mine_ref.shape[1]
    even = pos_ref[2] == 0
    first = jnp.where(even, mine_ref[...], theirs_ref[...])
    second = jnp.where(even, theirs_ref[...], mine_ref[...])
    g_ref[0:half, 0:half] = first[:half]
    g_ref[half:, half:] = second[:half]
    across = jnp.concatenate([first[half:], second[half:]], axis=0)
    g_ref[half:, 0:half] = across
    g_ref[0:half, half:] = across.T


def gather_gram(pos, mine, theirs):
    n = 2 * mine.shape[1]
    return pl.pallas_call(
        gather_kernel,
        out_shape=jax.ShapeDtypeStruct((n, n), F32),
        in_specs=[SMEM, VMEM, VMEM],
        out_specs=VMEM,
        compiler_params=params(),
        name="gather",
    )(pos, mine, theirs)


def passed(value, after):
    anywhere = pl.BlockSpec(memory_space=pl.ANY)
    return pl.pallas_call(
        lambda *refs: None,
        out_shape=jax.ShapeDtypeStruct(value.shape, value.dtype),
        in_specs=[anywhere, anywhere],
        out_specs=anywhere,
        input_output_aliases={0: 0},
        name="passed",
    )(value, after)


def leaf_inverse(block):
    n = block.shape[0]
    row = lax.broadcasted_iota(jnp.int32, (n, 2 * n), 0)
    lane = lax.broadcasted_iota(jnp.int32, (n, 2 * n), 1)
    eye = (row == lane).astype(F32)
    right = (lane == row + n).astype(F32)
    m = jnp.concatenate([block, right[:, n:]], axis=1)
    for j in range(0, n, PIVOTS):
        columns = [jnp.broadcast_to(m[:, j + b : j + b + 1], (n, 2 * n)) for b in range(PIVOTS)]
        pivot_rows = [m[j + a : j + a + 1, :] for a in range(PIVOTS)]
        splat = [[columns[b][j + a : j + a + 1, :] for b in range(PIVOTS)] for a in range(PIVOTS)]
        update = None
        inverses = []
        for a in range(PIVOTS):
            inverse = 1.0 / splat[a][a]
            for b in range(a + 1, PIVOTS):
                ratio = splat[a][b] * inverse
                for c in range(b, PIVOTS):
                    splat[b][c] = splat[b][c] - ratio * splat[a][c]
                pivot_rows[b] = pivot_rows[b] - ratio * pivot_rows[a]
            inverses.append(inverse)
        for a in range(PIVOTS):
            multiplier = jnp.where(row > j + a, columns[a] * inverses[a], 0.0)
            for b in range(a + 1, PIVOTS):
                columns[b] = columns[b] - multiplier * splat[a][b]
            term = multiplier * pivot_rows[a]
            update = term if update is None else update + term
        m = m - update
    diagonal = jnp.sum(m * eye, axis=1, keepdims=True)
    return m[:, n:] * lax.rsqrt(diagonal)


def mm(left, right, dims=((1,), (0,))):
    return lax.dot_general(left, right, (dims, ((), ())), precision=HIGHEST, preferred_element_type=F32)


def factor_kernel(first, leaves, *refs):
    g_ref, w_in_ref = (refs[0], None) if first == 0 else refs[:2]
    a_ref, w_ref = refs[-2:]
    n = g_ref.shape[0]
    a_ref[...] = g_ref[...]
    if first == 0:
        row = lax.broadcasted_iota(jnp.int32, (n, n), 0)
        lane = lax.broadcasted_iota(jnp.int32, (n, n), 1)
        w_ref[...] = (row == lane).astype(F32)
    else:
        w_ref[...] = w_in_ref[...]
    for leaf in range(first, first + leaves):
        j = leaf * LEAF
        k = j + LEAF
        own = slice(j, k)
        w = leaf_inverse(a_ref[own, own])
        done = mm(w, w_ref[own, :])
        w_ref[own, :] = done
        if k < n:
            u = mm(w, a_ref[own, :])
            a_ref[k:, :] -= mm(u[:, k:], u, ((0,), (0,)))
            w_ref[k:, :] -= mm(u[:, k:], done, ((0,), (0,)))


def factor_part(first, leaves, state, after=()):
    n = state[0].shape[0]
    skip = len(after)

    def kernel(*refs):
        factor_kernel(first, leaves, *refs[: len(state)], *refs[len(state) + skip :])

    return pl.pallas_call(
        kernel,
        out_shape=(jax.ShapeDtypeStruct((n, n), F32),) * 2,
        in_specs=[VMEM] * len(state) + [pl.BlockSpec(memory_space=pl.ANY)] * skip,
        out_specs=(VMEM,) * 2,
        compiler_params=params(),
        cost_estimate=cost(2 * n * n * n, 8 * n * n),
        name="factor",
    )(*state, *after)


def inverse_factor(gram):
    return factor_part(0, gram.shape[0] // LEAF, (gram,))[1]


def core_of(chip, group, count):
    behind = (group - chip + count) % count
    return jnp.where((behind == 1) | ((behind == 2) & (group > chip)), 0, 1)


def blocks_kernel(pos_ref, after_ref, xt_ref, near_ref, far_ref, *outs):
    del after_ref
    chip, group, core = pos_ref[0], pos_ref[1], pos_ref[2]
    count = len(outs)
    for r, panel_ref in ((1, near_ref), (2, far_ref)):
        owner = (group + jnp.where(core == 0, count - r, r)) % count

        @pl.when((r == 1) | (core_of(owner, group, count) == core))
        def _(panel_ref=panel_ref, owner=owner):
            block = jnp.dot(xt_ref[...], panel_ref[...], preferred_element_type=F32)
            for m in range(count):

                @pl.when(jnp.bitwise_xor(chip, m) == owner)
                def _(m=m):
                    outs[m][...] = block


def blocks(pos, after, xt, near, far, count):
    n = xt.shape[0]
    return pl.pallas_call(
        blocks_kernel,
        out_shape=(jax.ShapeDtypeStruct((n, n), F32),) * count,
        in_specs=[SMEM, pl.BlockSpec(memory_space=pl.ANY)] + [VMEM] * 3,
        out_specs=(VMEM,) * count,
        compiler_params=params(),
        cost_estimate=cost(2 * 2 * n * n * xt.shape[1], 4 * count * n * n),
        name="blocks",
    )(pos, after, xt, near, far)


def total_kernel(*refs):
    value = refs[0][...]
    for ref in refs[1:-1]:
        value = value + ref[...]
    refs[-1][...] = value


def total(parts):
    n = parts[0].shape[0]
    return pl.pallas_call(
        total_kernel,
        out_shape=jax.ShapeDtypeStruct((n, n), F32),
        in_specs=[VMEM] * len(parts),
        out_specs=VMEM,
        compiler_params=params(),
        name="total",
    )(*parts)


def merge_kernel(pos_ref, own_ref, cross_ref, mine_ref, sib_ref, top_ref, t_ref):
    n = own_ref.shape[0]
    half = n // 2
    t_ref[0:n] = own_ref[...].T + cross_ref[...]
    core = pos_ref[2]
    top_ref[...] = t_ref[0:8]
    mine_ref[...] = t_ref[pl.ds(pl.multiple_of(core * half, 8), half + 8)]
    sib_ref[...] = t_ref[pl.ds(pl.multiple_of((1 - core) * half, 8), half + 8)]


def merge(pos, own, cross):
    n = own.shape[0]
    half = n // 2
    return pl.pallas_call(
        merge_kernel,
        out_shape=tuple(jax.ShapeDtypeStruct((r, n), F32) for r in (half + 8, half + 8, 8)),
        in_specs=[SMEM] + [VMEM] * 2,
        out_specs=(VMEM,) * 3,
        scratch_shapes=[pltpu.VMEM((n + 8, n), F32)],
        compiler_params=params(),
        name="merge",
    )(pos, own, cross)


def tiles_kernel(pos_ref, w_ref, g_ref, own_ref, sib_ref, top_ref, out_ref, p_ref):
    chip, group, core, count = pos_ref[0], pos_ref[1], pos_ref[2], pos_ref[3]
    half = out_ref.shape[1]
    following = jnp.where(chip + 1 == count, 0, chip + 1)
    owner = core_of(chip, group, count)

    @pl.when(chip == group)
    def _():
        p_ref[0:half] = g_ref[pl.ds(pl.multiple_of(core * half, 8), half)]
        p_ref[half:] = g_ref[half : half + 8]

    @pl.when(chip != group)
    def _():
        p_ref[...] = jnp.where(core == owner, own_ref[...], sib_ref[...])

    @pl.when(core != 0)
    def _():
        p_ref[half:] = jnp.where(following == group, g_ref[0:8], top_ref[...])

    shifted = pltpu.roll(p_ref[...], half + 7, 0)[:half]
    out_ref[...] = mm(w_ref[...], shifted, ((1,), (1,)))


def tiles(pos, w, gram, slabs):
    n = w.shape[0]
    half = n // 2
    return pl.pallas_call(
        tiles_kernel,
        out_shape=jax.ShapeDtypeStruct((n, half), F32),
        in_specs=[SMEM] + [VMEM] * 5,
        out_specs=VMEM,
        scratch_shapes=[pltpu.VMEM((half + 8, n), F32)],
        compiler_params=params(),
        name="tiles",
    )(pos, w, gram, *slabs)


def start(velocity, metric, packed):
    count = lax.axis_size("space")
    space, group = lax.axis_index("space"), lax.axis_index("tm")
    odd = space % 2
    pos = jnp.stack([space // 2, group, odd, lax.axis_size("tm")]).astype(jnp.int32)
    x, column, inward, outward, head, tail = interior(pos, velocity, metric)
    inside = [(i, i ^ 1) for i in range(count)]
    outside = [(i, i + 1) for i in range(1, count - 1, 2)]
    outside += [(j, i) for i, j in outside]
    far = lax.ppermute(outward, "space", outside)
    near = lax.ppermute(inward, "space", inside)
    return pos, panel(pos, (x, head, tail), near, far, column, packed)


def paired_body(velocity, metric):
    groups = lax.axis_size("tm")
    axes = ("space", "tm")
    every = range(groups)
    cores = (0, 1)

    def at(chip, group, core):
        return (2 * chip + core) * groups + group

    def send(value, pairs):
        return lax.ppermute(value, axes, pairs)

    pos, (x, xt, away, mine) = start(velocity, metric, True)

    def hops(sources):
        pairs = [(at(k, z, 0), at(k, (z + 1) % groups, 0)) for k in every for z in sources]
        return pairs + [(at(k, 3 - z, 1), at(k, (2 - z) % groups, 1)) for k in every for z in sources]

    near = send(x, hops(every))

    siblings = [(at(k, z, c), at(k, z, 1 - c)) for k in every for z in every for c in cores]
    mine = mine + send(away, siblings)
    others = [
        send(mine, [(at(k, z, c), at(k ^ m, z, c)) for k in every for z in every for c in cores])
        for m in range(1, groups)
    ]
    for other in others:
        mine = mine + other
    gram = gather_gram(pos, mine, send(mine, siblings))
    state = factor_part(0, 1, (gram,))
    near = passed(near, state[0])
    far = send(near, hops((1, 2)))
    w = factor_part(1, 3, state)[1]
    parts = list(blocks(pos, w, xt, near, far, groups))

    def holder(k, z):
        return 0 if (z - k) % groups == 1 or z - k == 2 else 1

    homes = {(k, z): (k, z, holder(k, z)) for k in every for z in every if k != z}
    for m in range(1, groups):
        parts[m] = send(parts[m], [(at(k ^ m, z, c), at(k, z, c)) for k, z, c in homes.values()])
    own = total(parts)
    cross = send(own, [(at(*home), at(*homes[z, k])) for (k, z), home in homes.items()])
    mine, sib, top = merge(pos, own, cross)
    sib = send(sib, [(at(k, z, c), at(k, z, 1 - c)) for k, z, c in homes.values()])
    top = send(top, [(at(k, z, c), at((k - 1) % groups, z, 1)) for k, z, c in homes.values()])
    return tiles(pos, w, gram, (mine, sib, top))


def general_body(velocity, metric):
    _, (x, xt, gram) = start(velocity, metric, False)
    w = inverse_factor(lax.psum(gram, "space"))
    count = lax.axis_size("tm")
    following = lax.ppermute(x[:, :1], "tm", [(i, (i - 1) % count) for i in range(count)])
    shifted = jnp.concatenate([x[:, 1:], following], axis=1)
    gathered = lax.all_gather(shifted, "tm", axis=1, tiled=True)
    partial = jnp.dot(xt, gathered, preferred_element_type=F32)
    summed = lax.psum_scatter(partial, "space", scatter_dimension=1, tiled=True)
    return mm(w, summed)


def solution(mesh):
    groups = mesh.shape["tm"]
    paired = groups == 4 and mesh.shape["space"] == 8
    return jax.shard_map(
        paired_body if paired else general_body,
        mesh=mesh,
        in_specs=(P(None, "space", "tm"), P("space")),
        out_specs=P("tm", "space"),
        check_vma=False,
    )
```

```python
import functools

import jax
import jax.numpy as jnp
from jax import lax
from jax.experimental import pallas as pl
from jax.experimental.pallas import tpu as pltpu
from jax.sharding import PartitionSpec as P

F32 = jnp.float32
BF16 = jnp.bfloat16
HIGHEST = lax.Precision.HIGHEST
VMEM = pl.BlockSpec(memory_space=pltpu.VMEM)
SMEM = pl.BlockSpec(memory_space=pltpu.SMEM)
LEAF = 64
PIVOTS = 4


def params(mib=40):
    return pltpu.CompilerParams(vmem_limit_bytes=mib * 1024 * 1024)


def cost(flops, moved):
    return pl.CostEstimate(flops=flops, bytes_accessed=moved, transcendentals=0)


EDGE = 16


def combine(first, second, third, center0, center1):
    return third + center0 * second - center1 * first


def interior_kernel(pos_ref, vel_ref, row_ref, x_ref, met_ref, inside_ref, outside_ref, head_ref, tail_ref):
    rows, cols = vel_ref.shape[1:]
    even = pos_ref[2] == 0
    row = lax.broadcasted_iota(jnp.int32, (rows, cols), 0)
    metric = jnp.broadcast_to(row_ref[...][None, :], (8, rows)).T[:, 0:1]
    met_ref[...] = metric

    def gradient(k):
        field = vel_ref[k].astype(F32)
        head, tail = field[0:1], field[rows - 1 : rows]
        inside_ref[k : k + 1] = jnp.where(even, tail, head)
        outside_ref[k : k + 1] = jnp.where(even, head, tail)
        head_ref[k] = field[:8]
        tail_ref[k] = field[rows - 8 :]
        up = jnp.where(row == rows - 1, 0.0, pltpu.roll(field, rows - 1, 0))
        down = jnp.where(row == 0, 0.0, pltpu.roll(field, 1, 0))
        return metric * (up - down) * 0.5

    first = gradient(0)
    x_ref[0:rows] = first.astype(BF16)
    second = gradient(1)
    x_ref[rows : 2 * rows] = second.astype(BF16)
    third = combine(first, second, gradient(2), vel_ref[0].astype(F32), vel_ref[1].astype(F32))
    x_ref[2 * rows :] = third.astype(BF16)


def interior(pos, velocity, metric):
    _, rows, cols = velocity.shape
    return pl.pallas_call(
        interior_kernel,
        out_shape=(
            jax.ShapeDtypeStruct((3 * rows, cols), BF16),
            jax.ShapeDtypeStruct((rows, 1), F32),
            jax.ShapeDtypeStruct((8, cols), F32),
            jax.ShapeDtypeStruct((8, cols), F32),
            jax.ShapeDtypeStruct((3, 8, cols), F32),
            jax.ShapeDtypeStruct((3, 8, cols), F32),
        ),
        in_specs=[SMEM, VMEM, VMEM],
        out_specs=(VMEM,) * 6,
        compiler_params=params(),
        cost_estimate=cost(30 * rows * cols, 12 * rows * cols),
        name="interior",
    )(pos, velocity, metric)


def panel_kernel(pos_ref, x_in_ref, head_ref, tail_ref, near_ref, far_ref, met_ref, x_ref, xt_ref, *g_refs):
    cols = x_ref.shape[1]
    rows = x_ref.shape[0] // 3
    even = pos_ref[2] == 0
    row = lax.broadcasted_iota(jnp.int32, (EDGE, cols), 0)

    def edge(start, gradient, heads, at):
        first, second, third = [gradient(k) for k in range(3)]
        third = combine(first, second, third, heads[0], heads[1])
        for k, value in enumerate((first, second, third)):
            span = slice(k * rows + start, k * rows + start + EDGE)
            kept = x_in_ref[span].astype(F32)
            x_ref[span] = jnp.where(row == at, value, kept).astype(BF16)

    x_ref[...] = x_in_ref[...]
    lo = [jnp.where(even, far_ref[k : k + 1], near_ref[k : k + 1]) for k in range(3)]
    hi = [jnp.where(even, near_ref[k : k + 1], far_ref[k : k + 1]) for k in range(3)]
    low = met_ref[0:1]
    edge(0, lambda k: low * (head_ref[k, 1:2] - lo[k]) * 0.5, [head_ref[k, 0:1] for k in range(2)], 0)
    high = met_ref[rows - 1 : rows]
    edge(rows - EDGE, lambda k: high * (hi[k] - tail_ref[k, 6:7]) * 0.5, [tail_ref[k, 7:8] for k in range(2)], EDGE - 1)
    xt_ref[...] = x_ref[...].T
    gram = jnp.dot(xt_ref[...], x_ref[...], preferred_element_type=F32)
    if len(g_refs) == 1:
        g_refs[0][...] = gram
        return
    away_ref, mine_ref, g_ref = g_refs
    g_ref[...] = gram
    half = cols // 2
    for ref, core in ((mine_ref, pos_ref[2]), (away_ref, 1 - pos_ref[2])):
        ref[0:half] = jnp.where(core == 0, g_ref[0:half, 0:half], g_ref[half:, half:])
        ref[half:] = jnp.where(core == 0, g_ref[half : half + half // 2, 0:half], g_ref[half + half // 2 :, 0:half])


def panel(pos, inner, near, far, metric, packed):
    x, head, tail = inner
    height, cols = x.shape
    share = jax.ShapeDtypeStruct((3 * cols // 4, cols // 2), F32)
    whole = jax.ShapeDtypeStruct((cols, cols), F32)
    grams = (share, share) if packed else (whole,)
    return pl.pallas_call(
        panel_kernel,
        out_shape=(jax.ShapeDtypeStruct((height, cols), BF16), jax.ShapeDtypeStruct((cols, height), BF16)) + grams,
        in_specs=[SMEM] + [VMEM] * 6,
        out_specs=(VMEM,) * (2 + len(grams)),
        scratch_shapes=[pltpu.VMEM((cols, cols), F32)] if packed else [],
        compiler_params=params(),
        cost_estimate=cost(2 * height * cols * cols, 6 * height * cols),
        name="panel",
    )(pos, x, head, tail, near, far, metric)


def gather_kernel(pos_ref, mine_ref, theirs_ref, g_ref):
    half = mine_ref.shape[1]
    even = pos_ref[2] == 0
    first = jnp.where(even, mine_ref[...], theirs_ref[...])
    second = jnp.where(even, theirs_ref[...], mine_ref[...])
    g_ref[0:half, 0:half] = first[:half]
    g_ref[half:, half:] = second[:half]
    across = jnp.concatenate([first[half:], second[half:]], axis=0)
    g_ref[half:, 0:half] = across
    g_ref[0:half, half:] = across.T


def gather_gram(pos, mine, theirs):
    n = 2 * mine.shape[1]
    return pl.pallas_call(
        gather_kernel,
        out_shape=jax.ShapeDtypeStruct((n, n), F32),
        in_specs=[SMEM, VMEM, VMEM],
        out_specs=VMEM,
        compiler_params=params(),
        name="gather",
    )(pos, mine, theirs)


def passed(value, after):
    anywhere = pl.BlockSpec(memory_space=pl.ANY)
    return pl.pallas_call(
        lambda *refs: None,
        out_shape=jax.ShapeDtypeStruct(value.shape, value.dtype),
        in_specs=[anywhere, anywhere],
        out_specs=anywhere,
        input_output_aliases={0: 0},
        name="passed",
    )(value, after)


def leaf_inverse(block):
    n = block.shape[0]
    row = lax.broadcasted_iota(jnp.int32, (n, 2 * n), 0)
    lane = lax.broadcasted_iota(jnp.int32, (n, 2 * n), 1)
    eye = (row == lane).astype(F32)
    right = (lane == row + n).astype(F32)
    m = jnp.concatenate([block, right[:, n:]], axis=1)
    for j in range(0, n, PIVOTS):
        columns = [jnp.broadcast_to(m[:, j + b : j + b + 1], (n, 2 * n)) for b in range(PIVOTS)]
        pivot_rows = [m[j + a : j + a + 1, :] for a in range(PIVOTS)]
        splat = [[columns[b][j + a : j + a + 1, :] for b in range(PIVOTS)] for a in range(PIVOTS)]
        update = None
        inverses = []
        for a in range(PIVOTS):
            inverse = 1.0 / splat[a][a]
            for b in range(a + 1, PIVOTS):
                ratio = splat[a][b] * inverse
                for c in range(b, PIVOTS):
                    splat[b][c] = splat[b][c] - ratio * splat[a][c]
                pivot_rows[b] = pivot_rows[b] - ratio * pivot_rows[a]
            inverses.append(inverse)
        for a in range(PIVOTS):
            multiplier = jnp.where(row > j + a, columns[a] * inverses[a], 0.0)
            for b in range(a + 1, PIVOTS):
                columns[b] = columns[b] - multiplier * splat[a][b]
            term = multiplier * pivot_rows[a]
            update = term if update is None else update + term
        m = m - update
    diagonal = jnp.sum(m * eye, axis=1, keepdims=True)
    return m[:, n:] * lax.rsqrt(diagonal)


def mm(left, right, dims=((1,), (0,))):
    return lax.dot_general(left, right, (dims, ((), ())), precision=HIGHEST, preferred_element_type=F32)


def factor_kernel(first, leaves, *refs):
    g_ref, w_in_ref = (refs[0], None) if first == 0 else refs[:2]
    a_ref, w_ref = refs[-2:]
    n = g_ref.shape[0]
    a_ref[...] = g_ref[...]
    if first == 0:
        row = lax.broadcasted_iota(jnp.int32, (n, n), 0)
        lane = lax.broadcasted_iota(jnp.int32, (n, n), 1)
        w_ref[...] = (row == lane).astype(F32)
    else:
        w_ref[...] = w_in_ref[...]
    for leaf in range(first, first + leaves):
        j = leaf * LEAF
        k = j + LEAF
        own = slice(j, k)
        w = leaf_inverse(a_ref[own, own])
        done = mm(w, w_ref[own, :])
        w_ref[own, :] = done
        if k < n:
            u = mm(w, a_ref[own, :])
            a_ref[k:, :] -= mm(u[:, k:], u, ((0,), (0,)))
            w_ref[k:, :] -= mm(u[:, k:], done, ((0,), (0,)))


def factor_part(first, leaves, state, after=()):
    n = state[0].shape[0]
    skip = len(after)

    def kernel(*refs):
        factor_kernel(first, leaves, *refs[: len(state)], *refs[len(state) + skip :])

    return pl.pallas_call(
        kernel,
        out_shape=(jax.ShapeDtypeStruct((n, n), F32),) * 2,
        in_specs=[VMEM] * len(state) + [pl.BlockSpec(memory_space=pl.ANY)] * skip,
        out_specs=(VMEM,) * 2,
        compiler_params=params(),
        cost_estimate=cost(2 * n * n * n, 8 * n * n),
        name="factor",
    )(*state, *after)


def inverse_factor(gram):
    return factor_part(0, gram.shape[0] // LEAF, (gram,))[1]


def core_of(chip, group, count):
    behind = (group - chip + count) % count
    return jnp.where((behind == 1) | ((behind == 2) & (group > chip)), 0, 1)


def block_kernel(after_ref, xt_ref, panel_ref, out_ref):
    del after_ref
    out_ref[...] = jnp.dot(xt_ref[...], panel_ref[...], preferred_element_type=F32)


def pair_block(after, xt, panel):
    n = xt.shape[0]
    return pl.pallas_call(
        block_kernel,
        out_shape=jax.ShapeDtypeStruct((n, n), F32),
        in_specs=[pl.BlockSpec(memory_space=pl.ANY)] + [VMEM] * 2,
        out_specs=VMEM,
        compiler_params=params(),
        cost_estimate=cost(2 * n * n * xt.shape[1], 4 * n * n),
        name="block",
    )(after, xt, panel)


def total_kernel(after_ref, *refs):
    del after_ref
    value = refs[0][...]
    for ref in refs[1:-1]:
        value = value + ref[...]
    refs[-1][...] = value


def total(after, parts):
    n = parts[0].shape[0]
    return pl.pallas_call(
        total_kernel,
        out_shape=jax.ShapeDtypeStruct((n, n), F32),
        in_specs=[pl.BlockSpec(memory_space=pl.ANY)] + [VMEM] * len(parts),
        out_specs=VMEM,
        compiler_params=params(),
        name="total",
    )(after, *parts)


def merge_kernel(pos_ref, *refs):
    sums, (mine_ref, sib_ref, top_ref, t_ref) = refs[:4], refs[4:]
    n = t_ref.shape[0] - 8
    half = n // 2
    chip, group, core = pos_ref[0], pos_ref[1], pos_ref[2]

    def put(own_ref, cross_ref):
        t_ref[0:n] = own_ref[...].T + cross_ref[...]

    distant = jnp.abs(chip - group) == 2
    pl.when(jnp.logical_not(distant))(lambda: put(*sums[:2]))
    pl.when(distant)(lambda: put(*sums[2:]))
    top_ref[...] = t_ref[0:8]
    mine_ref[...] = t_ref[pl.ds(pl.multiple_of(core * half, 8), half + 8)]
    sib_ref[...] = t_ref[pl.ds(pl.multiple_of((1 - core) * half, 8), half + 8)]


def merge(pos, near, far):
    n = near[0].shape[0]
    half = n // 2
    return pl.pallas_call(
        merge_kernel,
        out_shape=tuple(jax.ShapeDtypeStruct((r, n), F32) for r in (half + 8, half + 8, 8)),
        in_specs=[SMEM] + [VMEM] * 4,
        out_specs=(VMEM,) * 3,
        scratch_shapes=[pltpu.VMEM((n + 8, n), F32)],
        compiler_params=params(),
        name="merge",
    )(pos, *near, *far)


def tiles_kernel(pos_ref, w_ref, g_ref, own_ref, sib_ref, top_ref, out_ref, p_ref):
    chip, group, core, count = pos_ref[0], pos_ref[1], pos_ref[2], pos_ref[3]
    half = out_ref.shape[1]
    following = jnp.where(chip + 1 == count, 0, chip + 1)
    owner = core_of(chip, group, count)

    @pl.when(chip == group)
    def _():
        p_ref[0:half] = g_ref[pl.ds(pl.multiple_of(core * half, 8), half)]
        p_ref[half:] = g_ref[half : half + 8]

    @pl.when(chip != group)
    def _():
        p_ref[...] = jnp.where(core == owner, own_ref[...], sib_ref[...])

    @pl.when(core != 0)
    def _():
        p_ref[half:] = jnp.where(following == group, g_ref[0:8], top_ref[...])

    shifted = pltpu.roll(p_ref[...], half + 7, 0)[:half]
    out_ref[...] = mm(w_ref[...], shifted, ((1,), (1,)))


def tiles(pos, w, gram, slabs):
    n = w.shape[0]
    half = n // 2
    return pl.pallas_call(
        tiles_kernel,
        out_shape=jax.ShapeDtypeStruct((n, half), F32),
        in_specs=[SMEM] + [VMEM] * 5,
        out_specs=VMEM,
        scratch_shapes=[pltpu.VMEM((half + 8, n), F32)],
        compiler_params=params(),
        name="tiles",
    )(pos, w, gram, *slabs)


def start(velocity, metric, packed):
    count = lax.axis_size("space")
    space, group = lax.axis_index("space"), lax.axis_index("tm")
    odd = space % 2
    pos = jnp.stack([space // 2, group, odd, lax.axis_size("tm")]).astype(jnp.int32)
    x, column, inward, outward, head, tail = interior(pos, velocity, metric)
    inside = [(i, i ^ 1) for i in range(count)]
    outside = [(i, i + 1) for i in range(1, count - 1, 2)]
    outside += [(j, i) for i, j in outside]
    far = lax.ppermute(outward, "space", outside)
    near = lax.ppermute(inward, "space", inside)
    return pos, panel(pos, (x, head, tail), near, far, column, packed)


def paired_body(velocity, metric):
    groups = lax.axis_size("tm")
    axes = ("space", "tm")
    every = range(groups)
    cores = (0, 1)

    def at(chip, group, core):
        return (2 * chip + core) * groups + group

    def send(value, pairs):
        return lax.ppermute(value, axes, pairs)

    pos, (x, xt, away, mine) = start(velocity, metric, True)

    def hops(sources):
        pairs = [(at(k, z, 0), at(k, (z + 1) % groups, 0)) for k in every for z in sources]
        return pairs + [(at(k, 3 - z, 1), at(k, (2 - z) % groups, 1)) for k in every for z in sources]

    near = send(x, hops(every))

    siblings = [(at(k, z, c), at(k, z, 1 - c)) for k in every for z in every for c in cores]
    mine = mine + send(away, siblings)
    others = [
        send(mine, [(at(k, z, c), at(k ^ m, z, c)) for k in every for z in every for c in cores])
        for m in range(1, groups)
    ]
    for other in others:
        mine = mine + other
    gram = gather_gram(pos, mine, send(mine, siblings))
    state = factor_part(0, 1, (gram,))
    near = passed(near, state[0])
    far = send(near, hops((1, 2)))

    def holder(k, z):
        return 0 if (z - k) % groups == 1 or z - k == 2 else 1

    homes = {(k, z): (k, z, holder(k, z)) for k in every for z in every if k != z}
    far_homes = {pair: home for pair, home in homes.items() if abs(pair[0] - pair[1]) == 2}
    near_homes = {pair: home for pair, home in homes.items() if pair not in far_homes}

    def gathered(block, group_homes):
        return [block] + [
            send(block, [(at(k ^ m, z, c), at(k, z, c)) for k, z, c in group_homes.values()]) for m in range(1, groups)
        ]

    def exchanged(own, group_homes):
        return send(own, [(at(*home), at(*homes[z, k])) for (k, z), home in group_homes.items()])

    near_block = pair_block(state[0], xt, near)
    near_parts = gathered(near_block, near_homes)
    w = factor_part(1, 3, state, (near_block,))[1]
    far_block = pair_block(w, xt, far)
    far_parts = gathered(far_block, far_homes)
    near_own = total(far_block, near_parts)
    near_cross = exchanged(near_own, near_homes)
    far_own = total(far_block, far_parts)
    far_cross = exchanged(far_own, far_homes)
    mine, sib, top = merge(pos, (near_own, near_cross), (far_own, far_cross))
    sib = send(sib, [(at(k, z, c), at(k, z, 1 - c)) for k, z, c in homes.values()])
    top = send(top, [(at(k, z, c), at((k - 1) % groups, z, 1)) for k, z, c in homes.values()])
    return tiles(pos, w, gram, (mine, sib, top))


def general_body(velocity, metric):
    _, (x, xt, gram) = start(velocity, metric, False)
    w = inverse_factor(lax.psum(gram, "space"))
    count = lax.axis_size("tm")
    following = lax.ppermute(x[:, :1], "tm", [(i, (i - 1) % count) for i in range(count)])
    shifted = jnp.concatenate([x[:, 1:], following], axis=1)
    gathered = lax.all_gather(shifted, "tm", axis=1, tiled=True)
    partial = jnp.dot(xt, gathered, preferred_element_type=F32)
    summed = lax.psum_scatter(partial, "space", scatter_dimension=1, tiled=True)
    return mm(w, summed)


def solution(mesh):
    groups = mesh.shape["tm"]
    paired = groups == 4 and mesh.shape["space"] == 8
    return jax.shard_map(
        paired_body if paired else general_body,
        mesh=mesh,
        in_specs=(P(None, "space", "tm"), P("space")),
        out_specs=P("tm", "space"),
        check_vma=False,
    )
```

```python
import functools

import jax
import jax.numpy as jnp
from jax import lax
from jax.experimental import pallas as pl
from jax.experimental.pallas import tpu as pltpu
from jax.sharding import PartitionSpec as P

F32 = jnp.float32
BF16 = jnp.bfloat16
HIGHEST = lax.Precision.HIGHEST
VMEM = pl.BlockSpec(memory_space=pltpu.VMEM)
SMEM = pl.BlockSpec(memory_space=pltpu.SMEM)
LEAF = 64
PIVOTS = 4


def params(mib=40):
    return pltpu.CompilerParams(vmem_limit_bytes=mib * 1024 * 1024)


def cost(flops, moved):
    return pl.CostEstimate(flops=flops, bytes_accessed=moved, transcendentals=0)


EDGE = 16


def combine(first, second, third, center0, center1):
    return third + center0 * second - center1 * first


def interior_kernel(vel_ref, met_ref, x_ref, head_ref, tail_ref):
    rows, cols = vel_ref.shape[1:]
    row = lax.broadcasted_iota(jnp.int32, (rows, cols), 0)
    metric = met_ref[...]

    def gradient(k):
        field = vel_ref[k].astype(F32)
        head_ref[k] = field[:8]
        tail_ref[k] = field[rows - 8 :]
        up = jnp.where(row == rows - 1, 0.0, pltpu.roll(field, rows - 1, 0))
        down = jnp.where(row == 0, 0.0, pltpu.roll(field, 1, 0))
        return metric * (up - down) * 0.5

    first = gradient(0)
    x_ref[0:rows] = first.astype(BF16)
    second = gradient(1)
    x_ref[rows : 2 * rows] = second.astype(BF16)
    third = combine(first, second, gradient(2), vel_ref[0].astype(F32), vel_ref[1].astype(F32))
    x_ref[2 * rows :] = third.astype(BF16)


def interior(velocity, metric):
    _, rows, cols = velocity.shape
    return pl.pallas_call(
        interior_kernel,
        out_shape=(
            jax.ShapeDtypeStruct((3 * rows, cols), BF16),
            jax.ShapeDtypeStruct((3, 8, cols), F32),
            jax.ShapeDtypeStruct((3, 8, cols), F32),
        ),
        in_specs=[VMEM] * 2,
        out_specs=(VMEM,) * 3,
        compiler_params=params(),
        cost_estimate=cost(30 * rows * cols, 12 * rows * cols),
        name="interior",
    )(velocity, metric)


def panel_kernel(pos_ref, x_in_ref, head_ref, tail_ref, near_ref, far_ref, met_ref, x_ref, xt_ref, *g_refs):
    cols = x_ref.shape[1]
    rows = x_ref.shape[0] // 3
    even = pos_ref[2] == 0
    row = lax.broadcasted_iota(jnp.int32, (EDGE, cols), 0)

    def edge(start, gradient, heads, at):
        first, second, third = [gradient(k) for k in range(3)]
        third = combine(first, second, third, heads[0], heads[1])
        for k, value in enumerate((first, second, third)):
            span = slice(k * rows + start, k * rows + start + EDGE)
            kept = x_in_ref[span].astype(F32)
            x_ref[span] = jnp.where(row == at, value, kept).astype(BF16)

    x_ref[...] = x_in_ref[...]
    lo = [jnp.where(even, far_ref[k].astype(F32), near_ref[k].astype(F32)) for k in range(3)]
    hi = [jnp.where(even, near_ref[k].astype(F32), far_ref[k].astype(F32)) for k in range(3)]
    low = met_ref[0:1]
    edge(0, lambda k: low * (head_ref[k, 1:2] - lo[k]) * 0.5, [head_ref[k, 0:1] for k in range(2)], 0)
    high = met_ref[rows - 1 : rows]
    edge(rows - EDGE, lambda k: high * (hi[k] - tail_ref[k, 6:7]) * 0.5, [tail_ref[k, 7:8] for k in range(2)], EDGE - 1)
    xt_ref[...] = x_ref[...].T
    gram = jnp.dot(xt_ref[...], x_ref[...], preferred_element_type=F32)
    if len(g_refs) == 1:
        g_refs[0][...] = gram
        return
    away_ref, mine_ref, g_ref = g_refs
    g_ref[...] = gram
    half = cols // 2
    for ref, core in ((mine_ref, pos_ref[2]), (away_ref, 1 - pos_ref[2])):
        ref[0:half] = jnp.where(core == 0, g_ref[0:half, 0:half], g_ref[half:, half:])
        ref[half:] = jnp.where(core == 0, g_ref[half : half + half // 2, 0:half], g_ref[half + half // 2 :, 0:half])


def panel(pos, inner, near, far, metric, packed):
    x, head, tail = inner
    height, cols = x.shape
    share = jax.ShapeDtypeStruct((3 * cols // 4, cols // 2), F32)
    whole = jax.ShapeDtypeStruct((cols, cols), F32)
    grams = (share, share) if packed else (whole,)
    return pl.pallas_call(
        panel_kernel,
        out_shape=(jax.ShapeDtypeStruct((height, cols), BF16), jax.ShapeDtypeStruct((cols, height), BF16)) + grams,
        in_specs=[SMEM] + [VMEM] * 6,
        out_specs=(VMEM,) * (2 + len(grams)),
        scratch_shapes=[pltpu.VMEM((cols, cols), F32)] if packed else [],
        compiler_params=params(),
        cost_estimate=cost(2 * height * cols * cols, 6 * height * cols),
        name="panel",
    )(pos, x, head, tail, near, far, metric)


def gather_kernel(pos_ref, mine_ref, theirs_ref, g_ref):
    half = mine_ref.shape[1]
    even = pos_ref[2] == 0
    first = jnp.where(even, mine_ref[...], theirs_ref[...])
    second = jnp.where(even, theirs_ref[...], mine_ref[...])
    g_ref[0:half, 0:half] = first[:half]
    g_ref[half:, half:] = second[:half]
    across = jnp.concatenate([first[half:], second[half:]], axis=0)
    g_ref[half:, 0:half] = across
    g_ref[0:half, half:] = across.T


def gather_gram(pos, mine, theirs):
    n = 2 * mine.shape[1]
    return pl.pallas_call(
        gather_kernel,
        out_shape=jax.ShapeDtypeStruct((n, n), F32),
        in_specs=[SMEM, VMEM, VMEM],
        out_specs=VMEM,
        compiler_params=params(),
        name="gather",
    )(pos, mine, theirs)


def passed(value, after):
    return pl.pallas_call(
        lambda *refs: None,
        out_shape=jax.ShapeDtypeStruct(value.shape, value.dtype),
        in_specs=[VMEM, VMEM],
        out_specs=VMEM,
        input_output_aliases={0: 0},
        compiler_params=params(),
        name="passed",
    )(value, after)


def leaf_inverse(block):
    n = block.shape[0]
    row = lax.broadcasted_iota(jnp.int32, (n, 2 * n), 0)
    lane = lax.broadcasted_iota(jnp.int32, (n, 2 * n), 1)
    eye = (row == lane).astype(F32)
    right = (lane == row + n).astype(F32)
    m = jnp.concatenate([block, right[:, n:]], axis=1)
    for j in range(0, n, PIVOTS):
        columns = [jnp.broadcast_to(m[:, j + b : j + b + 1], (n, 2 * n)) for b in range(PIVOTS)]
        pivot_rows = [m[j + a : j + a + 1, :] for a in range(PIVOTS)]
        splat = [[columns[b][j + a : j + a + 1, :] for b in range(PIVOTS)] for a in range(PIVOTS)]
        update = None
        inverses = []
        for a in range(PIVOTS):
            inverse = 1.0 / splat[a][a]
            for b in range(a + 1, PIVOTS):
                ratio = splat[a][b] * inverse
                for c in range(b, PIVOTS):
                    splat[b][c] = splat[b][c] - ratio * splat[a][c]
                pivot_rows[b] = pivot_rows[b] - ratio * pivot_rows[a]
            inverses.append(inverse)
        for a in range(PIVOTS):
            multiplier = jnp.where(row > j + a, columns[a] * inverses[a], 0.0)
            for b in range(a + 1, PIVOTS):
                columns[b] = columns[b] - multiplier * splat[a][b]
            term = multiplier * pivot_rows[a]
            update = term if update is None else update + term
        m = m - update
    diagonal = jnp.sum(m * eye, axis=1, keepdims=True)
    return m[:, n:] * lax.rsqrt(diagonal)


def mm(left, right, dims=((1,), (0,))):
    return lax.dot_general(left, right, (dims, ((), ())), precision=HIGHEST, preferred_element_type=F32)


def factor_kernel(first, leaves, *refs):
    g_ref, w_in_ref = (refs[0], None) if first == 0 else refs[:2]
    a_ref, w_ref = refs[-2:]
    n = g_ref.shape[0]
    a_ref[...] = g_ref[...]
    if first == 0:
        row = lax.broadcasted_iota(jnp.int32, (n, n), 0)
        lane = lax.broadcasted_iota(jnp.int32, (n, n), 1)
        w_ref[...] = (row == lane).astype(F32)
    else:
        w_ref[...] = w_in_ref[...]
    for leaf in range(first, first + leaves):
        j = leaf * LEAF
        k = j + LEAF
        own = slice(j, k)
        w = leaf_inverse(a_ref[own, own])
        done = mm(w, w_ref[own, :])
        w_ref[own, :] = done
        if k < n:
            u = mm(w, a_ref[own, :])
            a_ref[k:, :] -= mm(u[:, k:], u, ((0,), (0,)))
            w_ref[k:, :] -= mm(u[:, k:], done, ((0,), (0,)))


def factor_part(first, leaves, state, after=()):
    n = state[0].shape[0]
    skip = len(after)

    def kernel(*refs):
        factor_kernel(first, leaves, *refs[: len(state)], *refs[len(state) + skip :])

    return pl.pallas_call(
        kernel,
        out_shape=(jax.ShapeDtypeStruct((n, n), F32),) * 2,
        in_specs=[VMEM] * len(state) + [pl.BlockSpec(memory_space=pl.ANY)] * skip,
        out_specs=(VMEM,) * 2,
        compiler_params=params(),
        cost_estimate=cost(2 * n * n * n, 8 * n * n),
        name="factor",
    )(*state, *after)


def inverse_factor(gram):
    return factor_part(0, gram.shape[0] // LEAF, (gram,))[1]


def core_of(chip, group, count):
    behind = (group - chip + count) % count
    return jnp.where((behind == 1) | ((behind == 2) & (group > chip)), 0, 1)


def block_kernel(after_ref, xt_ref, panel_ref, out_ref):
    del after_ref
    out_ref[...] = jnp.dot(xt_ref[...], panel_ref[...], preferred_element_type=F32)


def pair_block(after, xt, panel):
    n = xt.shape[0]
    return pl.pallas_call(
        block_kernel,
        out_shape=jax.ShapeDtypeStruct((n, n), F32),
        in_specs=[pl.BlockSpec(memory_space=pl.ANY)] + [VMEM] * 2,
        out_specs=VMEM,
        compiler_params=params(),
        cost_estimate=cost(2 * n * n * xt.shape[1], 4 * n * n),
        name="block",
    )(after, xt, panel)


def total_kernel(after_ref, *refs):
    del after_ref
    value = refs[0][...]
    for ref in refs[1:-1]:
        value = value + ref[...]
    refs[-1][...] = value


def total(after, parts):
    n = parts[0].shape[0]
    return pl.pallas_call(
        total_kernel,
        out_shape=jax.ShapeDtypeStruct((n, n), F32),
        in_specs=[pl.BlockSpec(memory_space=pl.ANY)] + [VMEM] * len(parts),
        out_specs=VMEM,
        compiler_params=params(),
        name="total",
    )(after, *parts)


def merge_kernel(pos_ref, after_ref, *refs):
    del after_ref
    sums, (mine_ref, sib_ref, top_ref, t_ref) = refs[:4], refs[4:]
    n = t_ref.shape[0] - 8
    half = n // 2
    chip, group, core = pos_ref[0], pos_ref[1], pos_ref[2]

    def put(own_ref, cross_ref):
        t_ref[0:n] = own_ref[...].T + cross_ref[...]

    distant = jnp.abs(chip - group) == 2
    pl.when(jnp.logical_not(distant))(lambda: put(*sums[:2]))
    pl.when(distant)(lambda: put(*sums[2:]))
    top_ref[...] = t_ref[0:8]
    mine_ref[...] = t_ref[pl.ds(pl.multiple_of(core * half, 8), half + 8)]
    sib_ref[...] = t_ref[pl.ds(pl.multiple_of((1 - core) * half, 8), half + 8)]


def merge(pos, after, near, far):
    n = near[0].shape[0]
    half = n // 2
    return pl.pallas_call(
        merge_kernel,
        out_shape=tuple(jax.ShapeDtypeStruct((r, n), F32) for r in (half + 8, half + 8, 8)),
        in_specs=[SMEM, pl.BlockSpec(memory_space=pl.ANY)] + [VMEM] * 4,
        out_specs=(VMEM,) * 3,
        scratch_shapes=[pltpu.VMEM((n + 8, n), F32)],
        compiler_params=params(),
        name="merge",
    )(pos, after, *near, *far)


def tiles_kernel(pos_ref, w_ref, g_ref, own_ref, sib_ref, top_ref, out_ref, p_ref):
    chip, group, core, count = pos_ref[0], pos_ref[1], pos_ref[2], pos_ref[3]
    half = out_ref.shape[1]
    following = jnp.where(chip + 1 == count, 0, chip + 1)
    owner = core_of(chip, group, count)

    @pl.when(chip == group)
    def _():
        p_ref[0:half] = g_ref[pl.ds(pl.multiple_of(core * half, 8), half)]
        p_ref[half:] = g_ref[half : half + 8]

    @pl.when(chip != group)
    def _():
        p_ref[...] = jnp.where(core == owner, own_ref[...], sib_ref[...])

    @pl.when(core != 0)
    def _():
        p_ref[half:] = jnp.where(following == group, g_ref[0:8], top_ref[...])

    shifted = pltpu.roll(p_ref[...], half + 7, 0)[:half]
    out_ref[...] = mm(w_ref[...], shifted, ((1,), (1,)))


def tiles(pos, w, gram, slabs):
    n = w.shape[0]
    half = n // 2
    return pl.pallas_call(
        tiles_kernel,
        out_shape=jax.ShapeDtypeStruct((n, half), F32),
        in_specs=[SMEM] + [VMEM] * 5,
        out_specs=VMEM,
        scratch_shapes=[pltpu.VMEM((half + 8, n), F32)],
        compiler_params=params(),
        name="tiles",
    )(pos, w, gram, *slabs)


def start(velocity, metric, packed):
    count = lax.axis_size("space")
    space, group = lax.axis_index("space"), lax.axis_index("tm")
    odd = space % 2
    pos = jnp.stack([space // 2, group, odd, lax.axis_size("tm")]).astype(jnp.int32)
    head, tail = velocity[:, :1], velocity[:, -1:]
    inside = [(i, i ^ 1) for i in range(count)]
    outside = [(i, i + 1) for i in range(1, count - 1, 2)]
    outside += [(j, i) for i, j in outside]
    far = lax.ppermute(jnp.where(odd == 0, head, tail), "space", outside)
    near = lax.ppermute(jnp.where(odd == 0, tail, head), "space", inside)
    column = metric.reshape(-1, 1)
    return pos, panel(pos, interior(velocity, column), near, far, column, packed)


def paired_body(velocity, metric):
    groups = lax.axis_size("tm")
    axes = ("space", "tm")
    every = range(groups)
    cores = (0, 1)

    def at(chip, group, core):
        return (2 * chip + core) * groups + group

    def send(value, pairs):
        return lax.ppermute(value, axes, pairs)

    pos, (x, xt, away, mine) = start(velocity, metric, True)

    def hops(sources):
        pairs = [(at(k, z, 0), at(k, (z + 1) % groups, 0)) for k in every for z in sources]
        return pairs + [(at(k, 3 - z, 1), at(k, (2 - z) % groups, 1)) for k in every for z in sources]

    near = send(x, hops(every))

    siblings = [(at(k, z, c), at(k, z, 1 - c)) for k in every for z in every for c in cores]
    mine = mine + send(away, siblings)
    others = [
        send(mine, [(at(k, z, c), at(k ^ m, z, c)) for k in every for z in every for c in cores])
        for m in range(1, groups)
    ]
    for other in others:
        mine = mine + other
    gram = gather_gram(pos, mine, send(mine, siblings))
    state = factor_part(0, 1, (gram,))
    near = passed(near, state[0])
    far = send(near, hops((1, 2)))

    def holder(k, z):
        return 0 if (z - k) % groups == 1 or z - k == 2 else 1

    homes = {(k, z): (k, z, holder(k, z)) for k in every for z in every if k != z}
    far_homes = {pair: home for pair, home in homes.items() if abs(pair[0] - pair[1]) == 2}
    near_homes = {pair: home for pair, home in homes.items() if pair not in far_homes}

    def gathered(block, group_homes):
        return [block] + [
            send(block, [(at(k ^ m, z, c), at(k, z, c)) for k, z, c in group_homes.values()]) for m in range(1, groups)
        ]

    def exchanged(own, group_homes):
        return send(own, [(at(*home), at(*homes[z, k])) for (k, z), home in group_homes.items()])

    near_block = pair_block(state[0], xt, near)
    near_parts = gathered(near_block, near_homes)
    state = factor_part(1, 1, state, (near_block,))
    far_block = pair_block(state[0], xt, far)
    far_parts = gathered(far_block, far_homes)
    state = factor_part(2, 1, state, (far_block,))
    near_own = total(state[0], near_parts)
    near_cross = exchanged(near_own, near_homes)
    far_own = total(state[0], far_parts)
    far_cross = exchanged(far_own, far_homes)
    w = factor_part(3, 1, state, (far_own,))[1]
    mine, sib, top = merge(pos, w, (near_own, near_cross), (far_own, far_cross))
    sib = send(sib, [(at(k, z, c), at(k, z, 1 - c)) for k, z, c in homes.values()])
    top = send(top, [(at(k, z, c), at((k - 1) % groups, z, 1)) for k, z, c in homes.values()])
    return tiles(pos, w, gram, (mine, sib, top))


def general_body(velocity, metric):
    _, (x, xt, gram) = start(velocity, metric, False)
    w = inverse_factor(lax.psum(gram, "space"))
    count = lax.axis_size("tm")
    following = lax.ppermute(x[:, :1], "tm", [(i, (i - 1) % count) for i in range(count)])
    shifted = jnp.concatenate([x[:, 1:], following], axis=1)
    gathered = lax.all_gather(shifted, "tm", axis=1, tiled=True)
    partial = jnp.dot(xt, gathered, preferred_element_type=F32)
    summed = lax.psum_scatter(partial, "space", scatter_dimension=1, tiled=True)
    return mm(w, summed)


def solution(mesh):
    groups = mesh.shape["tm"]
    paired = groups == 4 and mesh.shape["space"] == 8
    return jax.shard_map(
        paired_body if paired else general_body,
        mesh=mesh,
        in_specs=(P(None, "space", "tm"), P("space")),
        out_specs=P("tm", "space"),
        check_vma=False,
    )
```

```python
import functools

import jax
import jax.numpy as jnp
from jax import lax
from jax.experimental import pallas as pl
from jax.experimental.pallas import tpu as pltpu
from jax.sharding import PartitionSpec as P

F32 = jnp.float32
BF16 = jnp.bfloat16
HIGHEST = lax.Precision.HIGHEST
VMEM = pl.BlockSpec(memory_space=pltpu.VMEM)
SMEM = pl.BlockSpec(memory_space=pltpu.SMEM)
LEAF = 64
PIVOTS = 4


def params(mib=40):
    return pltpu.CompilerParams(vmem_limit_bytes=mib * 1024 * 1024)


def cost(flops, moved):
    return pl.CostEstimate(flops=flops, bytes_accessed=moved, transcendentals=0)


EDGE = 16


def combine(first, second, third, center0, center1):
    return third + center0 * second - center1 * first


def interior_kernel(vel_ref, met_ref, x_ref, head_ref, tail_ref):
    rows, cols = vel_ref.shape[1:]
    row = lax.broadcasted_iota(jnp.int32, (rows, cols), 0)
    metric = met_ref[...]

    def gradient(k):
        field = vel_ref[k].astype(F32)
        head_ref[k] = field[:8]
        tail_ref[k] = field[rows - 8 :]
        up = jnp.where(row == rows - 1, 0.0, pltpu.roll(field, rows - 1, 0))
        down = jnp.where(row == 0, 0.0, pltpu.roll(field, 1, 0))
        return metric * (up - down) * 0.5

    first = gradient(0)
    x_ref[0:rows] = first.astype(BF16)
    second = gradient(1)
    x_ref[rows : 2 * rows] = second.astype(BF16)
    third = combine(first, second, gradient(2), vel_ref[0].astype(F32), vel_ref[1].astype(F32))
    x_ref[2 * rows :] = third.astype(BF16)


def interior(velocity, metric):
    _, rows, cols = velocity.shape
    return pl.pallas_call(
        interior_kernel,
        out_shape=(
            jax.ShapeDtypeStruct((3 * rows, cols), BF16),
            jax.ShapeDtypeStruct((3, 8, cols), F32),
            jax.ShapeDtypeStruct((3, 8, cols), F32),
        ),
        in_specs=[VMEM] * 2,
        out_specs=(VMEM,) * 3,
        compiler_params=params(),
        cost_estimate=cost(30 * rows * cols, 12 * rows * cols),
        name="interior",
    )(velocity, metric)


def panel_kernel(pos_ref, x_in_ref, head_ref, tail_ref, near_ref, far_ref, met_ref, x_ref, xt_ref, *g_refs):
    cols = x_ref.shape[1]
    rows = x_ref.shape[0] // 3
    even = pos_ref[2] == 0
    row = lax.broadcasted_iota(jnp.int32, (EDGE, cols), 0)

    def edge(start, gradient, heads, at):
        first, second, third = [gradient(k) for k in range(3)]
        third = combine(first, second, third, heads[0], heads[1])
        for k, value in enumerate((first, second, third)):
            span = slice(k * rows + start, k * rows + start + EDGE)
            kept = x_in_ref[span].astype(F32)
            x_ref[span] = jnp.where(row == at, value, kept).astype(BF16)

    x_ref[...] = x_in_ref[...]
    lo = [jnp.where(even, far_ref[k].astype(F32), near_ref[k].astype(F32)) for k in range(3)]
    hi = [jnp.where(even, near_ref[k].astype(F32), far_ref[k].astype(F32)) for k in range(3)]
    low = met_ref[0:1]
    edge(0, lambda k: low * (head_ref[k, 1:2] - lo[k]) * 0.5, [head_ref[k, 0:1] for k in range(2)], 0)
    high = met_ref[rows - 1 : rows]
    edge(rows - EDGE, lambda k: high * (hi[k] - tail_ref[k, 6:7]) * 0.5, [tail_ref[k, 7:8] for k in range(2)], EDGE - 1)
    xt_ref[...] = x_ref[...].T
    gram = jnp.dot(xt_ref[...], x_ref[...], preferred_element_type=F32)
    if len(g_refs) == 1:
        g_refs[0][...] = gram
        return
    away_ref, mine_ref, g_ref = g_refs
    g_ref[...] = gram
    half = cols // 2
    for ref, core in ((mine_ref, pos_ref[2]), (away_ref, 1 - pos_ref[2])):
        ref[0:half] = jnp.where(core == 0, g_ref[0:half, 0:half], g_ref[half:, half:])
        ref[half:] = jnp.where(core == 0, g_ref[half : half + half // 2, 0:half], g_ref[half + half // 2 :, 0:half])


def panel(pos, inner, near, far, metric, packed):
    x, head, tail = inner
    height, cols = x.shape
    share = jax.ShapeDtypeStruct((3 * cols // 4, cols // 2), F32)
    whole = jax.ShapeDtypeStruct((cols, cols), F32)
    grams = (share, share) if packed else (whole,)
    return pl.pallas_call(
        panel_kernel,
        out_shape=(jax.ShapeDtypeStruct((height, cols), BF16), jax.ShapeDtypeStruct((cols, height), BF16)) + grams,
        in_specs=[SMEM] + [VMEM] * 6,
        out_specs=(VMEM,) * (2 + len(grams)),
        scratch_shapes=[pltpu.VMEM((cols, cols), F32)] if packed else [],
        compiler_params=params(),
        cost_estimate=cost(2 * height * cols * cols, 6 * height * cols),
        name="panel",
    )(pos, x, head, tail, near, far, metric)


def gather_kernel(pos_ref, mine_ref, theirs_ref, g_ref):
    half = mine_ref.shape[1]
    even = pos_ref[2] == 0
    first = jnp.where(even, mine_ref[...], theirs_ref[...])
    second = jnp.where(even, theirs_ref[...], mine_ref[...])
    g_ref[0:half, 0:half] = first[:half]
    g_ref[half:, half:] = second[:half]
    across = jnp.concatenate([first[half:], second[half:]], axis=0)
    g_ref[half:, 0:half] = across
    g_ref[0:half, half:] = across.T


def gather_gram(pos, mine, theirs):
    n = 2 * mine.shape[1]
    return pl.pallas_call(
        gather_kernel,
        out_shape=jax.ShapeDtypeStruct((n, n), F32),
        in_specs=[SMEM, VMEM, VMEM],
        out_specs=VMEM,
        compiler_params=params(),
        name="gather",
    )(pos, mine, theirs)


def passed(value, after):
    return pl.pallas_call(
        lambda *refs: None,
        out_shape=jax.ShapeDtypeStruct(value.shape, value.dtype),
        in_specs=[VMEM, VMEM],
        out_specs=VMEM,
        input_output_aliases={0: 0},
        compiler_params=params(),
        name="passed",
    )(value, after)


def leaf_inverse(block):
    n = block.shape[0]
    row = lax.broadcasted_iota(jnp.int32, (n, 2 * n), 0)
    lane = lax.broadcasted_iota(jnp.int32, (n, 2 * n), 1)
    eye = (row == lane).astype(F32)
    right = (lane == row + n).astype(F32)
    m = jnp.concatenate([block, right[:, n:]], axis=1)
    for j in range(0, n, PIVOTS):
        columns = [jnp.broadcast_to(m[:, j + b : j + b + 1], (n, 2 * n)) for b in range(PIVOTS)]
        pivot_rows = [m[j + a : j + a + 1, :] for a in range(PIVOTS)]
        splat = [[columns[b][j + a : j + a + 1, :] for b in range(PIVOTS)] for a in range(PIVOTS)]
        update = None
        inverses = []
        for a in range(PIVOTS):
            inverse = 1.0 / splat[a][a]
            for b in range(a + 1, PIVOTS):
                ratio = splat[a][b] * inverse
                for c in range(b, PIVOTS):
                    splat[b][c] = splat[b][c] - ratio * splat[a][c]
                pivot_rows[b] = pivot_rows[b] - ratio * pivot_rows[a]
            inverses.append(inverse)
        for a in range(PIVOTS):
            multiplier = jnp.where(row > j + a, columns[a] * inverses[a], 0.0)
            for b in range(a + 1, PIVOTS):
                columns[b] = columns[b] - multiplier * splat[a][b]
            term = multiplier * pivot_rows[a]
            update = term if update is None else update + term
        m = m - update
    diagonal = jnp.sum(m * eye, axis=1, keepdims=True)
    return m[:, n:] * lax.rsqrt(diagonal)


def mm(left, right, dims=((1,), (0,))):
    return lax.dot_general(left, right, (dims, ((), ())), precision=HIGHEST, preferred_element_type=F32)


def factor_kernel(first, leaves, *refs):
    g_ref, w_in_ref = (refs[0], None) if first == 0 else refs[:2]
    a_ref, w_ref = refs[-2:]
    n = g_ref.shape[0]
    a_ref[...] = g_ref[...]
    if first == 0:
        row = lax.broadcasted_iota(jnp.int32, (n, n), 0)
        lane = lax.broadcasted_iota(jnp.int32, (n, n), 1)
        w_ref[...] = (row == lane).astype(F32)
    else:
        w_ref[...] = w_in_ref[...]
    for leaf in range(first, first + leaves):
        j = leaf * LEAF
        k = j + LEAF
        own = slice(j, k)
        w = leaf_inverse(a_ref[own, own])
        done = mm(w, w_ref[own, :])
        w_ref[own, :] = done
        if k < n:
            u = mm(w, a_ref[own, :])
            a_ref[k:, :] -= mm(u[:, k:], u, ((0,), (0,)))
            w_ref[k:, :] -= mm(u[:, k:], done, ((0,), (0,)))


def factor_part(first, leaves, state, after=()):
    n = state[0].shape[0]
    skip = len(after)

    def kernel(*refs):
        factor_kernel(first, leaves, *refs[: len(state)], *refs[len(state) + skip :])

    return pl.pallas_call(
        kernel,
        out_shape=(jax.ShapeDtypeStruct((n, n), F32),) * 2,
        in_specs=[VMEM] * len(state) + [pl.BlockSpec(memory_space=pl.ANY)] * skip,
        out_specs=(VMEM,) * 2,
        compiler_params=params(),
        cost_estimate=cost(2 * n * n * n, 8 * n * n),
        name="factor",
    )(*state, *after)


def inverse_factor(gram):
    return factor_part(0, gram.shape[0] // LEAF, (gram,))[1]


def core_of(chip, group, count):
    behind = (group - chip + count) % count
    return jnp.where((behind == 1) | ((behind == 2) & (group > chip)), 0, 1)


TOP = 14.0
TAIL = 16


def block_kernel(after_ref, xt_ref, panel_ref, out_ref):
    del after_ref
    n = xt_ref.shape[0]
    block = jnp.dot(xt_ref[...], panel_ref[...], preferred_element_type=F32)
    peak = jnp.max(jnp.abs(block), axis=(0, 1), keepdims=True)
    exponent = jnp.ceil(jnp.log2(jnp.maximum(peak, 1e-30)))
    out_ref[0:n] = block * jnp.exp2(TOP - exponent)
    out_ref[n:] = jnp.broadcast_to(exponent, (TAIL, n))


def pair_block(after, xt, panel):
    n = xt.shape[0]
    return pl.pallas_call(
        block_kernel,
        out_shape=jax.ShapeDtypeStruct((n + TAIL, n), F32),
        in_specs=[pl.BlockSpec(memory_space=pl.ANY)] + [VMEM] * 2,
        out_specs=VMEM,
        compiler_params=params(),
        cost_estimate=cost(2 * n * n * xt.shape[1], 4 * n * n),
        name="block",
    )(after, xt, panel)


def total(parts):
    parts = [part.astype(F32) for part in parts]
    n = parts[0].shape[1]
    exponents = [part[n : n + 1, 0:1] for part in parts]
    value = sum(part[:n] * jnp.exp2(exponent - TOP) for part, exponent in zip(parts, exponents))
    exponent = functools.reduce(jnp.maximum, exponents) + 2.0
    packed = jnp.concatenate([value * jnp.exp2(TOP - exponent), jnp.broadcast_to(exponent, (TAIL, n))])
    return value, packed.astype(jnp.float16)


def merge_kernel(pos_ref, after_ref, *refs):
    del after_ref
    sums, (mine_ref, sib_ref, top_ref, t_ref) = refs[:4], refs[4:]
    n = t_ref.shape[0] - 8
    half = n // 2
    chip, group, core = pos_ref[0], pos_ref[1], pos_ref[2]

    def put(own_ref, cross_ref):
        t_ref[0:n] = own_ref[...].T + cross_ref[0:n] * jnp.exp2(cross_ref[n : n + 1, 0:1] - TOP)

    distant = jnp.abs(chip - group) == 2
    pl.when(jnp.logical_not(distant))(lambda: put(*sums[:2]))
    pl.when(distant)(lambda: put(*sums[2:]))
    top_ref[...] = t_ref[0:8]
    mine_ref[...] = t_ref[pl.ds(pl.multiple_of(core * half, 8), half + 8)]
    sib_ref[...] = t_ref[pl.ds(pl.multiple_of((1 - core) * half, 8), half + 8)]


def merge(pos, after, near, far):
    n = near[0].shape[0]
    half = n // 2
    return pl.pallas_call(
        merge_kernel,
        out_shape=tuple(jax.ShapeDtypeStruct((r, n), F32) for r in (half + 8, half + 8, 8)),
        in_specs=[SMEM, pl.BlockSpec(memory_space=pl.ANY)] + [VMEM] * 4,
        out_specs=(VMEM,) * 3,
        scratch_shapes=[pltpu.VMEM((n + 8, n), F32)],
        compiler_params=params(),
        name="merge",
    )(pos, after, *near, *far)


def tiles_kernel(pos_ref, w_ref, g_ref, own_ref, sib_ref, top_ref, out_ref, p_ref):
    chip, group, core, count = pos_ref[0], pos_ref[1], pos_ref[2], pos_ref[3]
    half = out_ref.shape[1]
    following = jnp.where(chip + 1 == count, 0, chip + 1)
    owner = core_of(chip, group, count)

    @pl.when(chip == group)
    def _():
        p_ref[0:half] = g_ref[pl.ds(pl.multiple_of(core * half, 8), half)]
        p_ref[half:] = g_ref[half : half + 8]

    @pl.when(chip != group)
    def _():
        p_ref[...] = jnp.where(core == owner, own_ref[...], sib_ref[...])

    @pl.when(core != 0)
    def _():
        p_ref[half:] = jnp.where(following == group, g_ref[0:8], top_ref[...])

    shifted = pltpu.roll(p_ref[...], half + 7, 0)[:half]
    out_ref[...] = mm(w_ref[...], shifted, ((1,), (1,)))


def tiles(pos, w, gram, slabs):
    n = w.shape[0]
    half = n // 2
    return pl.pallas_call(
        tiles_kernel,
        out_shape=jax.ShapeDtypeStruct((n, half), F32),
        in_specs=[SMEM] + [VMEM] * 5,
        out_specs=VMEM,
        scratch_shapes=[pltpu.VMEM((half + 8, n), F32)],
        compiler_params=params(),
        name="tiles",
    )(pos, w, gram, *slabs)


def start(velocity, metric, packed):
    count = lax.axis_size("space")
    space, group = lax.axis_index("space"), lax.axis_index("tm")
    odd = space % 2
    pos = jnp.stack([space // 2, group, odd, lax.axis_size("tm")]).astype(jnp.int32)
    head, tail = velocity[:, :1], velocity[:, -1:]
    inside = [(i, i ^ 1) for i in range(count)]
    outside = [(i, i + 1) for i in range(1, count - 1, 2)]
    outside += [(j, i) for i, j in outside]
    far = lax.ppermute(jnp.where(odd == 0, head, tail), "space", outside)
    near = lax.ppermute(jnp.where(odd == 0, tail, head), "space", inside)
    column = metric.reshape(-1, 1)
    return pos, panel(pos, interior(velocity, column), near, far, column, packed)


def paired_body(velocity, metric):
    groups = lax.axis_size("tm")
    axes = ("space", "tm")
    every = range(groups)
    cores = (0, 1)

    def at(chip, group, core):
        return (2 * chip + core) * groups + group

    def send(value, pairs):
        return lax.ppermute(value, axes, pairs)

    pos, (x, xt, away, mine) = start(velocity, metric, True)

    def hops(sources):
        pairs = [(at(k, z, 0), at(k, (z + 1) % groups, 0)) for k in every for z in sources]
        return pairs + [(at(k, 3 - z, 1), at(k, (2 - z) % groups, 1)) for k in every for z in sources]

    near = send(x, hops(every))

    siblings = [(at(k, z, c), at(k, z, 1 - c)) for k in every for z in every for c in cores]
    mine = mine + send(away, siblings)
    others = [
        send(mine, [(at(k, z, c), at(k ^ m, z, c)) for k in every for z in every for c in cores])
        for m in range(1, groups)
    ]
    for other in others:
        mine = mine + other
    gram = gather_gram(pos, mine, send(mine, siblings))
    state = factor_part(0, 1, (gram,))
    near = passed(near, state[0])
    far = send(near, hops((1, 2)))

    def holder(k, z):
        return 0 if (z - k) % groups == 1 or z - k == 2 else 1

    homes = {(k, z): (k, z, holder(k, z)) for k in every for z in every if k != z}
    far_homes = {pair: home for pair, home in homes.items() if abs(pair[0] - pair[1]) == 2}
    near_homes = {pair: home for pair, home in homes.items() if pair not in far_homes}

    def gathered(block, group_homes):
        half = block.astype(jnp.float16)
        return [block] + [
            send(half, [(at(k ^ m, z, c), at(k, z, c)) for k, z, c in group_homes.values()]) for m in range(1, groups)
        ]

    def exchanged(packed, group_homes):
        received = send(packed, [(at(*home), at(*homes[z, k])) for (k, z), home in group_homes.items()])
        return received.astype(F32)

    near_block = pair_block(state[0], xt, near)
    near_parts = gathered(near_block, near_homes)
    state = factor_part(1, 1, state, (near_block,))
    far_block = pair_block(state[0], xt, far)
    far_parts = gathered(far_block, far_homes)
    state = factor_part(2, 1, state, (far_block,))
    near_own, packed = total([passed(near_parts[0], state[0])] + near_parts[1:])
    near_cross = exchanged(packed, near_homes)
    far_own, packed = total(far_parts)
    far_cross = exchanged(packed, far_homes)
    w = factor_part(3, 1, state, (far_own,))[1]
    mine, sib, top = merge(pos, w, (near_own, near_cross), (far_own, far_cross))
    sib = send(sib, [(at(k, z, c), at(k, z, 1 - c)) for k, z, c in homes.values()])
    top = send(top, [(at(k, z, c), at((k - 1) % groups, z, 1)) for k, z, c in homes.values()])
    return tiles(pos, w, gram, (mine, sib, top))


def general_body(velocity, metric):
    _, (x, xt, gram) = start(velocity, metric, False)
    w = inverse_factor(lax.psum(gram, "space"))
    count = lax.axis_size("tm")
    following = lax.ppermute(x[:, :1], "tm", [(i, (i - 1) % count) for i in range(count)])
    shifted = jnp.concatenate([x[:, 1:], following], axis=1)
    gathered = lax.all_gather(shifted, "tm", axis=1, tiled=True)
    partial = jnp.dot(xt, gathered, preferred_element_type=F32)
    summed = lax.psum_scatter(partial, "space", scatter_dimension=1, tiled=True)
    return mm(w, summed)


def solution(mesh):
    groups = mesh.shape["tm"]
    paired = groups == 4 and mesh.shape["space"] == 8
    return jax.shard_map(
        paired_body if paired else general_body,
        mesh=mesh,
        in_specs=(P(None, "space", "tm"), P("space")),
        out_specs=P("tm", "space"),
        check_vma=False,
    )
```

```python
import functools

import jax
import jax.numpy as jnp
from jax import lax
from jax.experimental import pallas as pl
from jax.experimental.pallas import tpu as pltpu
from jax.sharding import PartitionSpec as P

F32 = jnp.float32
BF16 = jnp.bfloat16
HIGHEST = lax.Precision.HIGHEST
VMEM = pl.BlockSpec(memory_space=pltpu.VMEM)
SMEM = pl.BlockSpec(memory_space=pltpu.SMEM)
LEAF = 64
PIVOTS = 4


def params(mib=40):
    return pltpu.CompilerParams(vmem_limit_bytes=mib * 1024 * 1024)


def cost(flops, moved):
    return pl.CostEstimate(flops=flops, bytes_accessed=moved, transcendentals=0)


EDGE = 16


def combine(first, second, third, center0, center1):
    return third + center0 * second - center1 * first


def interior_kernel(vel_ref, met_ref, x_ref, head_ref, tail_ref):
    rows, cols = vel_ref.shape[1:]
    row = lax.broadcasted_iota(jnp.int32, (rows, cols), 0)
    metric = met_ref[...]

    def gradient(k):
        field = vel_ref[k].astype(F32)
        head_ref[k] = field[:8]
        tail_ref[k] = field[rows - 8 :]
        up = jnp.where(row == rows - 1, 0.0, pltpu.roll(field, rows - 1, 0))
        down = jnp.where(row == 0, 0.0, pltpu.roll(field, 1, 0))
        return metric * (up - down) * 0.5

    first = gradient(0)
    x_ref[0:rows] = first.astype(BF16)
    second = gradient(1)
    x_ref[rows : 2 * rows] = second.astype(BF16)
    third = combine(first, second, gradient(2), vel_ref[0].astype(F32), vel_ref[1].astype(F32))
    x_ref[2 * rows :] = third.astype(BF16)


def interior(velocity, metric):
    _, rows, cols = velocity.shape
    return pl.pallas_call(
        interior_kernel,
        out_shape=(
            jax.ShapeDtypeStruct((3 * rows, cols), BF16),
            jax.ShapeDtypeStruct((3, 8, cols), F32),
            jax.ShapeDtypeStruct((3, 8, cols), F32),
        ),
        in_specs=[VMEM] * 2,
        out_specs=(VMEM,) * 3,
        compiler_params=params(),
        cost_estimate=cost(30 * rows * cols, 12 * rows * cols),
        name="interior",
    )(velocity, metric)


def panel_kernel(pos_ref, x_in_ref, head_ref, tail_ref, near_ref, far_ref, met_ref, x_ref, xt_ref, *g_refs):
    cols = x_ref.shape[1]
    rows = x_ref.shape[0] // 3
    even = pos_ref[2] == 0
    row = lax.broadcasted_iota(jnp.int32, (EDGE, cols), 0)

    def edge(start, gradient, heads, at):
        first, second, third = [gradient(k) for k in range(3)]
        third = combine(first, second, third, heads[0], heads[1])
        for k, value in enumerate((first, second, third)):
            span = slice(k * rows + start, k * rows + start + EDGE)
            kept = x_in_ref[span].astype(F32)
            x_ref[span] = jnp.where(row == at, value, kept).astype(BF16)

    x_ref[...] = x_in_ref[...]
    lo = [jnp.where(even, far_ref[k].astype(F32), near_ref[k].astype(F32)) for k in range(3)]
    hi = [jnp.where(even, near_ref[k].astype(F32), far_ref[k].astype(F32)) for k in range(3)]
    low = met_ref[0:1]
    edge(0, lambda k: low * (head_ref[k, 1:2] - lo[k]) * 0.5, [head_ref[k, 0:1] for k in range(2)], 0)
    high = met_ref[rows - 1 : rows]
    edge(rows - EDGE, lambda k: high * (hi[k] - tail_ref[k, 6:7]) * 0.5, [tail_ref[k, 7:8] for k in range(2)], EDGE - 1)
    xt_ref[...] = x_ref[...].T
    gram = jnp.dot(xt_ref[...], x_ref[...], preferred_element_type=F32)
    if len(g_refs) == 1:
        g_refs[0][...] = gram
        return
    away_ref, mine_ref, g_ref = g_refs
    g_ref[...] = gram
    half = cols // 2
    for ref, core in ((mine_ref, pos_ref[2]), (away_ref, 1 - pos_ref[2])):
        ref[0:half] = jnp.where(core == 0, g_ref[0:half, 0:half], g_ref[half:, half:])
        ref[half:] = jnp.where(core == 0, g_ref[half : half + half // 2, 0:half], g_ref[half + half // 2 :, 0:half])


def panel(pos, inner, near, far, metric, packed):
    x, head, tail = inner
    height, cols = x.shape
    share = jax.ShapeDtypeStruct((3 * cols // 4, cols // 2), F32)
    whole = jax.ShapeDtypeStruct((cols, cols), F32)
    grams = (share, share) if packed else (whole,)
    return pl.pallas_call(
        panel_kernel,
        out_shape=(jax.ShapeDtypeStruct((height, cols), BF16), jax.ShapeDtypeStruct((cols, height), BF16)) + grams,
        in_specs=[SMEM] + [VMEM] * 6,
        out_specs=(VMEM,) * (2 + len(grams)),
        scratch_shapes=[pltpu.VMEM((cols, cols), F32)] if packed else [],
        compiler_params=params(),
        cost_estimate=cost(2 * height * cols * cols, 6 * height * cols),
        name="panel",
    )(pos, x, head, tail, near, far, metric)


def gather_kernel(pos_ref, mine_ref, theirs_ref, g_ref):
    half = mine_ref.shape[1]
    even = pos_ref[2] == 0
    first = jnp.where(even, mine_ref[...], theirs_ref[...])
    second = jnp.where(even, theirs_ref[...], mine_ref[...])
    g_ref[0:half, 0:half] = first[:half]
    g_ref[half:, half:] = second[:half]
    across = jnp.concatenate([first[half:], second[half:]], axis=0)
    g_ref[half:, 0:half] = across
    g_ref[0:half, half:] = across.T


def gather_gram(pos, mine, theirs):
    n = 2 * mine.shape[1]
    return pl.pallas_call(
        gather_kernel,
        out_shape=jax.ShapeDtypeStruct((n, n), F32),
        in_specs=[SMEM, VMEM, VMEM],
        out_specs=VMEM,
        compiler_params=params(),
        name="gather",
    )(pos, mine, theirs)


def passed(value, after):
    return pl.pallas_call(
        lambda *refs: None,
        out_shape=jax.ShapeDtypeStruct(value.shape, value.dtype),
        in_specs=[VMEM, VMEM],
        out_specs=VMEM,
        input_output_aliases={0: 0},
        compiler_params=params(),
        name="passed",
    )(value, after)


def leaf_inverse(block):
    n = block.shape[0]
    row = lax.broadcasted_iota(jnp.int32, (n, 2 * n), 0)
    lane = lax.broadcasted_iota(jnp.int32, (n, 2 * n), 1)
    eye = (row == lane).astype(F32)
    right = (lane == row + n).astype(F32)
    m = jnp.concatenate([block, right[:, n:]], axis=1)
    for j in range(0, n, PIVOTS):
        columns = [jnp.broadcast_to(m[:, j + b : j + b + 1], (n, 2 * n)) for b in range(PIVOTS)]
        pivot_rows = [m[j + a : j + a + 1, :] for a in range(PIVOTS)]
        splat = [[columns[b][j + a : j + a + 1, :] for b in range(PIVOTS)] for a in range(PIVOTS)]
        update = None
        inverses = []
        for a in range(PIVOTS):
            inverse = 1.0 / splat[a][a]
            for b in range(a + 1, PIVOTS):
                ratio = splat[a][b] * inverse
                for c in range(b, PIVOTS):
                    splat[b][c] = splat[b][c] - ratio * splat[a][c]
                pivot_rows[b] = pivot_rows[b] - ratio * pivot_rows[a]
            inverses.append(inverse)
        for a in range(PIVOTS):
            multiplier = jnp.where(row > j + a, columns[a] * inverses[a], 0.0)
            for b in range(a + 1, PIVOTS):
                columns[b] = columns[b] - multiplier * splat[a][b]
            term = multiplier * pivot_rows[a]
            update = term if update is None else update + term
        m = m - update
    diagonal = jnp.sum(m * eye, axis=1, keepdims=True)
    return m[:, n:] * lax.rsqrt(diagonal)


def mm(left, right, dims=((1,), (0,))):
    return lax.dot_general(left, right, (dims, ((), ())), precision=HIGHEST, preferred_element_type=F32)


def factor_kernel(first, leaves, *refs):
    g_ref, w_in_ref = (refs[0], None) if first == 0 else refs[:2]
    a_ref, w_ref = refs[-2:]
    n = g_ref.shape[0]
    a_ref[...] = g_ref[...]
    if first == 0:
        row = lax.broadcasted_iota(jnp.int32, (n, n), 0)
        lane = lax.broadcasted_iota(jnp.int32, (n, n), 1)
        w_ref[...] = (row == lane).astype(F32)
    else:
        w_ref[...] = w_in_ref[...]
    for leaf in range(first, first + leaves):
        j = leaf * LEAF
        k = j + LEAF
        own = slice(j, k)
        w = leaf_inverse(a_ref[own, own])
        done = mm(w, w_ref[own, :])
        w_ref[own, :] = done
        if k < n:
            u = mm(w, a_ref[own, :])
            a_ref[k:, :] -= mm(u[:, k:], u, ((0,), (0,)))
            w_ref[k:, :] -= mm(u[:, k:], done, ((0,), (0,)))


def factor_part(first, leaves, state, after=()):
    n = state[0].shape[0]
    skip = len(after)

    def kernel(*refs):
        factor_kernel(first, leaves, *refs[: len(state)], *refs[len(state) + skip :])

    return pl.pallas_call(
        kernel,
        out_shape=(jax.ShapeDtypeStruct((n, n), F32),) * 2,
        in_specs=[VMEM] * len(state) + [pl.BlockSpec(memory_space=pl.ANY)] * skip,
        out_specs=(VMEM,) * 2,
        compiler_params=params(),
        cost_estimate=cost(2 * n * n * n, 8 * n * n),
        name="factor",
    )(*state, *after)


def inverse_factor(gram):
    return factor_part(0, gram.shape[0] // LEAF, (gram,))[1]


def core_of(chip, group, count):
    behind = (group - chip + count) % count
    return jnp.where((behind == 1) | ((behind == 2) & (group > chip)), 0, 1)


TOP = 14.0
TAIL = 16


def block_kernel(after_ref, xt_ref, panel_ref, out_ref):
    del after_ref
    n = xt_ref.shape[0]
    block = jnp.dot(xt_ref[...], panel_ref[...], preferred_element_type=F32)
    peak = jnp.max(jnp.abs(block), axis=(0, 1), keepdims=True)
    exponent = jnp.ceil(jnp.log2(jnp.maximum(peak, 1e-30)))
    out_ref[0:n] = block * jnp.exp2(TOP - exponent)
    out_ref[n:] = jnp.broadcast_to(exponent, (TAIL, n))


def pair_block(after, xt, panel):
    n = xt.shape[0]
    return pl.pallas_call(
        block_kernel,
        out_shape=jax.ShapeDtypeStruct((n + TAIL, n), F32),
        in_specs=[pl.BlockSpec(memory_space=pl.ANY)] + [VMEM] * 2,
        out_specs=VMEM,
        compiler_params=params(),
        cost_estimate=cost(2 * n * n * xt.shape[1], 4 * n * n),
        name="block",
    )(after, xt, panel)


def total_kernel(after_ref, *refs):
    del after_ref
    parts, (value_ref, packed_ref) = refs[:-2], refs[-2:]
    n = value_ref.shape[0]
    exponents = [part[n : n + 1] for part in parts]
    value = parts[0][0:n] * jnp.exp2(exponents[0] - TOP)
    for part, exponent in zip(parts[1:], exponents[1:]):
        value = value + part[0:n] * jnp.exp2(exponent - TOP)
    exponent = functools.reduce(jnp.maximum, exponents) + 2.0
    value_ref[...] = value
    packed_ref[0:n] = value * jnp.exp2(TOP - exponent)
    packed_ref[n:] = jnp.broadcast_to(exponent, (TAIL, n))


def total(after, parts):
    n = parts[0].shape[1]
    value, packed = pl.pallas_call(
        total_kernel,
        out_shape=(jax.ShapeDtypeStruct((n, n), F32), jax.ShapeDtypeStruct((n + TAIL, n), F32)),
        in_specs=[pl.BlockSpec(memory_space=pl.ANY)] + [VMEM] * len(parts),
        out_specs=(VMEM,) * 2,
        compiler_params=params(),
        name="total",
    )(after, *[part.astype(F32) for part in parts])
    return value, packed.astype(jnp.float16)


def merge_kernel(pos_ref, after_ref, *refs):
    del after_ref
    sums, (mine_ref, sib_ref, top_ref, t_ref) = refs[:4], refs[4:]
    n = t_ref.shape[0] - 8
    half = n // 2
    chip, group, core = pos_ref[0], pos_ref[1], pos_ref[2]

    def put(own_ref, cross_ref):
        t_ref[0:n] = own_ref[...].T + cross_ref[0:n] * jnp.exp2(cross_ref[n : n + 1] - TOP)

    distant = jnp.abs(chip - group) == 2
    pl.when(jnp.logical_not(distant))(lambda: put(*sums[:2]))
    pl.when(distant)(lambda: put(*sums[2:]))
    top_ref[...] = t_ref[0:8]
    mine_ref[...] = t_ref[pl.ds(pl.multiple_of(core * half, 8), half + 8)]
    sib_ref[...] = t_ref[pl.ds(pl.multiple_of((1 - core) * half, 8), half + 8)]


def merge(pos, after, near, far):
    n = near[0].shape[0]
    half = n // 2
    return pl.pallas_call(
        merge_kernel,
        out_shape=tuple(jax.ShapeDtypeStruct((r, n), F32) for r in (half + 8, half + 8, 8)),
        in_specs=[SMEM, pl.BlockSpec(memory_space=pl.ANY)] + [VMEM] * 4,
        out_specs=(VMEM,) * 3,
        scratch_shapes=[pltpu.VMEM((n + 8, n), F32)],
        compiler_params=params(),
        name="merge",
    )(pos, after, *near, *far)


def tiles_kernel(pos_ref, w_ref, g_ref, own_ref, sib_ref, top_ref, out_ref, p_ref):
    chip, group, core, count = pos_ref[0], pos_ref[1], pos_ref[2], pos_ref[3]
    half = out_ref.shape[1]
    following = jnp.where(chip + 1 == count, 0, chip + 1)
    owner = core_of(chip, group, count)

    @pl.when(chip == group)
    def _():
        p_ref[0:half] = g_ref[pl.ds(pl.multiple_of(core * half, 8), half)]
        p_ref[half:] = g_ref[half : half + 8]

    @pl.when(chip != group)
    def _():
        p_ref[...] = jnp.where(core == owner, own_ref[...], sib_ref[...])

    @pl.when(core != 0)
    def _():
        p_ref[half:] = jnp.where(following == group, g_ref[0:8], top_ref[...])

    shifted = pltpu.roll(p_ref[...], half + 7, 0)[:half]
    out_ref[...] = mm(w_ref[...], shifted, ((1,), (1,)))


def tiles(pos, w, gram, slabs):
    n = w.shape[0]
    half = n // 2
    return pl.pallas_call(
        tiles_kernel,
        out_shape=jax.ShapeDtypeStruct((n, half), F32),
        in_specs=[SMEM] + [VMEM] * 5,
        out_specs=VMEM,
        scratch_shapes=[pltpu.VMEM((half + 8, n), F32)],
        compiler_params=params(),
        name="tiles",
    )(pos, w, gram, *slabs)


def start(velocity, metric, packed):
    count = lax.axis_size("space")
    space, group = lax.axis_index("space"), lax.axis_index("tm")
    odd = space % 2
    pos = jnp.stack([space // 2, group, odd, lax.axis_size("tm")]).astype(jnp.int32)
    head, tail = velocity[:, :1], velocity[:, -1:]
    inside = [(i, i ^ 1) for i in range(count)]
    outside = [(i, i + 1) for i in range(1, count - 1, 2)]
    outside += [(j, i) for i, j in outside]
    far = lax.ppermute(jnp.where(odd == 0, head, tail), "space", outside)
    near = lax.ppermute(jnp.where(odd == 0, tail, head), "space", inside)
    column = metric.reshape(-1, 1)
    return pos, panel(pos, interior(velocity, column), near, far, column, packed)


def paired_body(velocity, metric):
    groups = lax.axis_size("tm")
    axes = ("space", "tm")
    every = range(groups)
    cores = (0, 1)

    def at(chip, group, core):
        return (2 * chip + core) * groups + group

    def send(value, pairs):
        return lax.ppermute(value, axes, pairs)

    pos, (x, xt, away, mine) = start(velocity, metric, True)

    def hops(sources):
        pairs = [(at(k, z, 0), at(k, (z + 1) % groups, 0)) for k in every for z in sources]
        return pairs + [(at(k, 3 - z, 1), at(k, (2 - z) % groups, 1)) for k in every for z in sources]

    near = send(x, hops(every))

    siblings = [(at(k, z, c), at(k, z, 1 - c)) for k in every for z in every for c in cores]
    mine = mine + send(away, siblings)
    others = [
        send(mine, [(at(k, z, c), at(k ^ m, z, c)) for k in every for z in every for c in cores])
        for m in range(1, groups)
    ]
    for other in others:
        mine = mine + other
    gram = gather_gram(pos, mine, send(mine, siblings))
    state = factor_part(0, 1, (gram,))
    near = passed(near, state[0])
    far = send(near, hops((1, 2)))

    def holder(k, z):
        return 0 if (z - k) % groups == 1 or z - k == 2 else 1

    homes = {(k, z): (k, z, holder(k, z)) for k in every for z in every if k != z}
    far_homes = {pair: home for pair, home in homes.items() if abs(pair[0] - pair[1]) == 2}
    near_homes = {pair: home for pair, home in homes.items() if pair not in far_homes}

    def gathered(block, group_homes):
        half = block.astype(jnp.float16)
        return [block] + [
            send(half, [(at(k ^ m, z, c), at(k, z, c)) for k, z, c in group_homes.values()]) for m in range(1, groups)
        ]

    def exchanged(packed, group_homes):
        received = send(packed, [(at(*home), at(*homes[z, k])) for (k, z), home in group_homes.items()])
        return received.astype(F32)

    near_block = pair_block(state[0], xt, near)
    near_parts = gathered(near_block, near_homes)
    state = factor_part(1, 1, state, (near_block,))
    far_block = pair_block(state[0], xt, far)
    far_parts = gathered(far_block, far_homes)
    state = factor_part(2, 1, state, (far_block,))
    near_own, packed = total(state[0], near_parts)
    near_cross = exchanged(packed, near_homes)
    far_own, packed = total(state[0], far_parts)
    far_cross = exchanged(packed, far_homes)
    w = factor_part(3, 1, state, (far_own,))[1]
    mine, sib, top = merge(pos, w, (near_own, near_cross), (far_own, far_cross))
    sib = send(sib, [(at(k, z, c), at(k, z, 1 - c)) for k, z, c in homes.values()])
    top = send(top, [(at(k, z, c), at((k - 1) % groups, z, 1)) for k, z, c in homes.values()])
    return tiles(pos, w, gram, (mine, sib, top))


def general_body(velocity, metric):
    _, (x, xt, gram) = start(velocity, metric, False)
    w = inverse_factor(lax.psum(gram, "space"))
    count = lax.axis_size("tm")
    following = lax.ppermute(x[:, :1], "tm", [(i, (i - 1) % count) for i in range(count)])
    shifted = jnp.concatenate([x[:, 1:], following], axis=1)
    gathered = lax.all_gather(shifted, "tm", axis=1, tiled=True)
    partial = jnp.dot(xt, gathered, preferred_element_type=F32)
    summed = lax.psum_scatter(partial, "space", scatter_dimension=1, tiled=True)
    return mm(w, summed)


def solution(mesh):
    groups = mesh.shape["tm"]
    paired = groups == 4 and mesh.shape["space"] == 8
    return jax.shard_map(
        paired_body if paired else general_body,
        mesh=mesh,
        in_specs=(P(None, "space", "tm"), P("space")),
        out_specs=P("tm", "space"),
        check_vma=False,
    )
```

```python
import functools

import jax
import jax.numpy as jnp
from jax import lax
from jax.experimental import pallas as pl
from jax.experimental.pallas import tpu as pltpu
from jax.sharding import PartitionSpec as P

F32 = jnp.float32
BF16 = jnp.bfloat16
HIGHEST = lax.Precision.HIGHEST
VMEM = pl.BlockSpec(memory_space=pltpu.VMEM)
SMEM = pl.BlockSpec(memory_space=pltpu.SMEM)
LEAF = 64
PIVOTS = 8


def params(mib=40):
    return pltpu.CompilerParams(vmem_limit_bytes=mib * 1024 * 1024)


def cost(flops, moved):
    return pl.CostEstimate(flops=flops, bytes_accessed=moved, transcendentals=0)


EDGE = 16


def combine(first, second, third, center0, center1):
    return third + center0 * second - center1 * first


def interior_kernel(vel_ref, met_ref, x_ref, head_ref, tail_ref):
    rows, cols = vel_ref.shape[1:]
    row = lax.broadcasted_iota(jnp.int32, (rows, cols), 0)
    metric = met_ref[...]

    def gradient(k):
        field = vel_ref[k].astype(F32)
        head_ref[k] = field[:8]
        tail_ref[k] = field[rows - 8 :]
        up = jnp.where(row == rows - 1, 0.0, pltpu.roll(field, rows - 1, 0))
        down = jnp.where(row == 0, 0.0, pltpu.roll(field, 1, 0))
        return metric * (up - down) * 0.5

    first = gradient(0)
    x_ref[0:rows] = first.astype(BF16)
    second = gradient(1)
    x_ref[rows : 2 * rows] = second.astype(BF16)
    third = combine(first, second, gradient(2), vel_ref[0].astype(F32), vel_ref[1].astype(F32))
    x_ref[2 * rows :] = third.astype(BF16)


def interior(velocity, metric):
    _, rows, cols = velocity.shape
    return pl.pallas_call(
        interior_kernel,
        out_shape=(
            jax.ShapeDtypeStruct((3 * rows, cols), BF16),
            jax.ShapeDtypeStruct((3, 8, cols), F32),
            jax.ShapeDtypeStruct((3, 8, cols), F32),
        ),
        in_specs=[VMEM] * 2,
        out_specs=(VMEM,) * 3,
        compiler_params=params(),
        cost_estimate=cost(30 * rows * cols, 12 * rows * cols),
        name="interior",
    )(velocity, metric)


def panel_kernel(pos_ref, x_in_ref, head_ref, tail_ref, near_ref, far_ref, met_ref, x_ref, xt_ref, *g_refs):
    cols = x_ref.shape[1]
    rows = x_ref.shape[0] // 3
    even = pos_ref[2] == 0
    row = lax.broadcasted_iota(jnp.int32, (EDGE, cols), 0)

    def edge(start, gradient, heads, at):
        first, second, third = [gradient(k) for k in range(3)]
        third = combine(first, second, third, heads[0], heads[1])
        for k, value in enumerate((first, second, third)):
            span = slice(k * rows + start, k * rows + start + EDGE)
            kept = x_in_ref[span].astype(F32)
            x_ref[span] = jnp.where(row == at, value, kept).astype(BF16)

    x_ref[...] = x_in_ref[...]
    lo = [jnp.where(even, far_ref[k].astype(F32), near_ref[k].astype(F32)) for k in range(3)]
    hi = [jnp.where(even, near_ref[k].astype(F32), far_ref[k].astype(F32)) for k in range(3)]
    low = met_ref[0:1]
    edge(0, lambda k: low * (head_ref[k, 1:2] - lo[k]) * 0.5, [head_ref[k, 0:1] for k in range(2)], 0)
    high = met_ref[rows - 1 : rows]
    edge(rows - EDGE, lambda k: high * (hi[k] - tail_ref[k, 6:7]) * 0.5, [tail_ref[k, 7:8] for k in range(2)], EDGE - 1)
    xt_ref[...] = x_ref[...].T
    gram = jnp.dot(xt_ref[...], x_ref[...], preferred_element_type=F32)
    if len(g_refs) == 1:
        g_refs[0][...] = gram
        return
    away_ref, mine_ref, g_ref = g_refs
    g_ref[...] = gram
    half = cols // 2
    for ref, core in ((mine_ref, pos_ref[2]), (away_ref, 1 - pos_ref[2])):
        ref[0:half] = jnp.where(core == 0, g_ref[0:half, 0:half], g_ref[half:, half:])
        ref[half:] = jnp.where(core == 0, g_ref[half : half + half // 2, 0:half], g_ref[half + half // 2 :, 0:half])


def panel(pos, inner, near, far, metric, packed):
    x, head, tail = inner
    height, cols = x.shape
    share = jax.ShapeDtypeStruct((3 * cols // 4, cols // 2), F32)
    whole = jax.ShapeDtypeStruct((cols, cols), F32)
    grams = (share, share) if packed else (whole,)
    return pl.pallas_call(
        panel_kernel,
        out_shape=(jax.ShapeDtypeStruct((height, cols), BF16), jax.ShapeDtypeStruct((cols, height), BF16)) + grams,
        in_specs=[SMEM] + [VMEM] * 6,
        out_specs=(VMEM,) * (2 + len(grams)),
        scratch_shapes=[pltpu.VMEM((cols, cols), F32)] if packed else [],
        compiler_params=params(),
        cost_estimate=cost(2 * height * cols * cols, 6 * height * cols),
        name="panel",
    )(pos, x, head, tail, near, far, metric)


def gather_kernel(pos_ref, mine_ref, theirs_ref, g_ref):
    half = mine_ref.shape[1]
    even = pos_ref[2] == 0
    first = jnp.where(even, mine_ref[...], theirs_ref[...])
    second = jnp.where(even, theirs_ref[...], mine_ref[...])
    g_ref[0:half, 0:half] = first[:half]
    g_ref[half:, half:] = second[:half]
    across = jnp.concatenate([first[half:], second[half:]], axis=0)
    g_ref[half:, 0:half] = across
    g_ref[0:half, half:] = across.T


def gather_gram(pos, mine, theirs):
    n = 2 * mine.shape[1]
    return pl.pallas_call(
        gather_kernel,
        out_shape=jax.ShapeDtypeStruct((n, n), F32),
        in_specs=[SMEM, VMEM, VMEM],
        out_specs=VMEM,
        compiler_params=params(),
        name="gather",
    )(pos, mine, theirs)


def passed(value, after):
    return pl.pallas_call(
        lambda *refs: None,
        out_shape=jax.ShapeDtypeStruct(value.shape, value.dtype),
        in_specs=[VMEM, VMEM],
        out_specs=VMEM,
        input_output_aliases={0: 0},
        compiler_params=params(),
        name="passed",
    )(value, after)


def leaf_inverse(block):
    n = block.shape[0]
    row = lax.broadcasted_iota(jnp.int32, (n, 2 * n), 0)
    lane = lax.broadcasted_iota(jnp.int32, (n, 2 * n), 1)
    eye = (row == lane).astype(F32)
    right = (lane == row + n).astype(F32)
    m = jnp.concatenate([block, right[:, n:]], axis=1)
    for j in range(0, n, PIVOTS):
        columns = [jnp.broadcast_to(m[:, j + b : j + b + 1], (n, 2 * n)) for b in range(PIVOTS)]
        pivot_rows = [m[j + a : j + a + 1, :] for a in range(PIVOTS)]
        splat = [[columns[b][j + a : j + a + 1, :] for b in range(PIVOTS)] for a in range(PIVOTS)]
        update = None
        inverses = []
        for a in range(PIVOTS):
            inverse = 1.0 / splat[a][a]
            for b in range(a + 1, PIVOTS):
                ratio = splat[a][b] * inverse
                for c in range(b, PIVOTS):
                    splat[b][c] = splat[b][c] - ratio * splat[a][c]
                pivot_rows[b] = pivot_rows[b] - ratio * pivot_rows[a]
            inverses.append(inverse)
        for a in range(PIVOTS):
            multiplier = jnp.where(row > j + a, columns[a] * inverses[a], 0.0)
            for b in range(a + 1, PIVOTS):
                columns[b] = columns[b] - multiplier * splat[a][b]
            term = multiplier * pivot_rows[a]
            update = term if update is None else update + term
        m = m - update
    diagonal = jnp.sum(m * eye, axis=1, keepdims=True)
    return m[:, n:] * lax.rsqrt(diagonal)


def mm(left, right, dims=((1,), (0,))):
    return lax.dot_general(left, right, (dims, ((), ())), precision=HIGHEST, preferred_element_type=F32)


def factor_kernel(first, leaves, *refs):
    g_ref, w_in_ref = (refs[0], None) if first == 0 else refs[:2]
    a_ref, w_ref = refs[-2:]
    n = g_ref.shape[0]
    a_ref[...] = g_ref[...]
    if first == 0:
        row = lax.broadcasted_iota(jnp.int32, (n, n), 0)
        lane = lax.broadcasted_iota(jnp.int32, (n, n), 1)
        w_ref[...] = (row == lane).astype(F32)
    else:
        w_ref[...] = w_in_ref[...]
    for leaf in range(first, first + leaves):
        j = leaf * LEAF
        k = j + LEAF
        own = slice(j, k)
        w = leaf_inverse(a_ref[own, own])
        done = mm(w, w_ref[own, :])
        w_ref[own, :] = done
        if k < n:
            u = mm(w, a_ref[own, :])
            a_ref[k:, :] -= mm(u[:, k:], u, ((0,), (0,)))
            w_ref[k:, :] -= mm(u[:, k:], done, ((0,), (0,)))


def factor_part(first, leaves, state, after=(), unit=False):
    n = state[0].shape[0]
    skip = len(after)

    def kernel(*refs):
        made = refs[len(state) + skip :]
        factor_kernel(first, leaves, *refs[: len(state)], *made[:2])
        if unit:
            made[2][...] = jnp.ones_like(made[2])

    return pl.pallas_call(
        kernel,
        out_shape=(jax.ShapeDtypeStruct((n, n), F32),) * 2 + (jax.ShapeDtypeStruct((8, n), F32),) * unit,
        in_specs=[VMEM] * len(state) + [pl.BlockSpec(memory_space=pl.ANY)] * skip,
        out_specs=(VMEM,) * (2 + unit),
        compiler_params=params(),
        cost_estimate=cost(2 * n * n * n, 8 * n * n),
        name="factor",
    )(*state, *after)


def inverse_factor(gram):
    return factor_part(0, gram.shape[0] // LEAF, (gram,))[1]


def core_of(chip, group, count):
    behind = (group - chip + count) % count
    return jnp.where((behind == 1) | ((behind == 2) & (group > chip)), 0, 1)


TOP = 14.0
TAIL = 16


def block_kernel(after_ref, xt_ref, panel_ref, out_ref):
    del after_ref
    n = xt_ref.shape[0]
    block = jnp.dot(xt_ref[...], panel_ref[...], preferred_element_type=F32)
    peak = jnp.max(jnp.abs(block), axis=(0, 1), keepdims=True)
    exponent = jnp.ceil(jnp.log2(jnp.maximum(peak, 1e-30)))
    out_ref[0:n] = block * jnp.exp2(TOP - exponent)
    out_ref[n:] = jnp.broadcast_to(exponent, (TAIL, n))


def pair_block(after, xt, panel):
    n = xt.shape[0]
    return pl.pallas_call(
        block_kernel,
        out_shape=jax.ShapeDtypeStruct((n + TAIL, n), F32),
        in_specs=[pl.BlockSpec(memory_space=pl.ANY)] + [VMEM] * 2,
        out_specs=VMEM,
        compiler_params=params(),
        cost_estimate=cost(2 * n * n * xt.shape[1], 4 * n * n),
        name="block",
    )(after, xt, panel)


def total_kernel(after_ref, *refs):
    del after_ref
    parts, (value_ref, packed_ref) = refs[:-2], refs[-2:]
    n = value_ref.shape[0]
    exponents = [part[n : n + 1] for part in parts]
    value = parts[0][0:n] * jnp.exp2(exponents[0] - TOP)
    for part, exponent in zip(parts[1:], exponents[1:]):
        value = value + part[0:n] * jnp.exp2(exponent - TOP)
    exponent = functools.reduce(jnp.maximum, exponents) + 2.0
    value_ref[...] = value
    packed_ref[0:n] = value * jnp.exp2(TOP - exponent)
    packed_ref[n:] = jnp.broadcast_to(exponent, (TAIL, n))


def total(after, parts):
    n = parts[0].shape[1]
    value, packed = pl.pallas_call(
        total_kernel,
        out_shape=(jax.ShapeDtypeStruct((n, n), F32), jax.ShapeDtypeStruct((n + TAIL, n), F32)),
        in_specs=[pl.BlockSpec(memory_space=pl.ANY)] + [VMEM] * len(parts),
        out_specs=(VMEM,) * 2,
        compiler_params=params(),
        name="total",
    )(after, *[part.astype(F32) for part in parts])
    return value, packed.astype(jnp.float16)


def merge_kernel(pos_ref, after_ref, *refs):
    del after_ref
    sums, (mine_ref, sib_ref, top_ref, t_ref) = refs[:4], refs[4:]
    n = t_ref.shape[0] - 8
    half = n // 2
    chip, group, core = pos_ref[0], pos_ref[1], pos_ref[2]

    def put(own_ref, cross_ref):
        t_ref[0:n] = own_ref[...].T + cross_ref[0:n] * jnp.exp2(cross_ref[n : n + 1] - TOP)

    distant = jnp.abs(chip - group) == 2
    pl.when(jnp.logical_not(distant))(lambda: put(*sums[:2]))
    pl.when(distant)(lambda: put(*sums[2:]))
    top_ref[...] = t_ref[0:8]
    mine_ref[...] = t_ref[pl.ds(pl.multiple_of(core * half, 8), half + 8)]
    sib_ref[...] = t_ref[pl.ds(pl.multiple_of((1 - core) * half, 8), half + 8)]


def merge(pos, after, near, far):
    n = near[0].shape[0]
    half = n // 2
    return pl.pallas_call(
        merge_kernel,
        out_shape=tuple(jax.ShapeDtypeStruct((r, n), F32) for r in (half + 8, half + 8, 8)),
        in_specs=[SMEM, pl.BlockSpec(memory_space=pl.ANY)] + [VMEM] * 4,
        out_specs=(VMEM,) * 3,
        scratch_shapes=[pltpu.VMEM((n + 8, n), F32)],
        compiler_params=params(),
        name="merge",
    )(pos, after, *near, *far)


def tiles_kernel(pos_ref, w_ref, g_ref, own_ref, sib_ref, top_ref, out_ref, p_ref):
    chip, group, core, count = pos_ref[0], pos_ref[1], pos_ref[2], pos_ref[3]
    half = out_ref.shape[1]
    following = jnp.where(chip + 1 == count, 0, chip + 1)
    owner = core_of(chip, group, count)

    @pl.when(chip == group)
    def _():
        p_ref[0:half] = g_ref[pl.ds(pl.multiple_of(core * half, 8), half)]
        p_ref[half:] = g_ref[half : half + 8]

    @pl.when(chip != group)
    def _():
        p_ref[...] = jnp.where(core == owner, own_ref[...], sib_ref[...])

    @pl.when(core != 0)
    def _():
        p_ref[half:] = jnp.where(following == group, g_ref[0:8], top_ref[...])

    shifted = pltpu.roll(p_ref[...], half + 7, 0)[:half]
    out_ref[...] = mm(w_ref[...], shifted, ((1,), (1,)))


def tiles(pos, w, gram, slabs):
    n = w.shape[0]
    half = n // 2
    return pl.pallas_call(
        tiles_kernel,
        out_shape=jax.ShapeDtypeStruct((n, half), F32),
        in_specs=[SMEM] + [VMEM] * 5,
        out_specs=VMEM,
        scratch_shapes=[pltpu.VMEM((half + 8, n), F32)],
        compiler_params=params(),
        name="tiles",
    )(pos, w, gram, *slabs)


def start(velocity, metric, packed):
    count = lax.axis_size("space")
    space, group = lax.axis_index("space"), lax.axis_index("tm")
    odd = space % 2
    pos = jnp.stack([space // 2, group, odd, lax.axis_size("tm")]).astype(jnp.int32)
    head, tail = velocity[:, :1], velocity[:, -1:]
    inside = [(i, i ^ 1) for i in range(count)]
    outside = [(i, i + 1) for i in range(1, count - 1, 2)]
    outside += [(j, i) for i, j in outside]
    far = lax.ppermute(jnp.where(odd == 0, head, tail), "space", outside)
    near = lax.ppermute(jnp.where(odd == 0, tail, head), "space", inside)
    column = metric.reshape(-1, 1)
    return pos, panel(pos, interior(velocity, column), near, far, column, packed)


def paired_body(velocity, metric):
    groups = lax.axis_size("tm")
    axes = ("space", "tm")
    every = range(groups)
    cores = (0, 1)

    def at(chip, group, core):
        return (2 * chip + core) * groups + group

    def send(value, pairs):
        return lax.ppermute(value, axes, pairs)

    pos, (x, xt, away, mine) = start(velocity, metric, True)

    def hops(sources):
        pairs = [(at(k, z, 0), at(k, (z + 1) % groups, 0)) for k in every for z in sources]
        return pairs + [(at(k, 3 - z, 1), at(k, (2 - z) % groups, 1)) for k in every for z in sources]

    near = send(x, hops(every))

    siblings = [(at(k, z, c), at(k, z, 1 - c)) for k in every for z in every for c in cores]
    mine = mine + send(away, siblings)
    others = [
        send(mine, [(at(k, z, c), at(k ^ m, z, c)) for k in every for z in every for c in cores])
        for m in range(1, groups)
    ]
    for other in others:
        mine = mine + other
    gram = gather_gram(pos, mine, send(mine, siblings))
    state = factor_part(0, 1, (gram,))
    near = passed(near, state[0])
    far = send(near, hops((1, 2)))

    def holder(k, z):
        return 0 if (z - k) % groups == 1 or z - k == 2 else 1

    homes = {(k, z): (k, z, holder(k, z)) for k in every for z in every if k != z}
    far_homes = {pair: home for pair, home in homes.items() if abs(pair[0] - pair[1]) == 2}
    near_homes = {pair: home for pair, home in homes.items() if pair not in far_homes}

    def gathered(block, group_homes):
        half = block.astype(jnp.float16)
        return [block] + [
            send(half, [(at(k ^ m, z, c), at(k, z, c)) for k, z, c in group_homes.values()]) for m in range(1, groups)
        ]

    def exchanged(packed, group_homes):
        return send(packed, [(at(*home), at(*homes[z, k])) for (k, z), home in group_homes.items()])

    near_block = pair_block(state[0], xt, near)
    near_parts = gathered(near_block, near_homes)
    state = factor_part(1, 1, state, (near_block,))
    far_block = pair_block(state[0], xt, far)
    far_parts = gathered(far_block, far_homes)
    state = factor_part(2, 1, state, (far_block,))
    near_own, packed = total(state[0], near_parts)
    near_cross = exchanged(packed, near_homes)
    far_own, packed = total(state[0], far_parts)
    far_cross = exchanged(packed, far_homes)
    _, w, unit = factor_part(3, 1, state, (far_own,), True)
    near_cross, far_cross = near_cross.astype(F32) * unit[0:1], far_cross.astype(F32)
    mine, sib, top = merge(pos, w, (near_own, near_cross), (far_own, far_cross))
    sib = send(sib, [(at(k, z, c), at(k, z, 1 - c)) for k, z, c in homes.values()])
    top = send(top, [(at(k, z, c), at((k - 1) % groups, z, 1)) for k, z, c in homes.values()])
    return tiles(pos, w, gram, (mine, sib, top))


def general_body(velocity, metric):
    _, (x, xt, gram) = start(velocity, metric, False)
    w = inverse_factor(lax.psum(gram, "space"))
    count = lax.axis_size("tm")
    following = lax.ppermute(x[:, :1], "tm", [(i, (i - 1) % count) for i in range(count)])
    shifted = jnp.concatenate([x[:, 1:], following], axis=1)
    gathered = lax.all_gather(shifted, "tm", axis=1, tiled=True)
    partial = jnp.dot(xt, gathered, preferred_element_type=F32)
    summed = lax.psum_scatter(partial, "space", scatter_dimension=1, tiled=True)
    return mm(w, summed)


def solution(mesh):
    groups = mesh.shape["tm"]
    paired = groups == 4 and mesh.shape["space"] == 8
    return jax.shard_map(
        paired_body if paired else general_body,
        mesh=mesh,
        in_specs=(P(None, "space", "tm"), P("space")),
        out_specs=P("tm", "space"),
        check_vma=False,
    )
```

```python
import functools

import jax
import jax.numpy as jnp
from jax import lax
from jax.experimental import pallas as pl
from jax.experimental.pallas import tpu as pltpu
from jax.sharding import PartitionSpec as P

F32 = jnp.float32
BF16 = jnp.bfloat16
HIGHEST = lax.Precision.HIGHEST
VMEM = pl.BlockSpec(memory_space=pltpu.VMEM)
SMEM = pl.BlockSpec(memory_space=pltpu.SMEM)
LEAF = 64
PIVOTS = 8


def params(mib=40):
    return pltpu.CompilerParams(vmem_limit_bytes=mib * 1024 * 1024)


def cost(flops, moved):
    return pl.CostEstimate(flops=flops, bytes_accessed=moved, transcendentals=0)


EDGE = 16


def combine(first, second, third, center0, center1):
    return third + center0 * second - center1 * first


def interior_kernel(vel_ref, met_ref, x_ref, head_ref, tail_ref):
    rows, cols = vel_ref.shape[1:]
    row = lax.broadcasted_iota(jnp.int32, (rows, cols), 0)
    metric = met_ref[...]

    def gradient(k):
        field = vel_ref[k].astype(F32)
        head_ref[k] = field[:8]
        tail_ref[k] = field[rows - 8 :]
        up = jnp.where(row == rows - 1, 0.0, pltpu.roll(field, rows - 1, 0))
        down = jnp.where(row == 0, 0.0, pltpu.roll(field, 1, 0))
        return metric * (up - down) * 0.5

    first = gradient(0)
    x_ref[0:rows] = first.astype(BF16)
    second = gradient(1)
    x_ref[rows : 2 * rows] = second.astype(BF16)
    third = combine(first, second, gradient(2), vel_ref[0].astype(F32), vel_ref[1].astype(F32))
    x_ref[2 * rows :] = third.astype(BF16)


def interior(velocity, metric):
    _, rows, cols = velocity.shape
    return pl.pallas_call(
        interior_kernel,
        out_shape=(
            jax.ShapeDtypeStruct((3 * rows, cols), BF16),
            jax.ShapeDtypeStruct((3, 8, cols), F32),
            jax.ShapeDtypeStruct((3, 8, cols), F32),
        ),
        in_specs=[VMEM] * 2,
        out_specs=(VMEM,) * 3,
        compiler_params=params(),
        cost_estimate=cost(30 * rows * cols, 12 * rows * cols),
        name="interior",
    )(velocity, metric)


def panel_kernel(pos_ref, x_in_ref, head_ref, tail_ref, near_ref, far_ref, met_ref, x_ref, xt_ref, *g_refs):
    cols = x_ref.shape[1]
    rows = x_ref.shape[0] // 3
    even = pos_ref[2] == 0
    row = lax.broadcasted_iota(jnp.int32, (EDGE, cols), 0)

    def edge(start, gradient, heads, at):
        first, second, third = [gradient(k) for k in range(3)]
        third = combine(first, second, third, heads[0], heads[1])
        for k, value in enumerate((first, second, third)):
            span = slice(k * rows + start, k * rows + start + EDGE)
            kept = x_in_ref[span].astype(F32)
            x_ref[span] = jnp.where(row == at, value, kept).astype(BF16)

    x_ref[...] = x_in_ref[...]
    lo = [jnp.where(even, far_ref[k].astype(F32), near_ref[k].astype(F32)) for k in range(3)]
    hi = [jnp.where(even, near_ref[k].astype(F32), far_ref[k].astype(F32)) for k in range(3)]
    low = met_ref[0:1]
    edge(0, lambda k: low * (head_ref[k, 1:2] - lo[k]) * 0.5, [head_ref[k, 0:1] for k in range(2)], 0)
    high = met_ref[rows - 1 : rows]
    edge(rows - EDGE, lambda k: high * (hi[k] - tail_ref[k, 6:7]) * 0.5, [tail_ref[k, 7:8] for k in range(2)], EDGE - 1)
    xt_ref[...] = x_ref[...].T
    gram = jnp.dot(xt_ref[...], x_ref[...], preferred_element_type=F32)
    if len(g_refs) == 1:
        g_refs[0][...] = gram
        return
    away_ref, mine_ref, g_ref = g_refs
    g_ref[...] = gram
    half = cols // 2
    for ref, core in ((mine_ref, pos_ref[2]), (away_ref, 1 - pos_ref[2])):
        ref[0:half] = jnp.where(core == 0, g_ref[0:half, 0:half], g_ref[half:, half:])
        ref[half:] = jnp.where(core == 0, g_ref[half : half + half // 2, 0:half], g_ref[half + half // 2 :, 0:half])


def panel(pos, inner, near, far, metric, packed):
    x, head, tail = inner
    height, cols = x.shape
    share = jax.ShapeDtypeStruct((3 * cols // 4, cols // 2), F32)
    whole = jax.ShapeDtypeStruct((cols, cols), F32)
    grams = (share, share) if packed else (whole,)
    return pl.pallas_call(
        panel_kernel,
        out_shape=(jax.ShapeDtypeStruct((height, cols), BF16), jax.ShapeDtypeStruct((cols, height), BF16)) + grams,
        in_specs=[SMEM] + [VMEM] * 6,
        out_specs=(VMEM,) * (2 + len(grams)),
        scratch_shapes=[pltpu.VMEM((cols, cols), F32)] if packed else [],
        compiler_params=params(),
        cost_estimate=cost(2 * height * cols * cols, 6 * height * cols),
        name="panel",
    )(pos, x, head, tail, near, far, metric)


def gather_kernel(pos_ref, mine_ref, theirs_ref, g_ref):
    half = mine_ref.shape[1]
    even = pos_ref[2] == 0
    first = jnp.where(even, mine_ref[...], theirs_ref[...])
    second = jnp.where(even, theirs_ref[...], mine_ref[...])
    g_ref[0:half, 0:half] = first[:half]
    g_ref[half:, half:] = second[:half]
    across = jnp.concatenate([first[half:], second[half:]], axis=0)
    g_ref[half:, 0:half] = across
    g_ref[0:half, half:] = across.T


def gather_gram(pos, mine, theirs):
    n = 2 * mine.shape[1]
    return pl.pallas_call(
        gather_kernel,
        out_shape=jax.ShapeDtypeStruct((n, n), F32),
        in_specs=[SMEM, VMEM, VMEM],
        out_specs=VMEM,
        compiler_params=params(),
        name="gather",
    )(pos, mine, theirs)


def passed(value, after):
    return pl.pallas_call(
        lambda *refs: None,
        out_shape=jax.ShapeDtypeStruct(value.shape, value.dtype),
        in_specs=[VMEM, VMEM],
        out_specs=VMEM,
        input_output_aliases={0: 0},
        compiler_params=params(),
        name="passed",
    )(value, after)


def leaf_inverse(block):
    n = block.shape[0]
    row = lax.broadcasted_iota(jnp.int32, (n, 2 * n), 0)
    lane = lax.broadcasted_iota(jnp.int32, (n, 2 * n), 1)
    eye = (row == lane).astype(F32)
    right = (lane == row + n).astype(F32)
    m = jnp.concatenate([block, right[:, n:]], axis=1)
    for j in range(0, n, PIVOTS):
        columns = [jnp.broadcast_to(m[:, j + b : j + b + 1], (n, 2 * n)) for b in range(PIVOTS)]
        pivot_rows = [m[j + a : j + a + 1, :] for a in range(PIVOTS)]
        splat = [[columns[b][j + a : j + a + 1, :] for b in range(PIVOTS)] for a in range(PIVOTS)]
        update = None
        inverses = []
        for a in range(PIVOTS):
            inverse = 1.0 / splat[a][a]
            for b in range(a + 1, PIVOTS):
                ratio = splat[a][b] * inverse
                for c in range(b, PIVOTS):
                    splat[b][c] = splat[b][c] - ratio * splat[a][c]
                pivot_rows[b] = pivot_rows[b] - ratio * pivot_rows[a]
            inverses.append(inverse)
        for a in range(PIVOTS):
            multiplier = jnp.where(row > j + a, columns[a] * inverses[a], 0.0)
            for b in range(a + 1, PIVOTS):
                columns[b] = columns[b] - multiplier * splat[a][b]
            term = multiplier * pivot_rows[a]
            update = term if update is None else update + term
        m = m - update
    diagonal = jnp.sum(m * eye, axis=1, keepdims=True)
    return m[:, n:] * lax.rsqrt(diagonal)


def mm(left, right, dims=((1,), (0,))):
    return lax.dot_general(left, right, (dims, ((), ())), precision=HIGHEST, preferred_element_type=F32)


def factor_kernel(first, leaves, *refs):
    g_ref, w_in_ref = (refs[0], None) if first == 0 else refs[:2]
    a_ref, w_ref = refs[-2:]
    n = g_ref.shape[0]
    a_ref[...] = g_ref[...]
    if first == 0:
        row = lax.broadcasted_iota(jnp.int32, (n, n), 0)
        lane = lax.broadcasted_iota(jnp.int32, (n, n), 1)
        w_ref[...] = (row == lane).astype(F32)
    else:
        w_ref[...] = w_in_ref[...]
    for leaf in range(first, first + leaves):
        j = leaf * LEAF
        k = j + LEAF
        own = slice(j, k)
        w = leaf_inverse(a_ref[own, own])
        done = mm(w, w_ref[own, :])
        w_ref[own, :] = done
        if k < n:
            u = mm(w, a_ref[own, :])
            a_ref[k:, :] -= mm(u[:, k:], u, ((0,), (0,)))
            w_ref[k:, :] -= mm(u[:, k:], done, ((0,), (0,)))


def factor_part(first, leaves, state, after=()):
    n = state[0].shape[0]
    skip = len(after)

    def kernel(*refs):
        factor_kernel(first, leaves, *refs[: len(state)], *refs[len(state) + skip :])

    return pl.pallas_call(
        kernel,
        out_shape=(jax.ShapeDtypeStruct((n, n), F32),) * 2,
        in_specs=[VMEM] * len(state) + [pl.BlockSpec(memory_space=pl.ANY)] * skip,
        out_specs=(VMEM,) * 2,
        compiler_params=params(),
        cost_estimate=cost(2 * n * n * n, 8 * n * n),
        name="factor",
    )(*state, *after)


def inverse_factor(gram):
    return factor_part(0, gram.shape[0] // LEAF, (gram,))[1]


def core_of(chip, group, count):
    behind = (group - chip + count) % count
    return jnp.where((behind == 1) | ((behind == 2) & (group > chip)), 0, 1)


TOP = 14.0
TAIL = 16


def blocks_kernel(pos_ref, after_ref, xt_ref, near_ref, far_ref, *outs):
    del after_ref
    chip, group, core = pos_ref[0], pos_ref[1], pos_ref[2]
    count = len(outs)
    n = xt_ref.shape[0]
    for r, panel_ref in ((1, near_ref), (2, far_ref)):
        owner = (group + jnp.where(core == 0, count - r, r)) % count

        @pl.when((r == 1) | (core_of(owner, group, count) == core))
        def _(panel_ref=panel_ref, owner=owner):
            block = jnp.dot(xt_ref[...], panel_ref[...], preferred_element_type=F32)
            peak = jnp.max(jnp.abs(block), axis=(0, 1), keepdims=True)
            exponent = jnp.ceil(jnp.log2(jnp.maximum(peak, 1e-30)))
            scaled = block * jnp.exp2(TOP - exponent)
            for m in range(count):

                @pl.when(jnp.bitwise_xor(chip, m) == owner)
                def _(m=m):
                    outs[m][0:n] = scaled
                    outs[m][n:] = jnp.broadcast_to(exponent, (TAIL, n))


def blocks(pos, after, xt, near, far, count):
    n = xt.shape[0]
    return pl.pallas_call(
        blocks_kernel,
        out_shape=(jax.ShapeDtypeStruct((n + TAIL, n), F32),) * count,
        in_specs=[SMEM, pl.BlockSpec(memory_space=pl.ANY)] + [VMEM] * 3,
        out_specs=(VMEM,) * count,
        compiler_params=params(),
        cost_estimate=cost(2 * 2 * n * n * xt.shape[1], 4 * count * n * n),
        name="blocks",
    )(pos, after, xt, near, far)


def total_kernel(after_ref, *refs):
    del after_ref
    parts, (value_ref, packed_ref) = refs[:-2], refs[-2:]
    n = value_ref.shape[0]
    exponents = [part[n : n + 1] for part in parts]
    value = parts[0][0:n] * jnp.exp2(exponents[0] - TOP)
    for part, exponent in zip(parts[1:], exponents[1:]):
        value = value + part[0:n] * jnp.exp2(exponent - TOP)
    exponent = functools.reduce(jnp.maximum, exponents) + 2.0
    value_ref[...] = value
    packed_ref[0:n] = value * jnp.exp2(TOP - exponent)
    packed_ref[n:] = jnp.broadcast_to(exponent, (TAIL, n))


def total(after, parts):
    n = parts[0].shape[1]
    value, packed = pl.pallas_call(
        total_kernel,
        out_shape=(jax.ShapeDtypeStruct((n, n), F32), jax.ShapeDtypeStruct((n + TAIL, n), F32)),
        in_specs=[pl.BlockSpec(memory_space=pl.ANY)] + [VMEM] * len(parts),
        out_specs=(VMEM,) * 2,
        compiler_params=params(),
        name="total",
    )(after, *[part.astype(F32) for part in parts])
    return value, packed.astype(jnp.float16)


def merge_kernel(pos_ref, own_ref, cross_ref, mine_ref, sib_ref, top_ref, t_ref):
    n = own_ref.shape[0]
    half = n // 2
    t_ref[0:n] = own_ref[...].T + cross_ref[0:n] * jnp.exp2(cross_ref[n : n + 1] - TOP)
    core = pos_ref[2]
    top_ref[...] = t_ref[0:8]
    mine_ref[...] = t_ref[pl.ds(pl.multiple_of(core * half, 8), half + 8)]
    sib_ref[...] = t_ref[pl.ds(pl.multiple_of((1 - core) * half, 8), half + 8)]


def merge(pos, own, cross):
    n = own.shape[0]
    half = n // 2
    return pl.pallas_call(
        merge_kernel,
        out_shape=tuple(jax.ShapeDtypeStruct((r, n), F32) for r in (half + 8, half + 8, 8)),
        in_specs=[SMEM] + [VMEM] * 2,
        out_specs=(VMEM,) * 3,
        scratch_shapes=[pltpu.VMEM((n + 8, n), F32)],
        compiler_params=params(),
        name="merge",
    )(pos, own, cross)


def tiles_kernel(pos_ref, w_ref, g_ref, own_ref, sib_ref, top_ref, out_ref, p_ref):
    chip, group, core, count = pos_ref[0], pos_ref[1], pos_ref[2], pos_ref[3]
    half = out_ref.shape[1]
    following = jnp.where(chip + 1 == count, 0, chip + 1)
    owner = core_of(chip, group, count)

    @pl.when(chip == group)
    def _():
        p_ref[0:half] = g_ref[pl.ds(pl.multiple_of(core * half, 8), half)]
        p_ref[half:] = g_ref[half : half + 8]

    @pl.when(chip != group)
    def _():
        p_ref[...] = jnp.where(core == owner, own_ref[...], sib_ref[...])

    @pl.when(core != 0)
    def _():
        p_ref[half:] = jnp.where(following == group, g_ref[0:8], top_ref[...])

    shifted = pltpu.roll(p_ref[...], half + 7, 0)[:half]
    out_ref[...] = mm(w_ref[...], shifted, ((1,), (1,)))


def tiles(pos, w, gram, slabs):
    n = w.shape[0]
    half = n // 2
    return pl.pallas_call(
        tiles_kernel,
        out_shape=jax.ShapeDtypeStruct((n, half), F32),
        in_specs=[SMEM] + [VMEM] * 5,
        out_specs=VMEM,
        scratch_shapes=[pltpu.VMEM((half + 8, n), F32)],
        compiler_params=params(),
        name="tiles",
    )(pos, w, gram, *slabs)


def start(velocity, metric, packed):
    count = lax.axis_size("space")
    space, group = lax.axis_index("space"), lax.axis_index("tm")
    odd = space % 2
    pos = jnp.stack([space // 2, group, odd, lax.axis_size("tm")]).astype(jnp.int32)
    head, tail = velocity[:, :1], velocity[:, -1:]
    inside = [(i, i ^ 1) for i in range(count)]
    outside = [(i, i + 1) for i in range(1, count - 1, 2)]
    outside += [(j, i) for i, j in outside]
    far = lax.ppermute(jnp.where(odd == 0, head, tail), "space", outside)
    near = lax.ppermute(jnp.where(odd == 0, tail, head), "space", inside)
    column = metric.reshape(-1, 1)
    return pos, panel(pos, interior(velocity, column), near, far, column, packed)


def paired_body(velocity, metric):
    groups = lax.axis_size("tm")
    axes = ("space", "tm")
    every = range(groups)
    cores = (0, 1)

    def at(chip, group, core):
        return (2 * chip + core) * groups + group

    def send(value, pairs):
        return lax.ppermute(value, axes, pairs)

    pos, (x, xt, away, mine) = start(velocity, metric, True)

    def hops(sources):
        pairs = [(at(k, z, 0), at(k, (z + 1) % groups, 0)) for k in every for z in sources]
        return pairs + [(at(k, 3 - z, 1), at(k, (2 - z) % groups, 1)) for k in every for z in sources]

    near = send(x, hops(every))

    siblings = [(at(k, z, c), at(k, z, 1 - c)) for k in every for z in every for c in cores]
    mine = mine + send(away, siblings)
    others = [
        send(mine, [(at(k, z, c), at(k ^ m, z, c)) for k in every for z in every for c in cores])
        for m in range(1, groups)
    ]
    for other in others:
        mine = mine + other
    gram = gather_gram(pos, mine, send(mine, siblings))
    state = factor_part(0, 1, (gram,))
    near = passed(near, state[0])
    far = send(near, hops((1, 2)))

    def holder(k, z):
        return 0 if (z - k) % groups == 1 or z - k == 2 else 1

    homes = {(k, z): (k, z, holder(k, z)) for k in every for z in every if k != z}

    state = factor_part(1, 2, state)
    slots = blocks(pos, state[0], xt, near, far, groups)
    parts = [slots[0]] + [
        send(slots[m].astype(jnp.float16), [(at(k ^ m, z, c), at(k, z, c)) for k, z, c in homes.values()])
        for m in range(1, groups)
    ]
    w = factor_part(3, 1, state, (slots[0],))[1]
    own, packed = total(w, parts)
    cross = send(packed, [(at(*home), at(*homes[z, k])) for (k, z), home in homes.items()])
    mine, sib, top = merge(pos, own, cross.astype(F32))
    sib = send(sib, [(at(k, z, c), at(k, z, 1 - c)) for k, z, c in homes.values()])
    top = send(top, [(at(k, z, c), at((k - 1) % groups, z, 1)) for k, z, c in homes.values()])
    return tiles(pos, w, gram, (mine, sib, top))


def general_body(velocity, metric):
    _, (x, xt, gram) = start(velocity, metric, False)
    w = inverse_factor(lax.psum(gram, "space"))
    count = lax.axis_size("tm")
    following = lax.ppermute(x[:, :1], "tm", [(i, (i - 1) % count) for i in range(count)])
    shifted = jnp.concatenate([x[:, 1:], following], axis=1)
    gathered = lax.all_gather(shifted, "tm", axis=1, tiled=True)
    partial = jnp.dot(xt, gathered, preferred_element_type=F32)
    summed = lax.psum_scatter(partial, "space", scatter_dimension=1, tiled=True)
    return mm(w, summed)


def solution(mesh):
    groups = mesh.shape["tm"]
    paired = groups == 4 and mesh.shape["space"] == 8
    return jax.shard_map(
        paired_body if paired else general_body,
        mesh=mesh,
        in_specs=(P(None, "space", "tm"), P("space")),
        out_specs=P("tm", "space"),
        check_vma=False,
    )
```

```python
import functools

import jax
import jax.numpy as jnp
from jax import lax
from jax.experimental import pallas as pl
from jax.experimental.pallas import tpu as pltpu
from jax.sharding import PartitionSpec as P

F32 = jnp.float32
BF16 = jnp.bfloat16
HIGHEST = lax.Precision.HIGHEST
VMEM = pl.BlockSpec(memory_space=pltpu.VMEM)
SMEM = pl.BlockSpec(memory_space=pltpu.SMEM)
LEAF = 64
PIVOTS = 8


def params(mib=40):
    return pltpu.CompilerParams(vmem_limit_bytes=mib * 1024 * 1024)


def cost(flops, moved):
    return pl.CostEstimate(flops=flops, bytes_accessed=moved, transcendentals=0)


EDGE = 16


def combine(first, second, third, center0, center1):
    return third + center0 * second - center1 * first


def interior_kernel(vel_ref, met_ref, x_ref, head_ref, tail_ref):
    rows, cols = vel_ref.shape[1:]
    row = lax.broadcasted_iota(jnp.int32, (rows, cols), 0)
    metric = met_ref[...]

    def gradient(k):
        field = vel_ref[k].astype(F32)
        head_ref[k] = field[:8]
        tail_ref[k] = field[rows - 8 :]
        up = jnp.where(row == rows - 1, 0.0, pltpu.roll(field, rows - 1, 0))
        down = jnp.where(row == 0, 0.0, pltpu.roll(field, 1, 0))
        return metric * (up - down) * 0.5

    first = gradient(0)
    x_ref[0:rows] = first.astype(BF16)
    second = gradient(1)
    x_ref[rows : 2 * rows] = second.astype(BF16)
    third = combine(first, second, gradient(2), vel_ref[0].astype(F32), vel_ref[1].astype(F32))
    x_ref[2 * rows :] = third.astype(BF16)


def interior(velocity, metric):
    _, rows, cols = velocity.shape
    return pl.pallas_call(
        interior_kernel,
        out_shape=(
            jax.ShapeDtypeStruct((3 * rows, cols), BF16),
            jax.ShapeDtypeStruct((3, 8, cols), F32),
            jax.ShapeDtypeStruct((3, 8, cols), F32),
        ),
        in_specs=[VMEM] * 2,
        out_specs=(VMEM,) * 3,
        compiler_params=params(),
        cost_estimate=cost(30 * rows * cols, 12 * rows * cols),
        name="interior",
    )(velocity, metric)


def edges_kernel(pos_ref, x_in_ref, head_ref, tail_ref, near_ref, far_ref, met_ref, x_ref):
    cols = x_ref.shape[1]
    rows = x_ref.shape[0] // 3
    even = pos_ref[2] == 0
    row = lax.broadcasted_iota(jnp.int32, (EDGE, cols), 0)

    def edge(start, gradient, heads, at):
        first, second, third = [gradient(k) for k in range(3)]
        third = combine(first, second, third, heads[0], heads[1])
        for k, value in enumerate((first, second, third)):
            span = slice(k * rows + start, k * rows + start + EDGE)
            kept = x_ref[span].astype(F32)
            x_ref[span] = jnp.where(row == at, value, kept).astype(BF16)

    del x_in_ref
    lo = [jnp.where(even, far_ref[k].astype(F32), near_ref[k].astype(F32)) for k in range(3)]
    hi = [jnp.where(even, near_ref[k].astype(F32), far_ref[k].astype(F32)) for k in range(3)]
    low = met_ref[0:1]
    edge(0, lambda k: low * (head_ref[k, 1:2] - lo[k]) * 0.5, [head_ref[k, 0:1] for k in range(2)], 0)
    high = met_ref[rows - 1 : rows]
    edge(rows - EDGE, lambda k: high * (hi[k] - tail_ref[k, 6:7]) * 0.5, [tail_ref[k, 7:8] for k in range(2)], EDGE - 1)


def panel_kernel(pos_ref, x_ref, xt_ref, *g_refs):
    xt_ref[...] = x_ref[...].T
    gram = jnp.dot(xt_ref[...], x_ref[...], preferred_element_type=F32)
    if len(g_refs) == 1:
        g_refs[0][...] = gram
        return
    away_ref, mine_ref, g_ref = g_refs
    g_ref[...] = gram
    cols = x_ref.shape[1]
    half = cols // 2
    for ref, core in ((mine_ref, pos_ref[2]), (away_ref, 1 - pos_ref[2])):
        ref[0:half] = jnp.where(core == 0, g_ref[0:half, 0:half], g_ref[half:, half:])
        ref[half:] = jnp.where(core == 0, g_ref[half : half + half // 2, 0:half], g_ref[half + half // 2 :, 0:half])


def edges(pos, inner, near, far, metric):
    x, head, tail = inner
    return pl.pallas_call(
        edges_kernel,
        out_shape=jax.ShapeDtypeStruct(x.shape, BF16),
        in_specs=[SMEM] + [VMEM] * 6,
        out_specs=VMEM,
        input_output_aliases={1: 0},
        compiler_params=params(),
        name="edges",
    )(pos, x, head, tail, near, far, metric)


def panel(pos, x, packed):
    height, cols = x.shape
    share = jax.ShapeDtypeStruct((3 * cols // 4, cols // 2), F32)
    whole = jax.ShapeDtypeStruct((cols, cols), F32)
    grams = (share, share) if packed else (whole,)
    return pl.pallas_call(
        panel_kernel,
        out_shape=(jax.ShapeDtypeStruct((cols, height), BF16),) + grams,
        in_specs=[SMEM, VMEM],
        out_specs=(VMEM,) * (1 + len(grams)),
        scratch_shapes=[pltpu.VMEM((cols, cols), F32)] if packed else [],
        compiler_params=params(),
        cost_estimate=cost(2 * height * cols * cols, 6 * height * cols),
        name="panel",
    )(pos, x)


def gather_kernel(pos_ref, mine_ref, theirs_ref, g_ref):
    half = mine_ref.shape[1]
    even = pos_ref[2] == 0
    first = jnp.where(even, mine_ref[...], theirs_ref[...])
    second = jnp.where(even, theirs_ref[...], mine_ref[...])
    g_ref[0:half, 0:half] = first[:half]
    g_ref[half:, half:] = second[:half]
    across = jnp.concatenate([first[half:], second[half:]], axis=0)
    g_ref[half:, 0:half] = across
    g_ref[0:half, half:] = across.T


def gather_gram(pos, mine, theirs):
    n = 2 * mine.shape[1]
    return pl.pallas_call(
        gather_kernel,
        out_shape=jax.ShapeDtypeStruct((n, n), F32),
        in_specs=[SMEM, VMEM, VMEM],
        out_specs=VMEM,
        compiler_params=params(),
        name="gather",
    )(pos, mine, theirs)


def passed(value, after):
    return pl.pallas_call(
        lambda *refs: None,
        out_shape=jax.ShapeDtypeStruct(value.shape, value.dtype),
        in_specs=[VMEM, VMEM],
        out_specs=VMEM,
        input_output_aliases={0: 0},
        compiler_params=params(),
        name="passed",
    )(value, after)


def leaf_inverse(block):
    n = block.shape[0]
    row = lax.broadcasted_iota(jnp.int32, (n, 2 * n), 0)
    lane = lax.broadcasted_iota(jnp.int32, (n, 2 * n), 1)
    eye = (row == lane).astype(F32)
    right = (lane == row + n).astype(F32)
    m = jnp.concatenate([block, right[:, n:]], axis=1)
    for j in range(0, n, PIVOTS):
        columns = [jnp.broadcast_to(m[:, j + b : j + b + 1], (n, 2 * n)) for b in range(PIVOTS)]
        pivot_rows = [m[j + a : j + a + 1, :] for a in range(PIVOTS)]
        splat = [[columns[b][j + a : j + a + 1, :] for b in range(PIVOTS)] for a in range(PIVOTS)]
        update = None
        inverses = []
        for a in range(PIVOTS):
            inverse = 1.0 / splat[a][a]
            for b in range(a + 1, PIVOTS):
                ratio = splat[a][b] * inverse
                for c in range(b, PIVOTS):
                    splat[b][c] = splat[b][c] - ratio * splat[a][c]
                pivot_rows[b] = pivot_rows[b] - ratio * pivot_rows[a]
            inverses.append(inverse)
        for a in range(PIVOTS):
            multiplier = jnp.where(row > j + a, columns[a] * inverses[a], 0.0)
            for b in range(a + 1, PIVOTS):
                columns[b] = columns[b] - multiplier * splat[a][b]
            term = multiplier * pivot_rows[a]
            update = term if update is None else update + term
        m = m - update
    diagonal = jnp.sum(m * eye, axis=1, keepdims=True)
    return m[:, n:] * lax.rsqrt(diagonal)


def mm(left, right, dims=((1,), (0,))):
    return lax.dot_general(left, right, (dims, ((), ())), precision=HIGHEST, preferred_element_type=F32)


def factor_kernel(first, leaves, *refs):
    g_ref, w_in_ref = (refs[0], None) if first == 0 else refs[:2]
    a_ref, w_ref = refs[-2:]
    n = g_ref.shape[0]
    a_ref[...] = g_ref[...]
    if first == 0:
        row = lax.broadcasted_iota(jnp.int32, (n, n), 0)
        lane = lax.broadcasted_iota(jnp.int32, (n, n), 1)
        w_ref[...] = (row == lane).astype(F32)
    else:
        w_ref[...] = w_in_ref[...]
    for leaf in range(first, first + leaves):
        j = leaf * LEAF
        k = j + LEAF
        own = slice(j, k)
        w = leaf_inverse(a_ref[own, own])
        done = mm(w, w_ref[own, :])
        w_ref[own, :] = done
        if k < n:
            u = mm(w, a_ref[own, :])
            a_ref[k:, :] -= mm(u[:, k:], u, ((0,), (0,)))
            w_ref[k:, :] -= mm(u[:, k:], done, ((0,), (0,)))


def halves(value):
    high = value.astype(BF16)
    return high, (value - high.astype(F32)).astype(BF16)


def factor_part(first, leaves, state, after=(), split=False):
    n = state[0].shape[0]
    skip = len(after)

    def kernel(*refs):
        made = refs[len(state) + skip :]
        factor_kernel(first, leaves, *refs[: len(state)], *made[-2:])
        if split:
            made[0][...], made[1][...] = halves(made[-1][...])

    return pl.pallas_call(
        kernel,
        out_shape=(jax.ShapeDtypeStruct((n, n), BF16 if split else F32),) * 2,
        in_specs=[VMEM] * len(state) + [pl.BlockSpec(memory_space=pl.ANY)] * skip,
        out_specs=(VMEM,) * 2,
        scratch_shapes=[pltpu.VMEM((n, n), F32)] * 2 if split else [],
        compiler_params=params(),
        cost_estimate=cost(2 * n * n * n, 8 * n * n),
        name="factor",
    )(*state, *after)


def inverse_factor(gram):
    return factor_part(0, gram.shape[0] // LEAF, (gram,))[1]


def core_of(chip, group, count):
    behind = (group - chip + count) % count
    return jnp.where((behind == 1) | ((behind == 2) & (group > chip)), 0, 1)


TOP = 14.0
TAIL = 16


def block_kernel(after_ref, xt_ref, panel_ref, out_ref):
    del after_ref
    n = xt_ref.shape[0]
    block = jnp.dot(xt_ref[...], panel_ref[...], preferred_element_type=F32)
    peak = jnp.max(jnp.abs(block), axis=(0, 1), keepdims=True)
    exponent = jnp.ceil(jnp.log2(jnp.maximum(peak, 1e-30)))
    out_ref[0:n] = block * jnp.exp2(TOP - exponent)
    out_ref[n:] = jnp.broadcast_to(exponent, (TAIL, n))


def pair_block(after, xt, panel):
    n = xt.shape[0]
    return pl.pallas_call(
        block_kernel,
        out_shape=jax.ShapeDtypeStruct((n + TAIL, n), F32),
        in_specs=[pl.BlockSpec(memory_space=pl.ANY)] + [VMEM] * 2,
        out_specs=VMEM,
        compiler_params=params(),
        cost_estimate=cost(2 * n * n * xt.shape[1], 4 * n * n),
        name="block",
    )(after, xt, panel)


def total_kernel(after_ref, *refs):
    del after_ref
    parts, (value_ref, packed_ref) = refs[:-2], refs[-2:]
    n = value_ref.shape[0]
    exponents = [part[n : n + 1] for part in parts]
    value = parts[0][0:n] * jnp.exp2(exponents[0] - TOP)
    for part, exponent in zip(parts[1:], exponents[1:]):
        value = value + part[0:n] * jnp.exp2(exponent - TOP)
    exponent = functools.reduce(jnp.maximum, exponents) + 2.0
    value_ref[...] = value
    packed_ref[0:n] = value * jnp.exp2(TOP - exponent)
    packed_ref[n:] = jnp.broadcast_to(exponent, (TAIL, n))


def total(after, parts):
    n = parts[0].shape[1]
    value, packed = pl.pallas_call(
        total_kernel,
        out_shape=(jax.ShapeDtypeStruct((n, n), F32), jax.ShapeDtypeStruct((n + TAIL, n), F32)),
        in_specs=[pl.BlockSpec(memory_space=pl.ANY)] + [VMEM] * len(parts),
        out_specs=(VMEM,) * 2,
        compiler_params=params(),
        name="total",
    )(after, *[part.astype(F32) for part in parts])
    return value, packed.astype(jnp.float16)


def merge_kernel(pos_ref, after_ref, *refs):
    del after_ref
    sums, (mine_ref, sib_ref, top_ref, t_ref) = refs[:4], refs[4:]
    n = t_ref.shape[0] - 8
    half = n // 2
    chip, group, core = pos_ref[0], pos_ref[1], pos_ref[2]

    def put(own_ref, cross_ref):
        t_ref[0:n] = own_ref[...].T + cross_ref[0:n] * jnp.exp2(cross_ref[n : n + 1] - TOP)

    distant = jnp.abs(chip - group) == 2
    pl.when(jnp.logical_not(distant))(lambda: put(*sums[:2]))
    pl.when(distant)(lambda: put(*sums[2:]))
    top_ref[...] = t_ref[0:8]
    mine_ref[...] = t_ref[pl.ds(pl.multiple_of(core * half, 8), half + 8)]
    sib_ref[...] = t_ref[pl.ds(pl.multiple_of((1 - core) * half, 8), half + 8)]


def merge(pos, after, near, far):
    n = near[0].shape[0]
    half = n // 2
    return pl.pallas_call(
        merge_kernel,
        out_shape=tuple(jax.ShapeDtypeStruct((r, n), F32) for r in (half + 8, half + 8, 8)),
        in_specs=[SMEM, pl.BlockSpec(memory_space=pl.ANY)] + [VMEM] * 4,
        out_specs=(VMEM,) * 3,
        scratch_shapes=[pltpu.VMEM((n + 8, n), F32)],
        compiler_params=params(),
        name="merge",
    )(pos, after, *near, *far)


def tiles_kernel(pos_ref, high_ref, low_ref, g_ref, own_ref, sib_ref, top_ref, out_ref, p_ref):
    chip, group, core, count = pos_ref[0], pos_ref[1], pos_ref[2], pos_ref[3]
    half = out_ref.shape[1]
    following = jnp.where(chip + 1 == count, 0, chip + 1)
    owner = core_of(chip, group, count)

    @pl.when(chip == group)
    def _():
        p_ref[0:half] = g_ref[pl.ds(pl.multiple_of(core * half, 8), half)]
        p_ref[half:] = g_ref[half : half + 8]

    @pl.when(chip != group)
    def _():
        p_ref[...] = jnp.where(core == owner, own_ref[...], sib_ref[...])

    @pl.when(core != 0)
    def _():
        p_ref[half:] = jnp.where(following == group, g_ref[0:8], top_ref[...])

    shifted = pltpu.roll(p_ref[...], half + 7, 0)[:half]
    high, low = halves(shifted)
    dims = (((1,), (1,)), ((), ()))
    product = functools.partial(lax.dot_general, dimension_numbers=dims, preferred_element_type=F32)
    out_ref[...] = product(high_ref[...], high) + (product(high_ref[...], low) + product(low_ref[...], high))


def tiles(pos, w, gram, slabs):
    n = gram.shape[0]
    half = n // 2
    return pl.pallas_call(
        tiles_kernel,
        out_shape=jax.ShapeDtypeStruct((n, half), F32),
        in_specs=[SMEM] + [VMEM] * 6,
        out_specs=VMEM,
        scratch_shapes=[pltpu.VMEM((half + 8, n), F32)],
        compiler_params=params(),
        name="tiles",
    )(pos, *w, gram, *slabs)


def start(velocity, metric, packed):
    count = lax.axis_size("space")
    space, group = lax.axis_index("space"), lax.axis_index("tm")
    odd = space % 2
    pos = jnp.stack([space // 2, group, odd, lax.axis_size("tm")]).astype(jnp.int32)
    head, tail = velocity[:, :1], velocity[:, -1:]
    inside = [(i, i ^ 1) for i in range(count)]
    outside = [(i, i + 1) for i in range(1, count - 1, 2)]
    outside += [(j, i) for i, j in outside]
    far = lax.ppermute(jnp.where(odd == 0, head, tail), "space", outside)
    near = lax.ppermute(jnp.where(odd == 0, tail, head), "space", inside)
    column = metric.reshape(-1, 1)
    x = edges(pos, interior(velocity, column), near, far, column)
    return pos, (x, *panel(pos, x, packed))


def paired_body(velocity, metric):
    groups = lax.axis_size("tm")
    axes = ("space", "tm")
    every = range(groups)
    cores = (0, 1)

    def at(chip, group, core):
        return (2 * chip + core) * groups + group

    def send(value, pairs):
        return lax.ppermute(value, axes, pairs)

    pos, (x, xt, away, mine) = start(velocity, metric, True)

    def hops(sources):
        pairs = [(at(k, z, 0), at(k, (z + 1) % groups, 0)) for k in every for z in sources]
        return pairs + [(at(k, 3 - z, 1), at(k, (2 - z) % groups, 1)) for k in every for z in sources]

    near = send(x, hops(every))

    siblings = [(at(k, z, c), at(k, z, 1 - c)) for k in every for z in every for c in cores]
    mine = mine + send(away, siblings)
    others = [
        send(mine, [(at(k, z, c), at(k ^ m, z, c)) for k in every for z in every for c in cores])
        for m in range(1, groups)
    ]
    for other in others:
        mine = mine + other
    gram = gather_gram(pos, mine, send(mine, siblings))
    state = factor_part(0, 1, (gram,))
    near = passed(near, state[0])
    far = send(near, hops((1, 2)))

    def holder(k, z):
        return 0 if (z - k) % groups == 1 or z - k == 2 else 1

    homes = {(k, z): (k, z, holder(k, z)) for k in every for z in every if k != z}
    far_homes = {pair: home for pair, home in homes.items() if abs(pair[0] - pair[1]) == 2}
    near_homes = {pair: home for pair, home in homes.items() if pair not in far_homes}

    def gathered(block, group_homes):
        half = block.astype(jnp.float16)
        return [block] + [
            send(half, [(at(k ^ m, z, c), at(k, z, c)) for k, z, c in group_homes.values()]) for m in range(1, groups)
        ]

    def exchanged(packed, group_homes):
        received = send(packed, [(at(*home), at(*homes[z, k])) for (k, z), home in group_homes.items()])
        return received.astype(F32)

    near_block = pair_block(state[0], xt, near)
    near_parts = gathered(near_block, near_homes)
    state = factor_part(1, 1, state, (near_block,))
    far_block = pair_block(state[0], xt, far)
    far_parts = gathered(far_block, far_homes)
    state = factor_part(2, 1, state, (far_block,))
    near_own, packed = total(state[0], near_parts)
    near_cross = exchanged(packed, near_homes)
    far_own, packed = total(state[0], far_parts)
    far_cross = exchanged(packed, far_homes)
    w = factor_part(3, 1, state, (far_own, near_cross), True)
    mine, sib, top = merge(pos, w[0], (near_own, near_cross), (far_own, far_cross))
    sib = send(sib, [(at(k, z, c), at(k, z, 1 - c)) for k, z, c in homes.values()])
    top = send(top, [(at(k, z, c), at((k - 1) % groups, z, 1)) for k, z, c in homes.values()])
    return tiles(pos, w, gram, (mine, sib, top))


def general_body(velocity, metric):
    _, (x, xt, gram) = start(velocity, metric, False)
    w = inverse_factor(lax.psum(gram, "space"))
    count = lax.axis_size("tm")
    following = lax.ppermute(x[:, :1], "tm", [(i, (i - 1) % count) for i in range(count)])
    shifted = jnp.concatenate([x[:, 1:], following], axis=1)
    gathered = lax.all_gather(shifted, "tm", axis=1, tiled=True)
    partial = jnp.dot(xt, gathered, preferred_element_type=F32)
    summed = lax.psum_scatter(partial, "space", scatter_dimension=1, tiled=True)
    return mm(w, summed)


def solution(mesh):
    groups = mesh.shape["tm"]
    paired = groups == 4 and mesh.shape["space"] == 8
    return jax.shard_map(
        paired_body if paired else general_body,
        mesh=mesh,
        in_specs=(P(None, "space", "tm"), P("space")),
        out_specs=P("tm", "space"),
        check_vma=False,
    )
```

```python
import functools

import jax
import jax.numpy as jnp
from jax import lax
from jax.experimental import pallas as pl
from jax.experimental.pallas import tpu as pltpu
from jax.sharding import PartitionSpec as P

F32 = jnp.float32
BF16 = jnp.bfloat16
HIGHEST = lax.Precision.HIGHEST
VMEM = pl.BlockSpec(memory_space=pltpu.VMEM)
SMEM = pl.BlockSpec(memory_space=pltpu.SMEM)
LEAF = 64
PIVOTS = 8


def params(mib=40):
    return pltpu.CompilerParams(vmem_limit_bytes=mib * 1024 * 1024)


def cost(flops, moved):
    return pl.CostEstimate(flops=flops, bytes_accessed=moved, transcendentals=0)


EDGE = 16


def combine(first, second, third, center0, center1):
    return third + center0 * second - center1 * first


def interior_kernel(vel_ref, met_ref, x_ref, head_ref, tail_ref):
    rows, cols = vel_ref.shape[1:]
    row = lax.broadcasted_iota(jnp.int32, (rows, cols), 0)
    metric = met_ref[...]

    def gradient(k):
        field = vel_ref[k].astype(F32)
        head_ref[k] = field[:8]
        tail_ref[k] = field[rows - 8 :]
        up = jnp.where(row == rows - 1, 0.0, pltpu.roll(field, rows - 1, 0))
        down = jnp.where(row == 0, 0.0, pltpu.roll(field, 1, 0))
        return metric * (up - down) * 0.5

    first = gradient(0)
    x_ref[0:rows] = first.astype(BF16)
    second = gradient(1)
    x_ref[rows : 2 * rows] = second.astype(BF16)
    third = combine(first, second, gradient(2), vel_ref[0].astype(F32), vel_ref[1].astype(F32))
    x_ref[2 * rows :] = third.astype(BF16)


def interior(velocity, metric):
    _, rows, cols = velocity.shape
    return pl.pallas_call(
        interior_kernel,
        out_shape=(
            jax.ShapeDtypeStruct((3 * rows, cols), BF16),
            jax.ShapeDtypeStruct((3, 8, cols), F32),
            jax.ShapeDtypeStruct((3, 8, cols), F32),
        ),
        in_specs=[VMEM] * 2,
        out_specs=(VMEM,) * 3,
        compiler_params=params(),
        cost_estimate=cost(30 * rows * cols, 12 * rows * cols),
        name="interior",
    )(velocity, metric)


def edges_kernel(pos_ref, x_in_ref, head_ref, tail_ref, near_ref, far_ref, met_ref, x_ref):
    cols = x_ref.shape[1]
    rows = x_ref.shape[0] // 3
    even = pos_ref[2] == 0
    row = lax.broadcasted_iota(jnp.int32, (EDGE, cols), 0)

    def edge(start, gradient, heads, at):
        first, second, third = [gradient(k) for k in range(3)]
        third = combine(first, second, third, heads[0], heads[1])
        for k, value in enumerate((first, second, third)):
            span = slice(k * rows + start, k * rows + start + EDGE)
            kept = x_ref[span].astype(F32)
            x_ref[span] = jnp.where(row == at, value, kept).astype(BF16)

    del x_in_ref
    lo = [jnp.where(even, far_ref[k].astype(F32), near_ref[k].astype(F32)) for k in range(3)]
    hi = [jnp.where(even, near_ref[k].astype(F32), far_ref[k].astype(F32)) for k in range(3)]
    low = met_ref[0:1]
    edge(0, lambda k: low * (head_ref[k, 1:2] - lo[k]) * 0.5, [head_ref[k, 0:1] for k in range(2)], 0)
    high = met_ref[rows - 1 : rows]
    edge(rows - EDGE, lambda k: high * (hi[k] - tail_ref[k, 6:7]) * 0.5, [tail_ref[k, 7:8] for k in range(2)], EDGE - 1)


def panel_kernel(pos_ref, x_ref, xt_ref, *g_refs):
    xt_ref[...] = x_ref[...].T
    gram = jnp.dot(xt_ref[...], x_ref[...], preferred_element_type=F32)
    if len(g_refs) == 1:
        g_refs[0][...] = gram
        return
    away_ref, mine_ref, g_ref = g_refs
    g_ref[...] = gram
    cols = x_ref.shape[1]
    half = cols // 2
    for ref, core in ((mine_ref, pos_ref[2]), (away_ref, 1 - pos_ref[2])):
        ref[0:half] = jnp.where(core == 0, g_ref[0:half, 0:half], g_ref[half:, half:])
        ref[half:] = jnp.where(core == 0, g_ref[half : half + half // 2, 0:half], g_ref[half + half // 2 :, 0:half])


def edges(pos, inner, near, far, metric):
    x, head, tail = inner
    return pl.pallas_call(
        edges_kernel,
        out_shape=jax.ShapeDtypeStruct(x.shape, BF16),
        in_specs=[SMEM] + [VMEM] * 6,
        out_specs=VMEM,
        input_output_aliases={1: 0},
        compiler_params=params(),
        name="edges",
    )(pos, x, head, tail, near, far, metric)


def panel(pos, x, packed):
    height, cols = x.shape
    share = jax.ShapeDtypeStruct((3 * cols // 4, cols // 2), F32)
    whole = jax.ShapeDtypeStruct((cols, cols), F32)
    grams = (share, share) if packed else (whole,)
    return pl.pallas_call(
        panel_kernel,
        out_shape=(jax.ShapeDtypeStruct((cols, height), BF16),) + grams,
        in_specs=[SMEM, VMEM],
        out_specs=(VMEM,) * (1 + len(grams)),
        scratch_shapes=[pltpu.VMEM((cols, cols), F32)] if packed else [],
        compiler_params=params(),
        cost_estimate=cost(2 * height * cols * cols, 6 * height * cols),
        name="panel",
    )(pos, x)


def gather_kernel(pos_ref, mine_ref, theirs_ref, g_ref):
    half = mine_ref.shape[1]
    even = pos_ref[2] == 0
    first = jnp.where(even, mine_ref[...], theirs_ref[...])
    second = jnp.where(even, theirs_ref[...], mine_ref[...])
    g_ref[0:half, 0:half] = first[:half]
    g_ref[half:, half:] = second[:half]
    across = jnp.concatenate([first[half:], second[half:]], axis=0)
    g_ref[half:, 0:half] = across
    g_ref[0:half, half:] = across.T


def gather_gram(pos, mine, theirs):
    n = 2 * mine.shape[1]
    return pl.pallas_call(
        gather_kernel,
        out_shape=jax.ShapeDtypeStruct((n, n), F32),
        in_specs=[SMEM, VMEM, VMEM],
        out_specs=VMEM,
        compiler_params=params(),
        name="gather",
    )(pos, mine, theirs)


def passed(value, after):
    return pl.pallas_call(
        lambda *refs: None,
        out_shape=jax.ShapeDtypeStruct(value.shape, value.dtype),
        in_specs=[VMEM, VMEM],
        out_specs=VMEM,
        input_output_aliases={0: 0},
        compiler_params=params(),
        name="passed",
    )(value, after)


def leaf_inverse(block):
    n = block.shape[0]
    row = lax.broadcasted_iota(jnp.int32, (n, 2 * n), 0)
    lane = lax.broadcasted_iota(jnp.int32, (n, 2 * n), 1)
    eye = (row == lane).astype(F32)
    right = (lane == row + n).astype(F32)
    m = jnp.concatenate([block, right[:, n:]], axis=1)
    for j in range(0, n, PIVOTS):
        columns = [jnp.broadcast_to(m[:, j + b : j + b + 1], (n, 2 * n)) for b in range(PIVOTS)]
        pivot_rows = [m[j + a : j + a + 1, :] for a in range(PIVOTS)]
        splat = [[columns[b][j + a : j + a + 1, :] for b in range(PIVOTS)] for a in range(PIVOTS)]
        update = None
        inverses = []
        for a in range(PIVOTS):
            inverse = 1.0 / splat[a][a]
            for b in range(a + 1, PIVOTS):
                ratio = splat[a][b] * inverse
                for c in range(b, PIVOTS):
                    splat[b][c] = splat[b][c] - ratio * splat[a][c]
                pivot_rows[b] = pivot_rows[b] - ratio * pivot_rows[a]
            inverses.append(inverse)
        for a in range(PIVOTS):
            multiplier = jnp.where(row > j + a, columns[a] * inverses[a], 0.0)
            for b in range(a + 1, PIVOTS):
                columns[b] = columns[b] - multiplier * splat[a][b]
            term = multiplier * pivot_rows[a]
            update = term if update is None else update + term
        m = m - update
    diagonal = jnp.sum(m * eye, axis=1, keepdims=True)
    return m[:, n:] * lax.rsqrt(diagonal)


def mm(left, right, dims=((1,), (0,))):
    return lax.dot_general(left, right, (dims, ((), ())), precision=HIGHEST, preferred_element_type=F32)


def factor_kernel(first, leaves, *refs):
    g_ref, w_in_ref = (refs[0], None) if first == 0 else refs[:2]
    a_ref, w_ref = refs[-2:]
    n = g_ref.shape[0]
    a_ref[...] = g_ref[...]
    if first == 0:
        row = lax.broadcasted_iota(jnp.int32, (n, n), 0)
        lane = lax.broadcasted_iota(jnp.int32, (n, n), 1)
        w_ref[...] = (row == lane).astype(F32)
    else:
        w_ref[...] = w_in_ref[...]
    for leaf in range(first, first + leaves):
        j = leaf * LEAF
        k = j + LEAF
        own = slice(j, k)
        w = leaf_inverse(a_ref[own, own])
        done = mm(w, w_ref[own, :])
        w_ref[own, :] = done
        if k < n:
            u = mm(w, a_ref[own, :])
            a_ref[k:, :] -= mm(u[:, k:], u, ((0,), (0,)))
            w_ref[k:, :] -= mm(u[:, k:], done, ((0,), (0,)))


def halves(value):
    high = value.astype(BF16)
    return high, (value - high.astype(F32)).astype(BF16)


def factor_part(first, leaves, state, after=(), split=False):
    n = state[0].shape[0]
    skip = len(after)

    def kernel(*refs):
        made = refs[len(state) + skip :]
        factor_kernel(first, leaves, *refs[: len(state)], *made[-2:])
        if split:
            made[0][...], made[1][...] = halves(made[-1][...])

    return pl.pallas_call(
        kernel,
        out_shape=(jax.ShapeDtypeStruct((n, n), BF16 if split else F32),) * 2,
        in_specs=[VMEM] * len(state) + [pl.BlockSpec(memory_space=pl.ANY)] * skip,
        out_specs=(VMEM,) * 2,
        scratch_shapes=[pltpu.VMEM((n, n), F32)] * 2 if split else [],
        compiler_params=params(),
        cost_estimate=cost(2 * n * n * n, 8 * n * n),
        name="factor",
    )(*state, *after)


def inverse_factor(gram):
    return factor_part(0, gram.shape[0] // LEAF, (gram,))[1]


def core_of(chip, group, count):
    behind = (group - chip + count) % count
    return jnp.where((behind == 1) | ((behind == 2) & (group > chip)), 0, 1)


TOP = 14.0
TAIL = 16


def block_kernel(after_ref, xt_ref, panel_ref, out_ref):
    del after_ref
    n = xt_ref.shape[0]
    block = jnp.dot(xt_ref[...], panel_ref[...], preferred_element_type=F32)
    peak = jnp.max(jnp.abs(block), axis=(0, 1), keepdims=True)
    exponent = jnp.ceil(jnp.log2(jnp.maximum(peak, 1e-30)))
    out_ref[0:n] = block * jnp.exp2(TOP - exponent)
    out_ref[n:] = jnp.broadcast_to(exponent, (TAIL, n))


def pair_block(after, xt, panel):
    n = xt.shape[0]
    return pl.pallas_call(
        block_kernel,
        out_shape=jax.ShapeDtypeStruct((n + TAIL, n), F32),
        in_specs=[pl.BlockSpec(memory_space=pl.ANY)] + [VMEM] * 2,
        out_specs=VMEM,
        compiler_params=params(),
        cost_estimate=cost(2 * n * n * xt.shape[1], 4 * n * n),
        name="block",
    )(after, xt, panel)


def total_kernel(after_ref, *refs):
    del after_ref
    parts, (value_ref, packed_ref) = refs[:-2], refs[-2:]
    n = value_ref.shape[0]
    exponents = [part[n : n + 1] for part in parts]
    value = parts[0][0:n] * jnp.exp2(exponents[0] - TOP)
    for part, exponent in zip(parts[1:], exponents[1:]):
        value = value + part[0:n] * jnp.exp2(exponent - TOP)
    exponent = functools.reduce(jnp.maximum, exponents) + 2.0
    value_ref[...] = value
    packed_ref[0:n] = value * jnp.exp2(TOP - exponent)
    packed_ref[n:] = jnp.broadcast_to(exponent, (TAIL, n))


def total(after, parts):
    n = parts[0].shape[1]
    value, packed = pl.pallas_call(
        total_kernel,
        out_shape=(jax.ShapeDtypeStruct((n, n), F32), jax.ShapeDtypeStruct((n + TAIL, n), F32)),
        in_specs=[pl.BlockSpec(memory_space=pl.ANY)] + [VMEM] * len(parts),
        out_specs=(VMEM,) * 2,
        compiler_params=params(),
        name="total",
    )(after, *[part.astype(F32) for part in parts])
    return value, packed.astype(jnp.float16)


def paired_sums(pos_ref, refs, put):
    distant = jnp.abs(pos_ref[0] - pos_ref[1]) == 2
    pl.when(jnp.logical_not(distant))(lambda: put(*refs[:2]))
    pl.when(distant)(lambda: put(*refs[2:4]))


def unscaled(ref, rows, n):
    return ref[0:rows] * jnp.exp2(ref[n : n + 1] - TOP)


def first_kernel(pos_ref, after_ref, *refs):
    del after_ref
    top_ref = refs[4]
    n = top_ref.shape[1]

    def put(own_ref, cross_ref):
        top_ref[...] = own_ref[:, 0:128].T[0:8] + unscaled(cross_ref, 8, n)

    paired_sums(pos_ref, refs, put)


def first_rows(pos, after, near, far):
    n = near[0].shape[0]
    return pl.pallas_call(
        first_kernel,
        out_shape=jax.ShapeDtypeStruct((8, n), F32),
        in_specs=[SMEM, pl.BlockSpec(memory_space=pl.ANY)] + [VMEM] * 4,
        out_specs=VMEM,
        compiler_params=params(),
        name="first",
    )(pos, after, *near, *far)


def merge_kernel(pos_ref, after_ref, *refs):
    del after_ref
    mine_ref, sib_ref, t_ref = refs[4:]
    n = t_ref.shape[0] - 8
    half = n // 2
    core = pos_ref[2]

    def put(own_ref, cross_ref):
        t_ref[0:n] = own_ref[...].T + unscaled(cross_ref, n, n)

    paired_sums(pos_ref, refs, put)
    mine_ref[...] = t_ref[pl.ds(pl.multiple_of(core * half, 8), half + 8)]
    sib_ref[...] = t_ref[pl.ds(pl.multiple_of((1 - core) * half, 8), half + 8)]


def merge(pos, after, near, far):
    n = near[0].shape[0]
    half = n // 2
    return pl.pallas_call(
        merge_kernel,
        out_shape=(jax.ShapeDtypeStruct((half + 8, n), F32),) * 2,
        in_specs=[SMEM, pl.BlockSpec(memory_space=pl.ANY)] + [VMEM] * 4,
        out_specs=(VMEM,) * 2,
        scratch_shapes=[pltpu.VMEM((n + 8, n), F32)],
        compiler_params=params(),
        name="merge",
    )(pos, after, *near, *far)


def tiles_kernel(pos_ref, high_ref, low_ref, g_ref, own_ref, sib_ref, top_ref, out_ref, p_ref):
    chip, group, core, count = pos_ref[0], pos_ref[1], pos_ref[2], pos_ref[3]
    half = out_ref.shape[1]
    following = jnp.where(chip + 1 == count, 0, chip + 1)
    owner = core_of(chip, group, count)

    @pl.when(chip == group)
    def _():
        p_ref[0:half] = g_ref[pl.ds(pl.multiple_of(core * half, 8), half)]
        p_ref[half:] = g_ref[half : half + 8]

    @pl.when(chip != group)
    def _():
        p_ref[...] = jnp.where(core == owner, own_ref[...], sib_ref[...])

    @pl.when(core != 0)
    def _():
        p_ref[half:] = jnp.where(following == group, g_ref[0:8], top_ref[...])

    shifted = pltpu.roll(p_ref[...], half + 7, 0)[:half]
    high, low = halves(shifted)
    dims = (((1,), (1,)), ((), ()))
    product = functools.partial(lax.dot_general, dimension_numbers=dims, preferred_element_type=F32)
    out_ref[...] = product(high_ref[...], high) + (product(high_ref[...], low) + product(low_ref[...], high))


def tiles(pos, w, gram, slabs):
    n = gram.shape[0]
    half = n // 2
    return pl.pallas_call(
        tiles_kernel,
        out_shape=jax.ShapeDtypeStruct((n, half), F32),
        in_specs=[SMEM] + [VMEM] * 6,
        out_specs=VMEM,
        scratch_shapes=[pltpu.VMEM((half + 8, n), F32)],
        compiler_params=params(),
        name="tiles",
    )(pos, *w, gram, *slabs)


def start(velocity, metric, packed):
    count = lax.axis_size("space")
    space, group = lax.axis_index("space"), lax.axis_index("tm")
    odd = space % 2
    pos = jnp.stack([space // 2, group, odd, lax.axis_size("tm")]).astype(jnp.int32)
    head, tail = velocity[:, :1], velocity[:, -1:]
    inside = [(i, i ^ 1) for i in range(count)]
    outside = [(i, i + 1) for i in range(1, count - 1, 2)]
    outside += [(j, i) for i, j in outside]
    far = lax.ppermute(jnp.where(odd == 0, head, tail), "space", outside)
    near = lax.ppermute(jnp.where(odd == 0, tail, head), "space", inside)
    column = metric.reshape(-1, 1)
    x = edges(pos, interior(velocity, column), near, far, column)
    return pos, (x, *panel(pos, x, packed))


def paired_body(velocity, metric):
    groups = lax.axis_size("tm")
    axes = ("space", "tm")
    every = range(groups)
    cores = (0, 1)

    def at(chip, group, core):
        return (2 * chip + core) * groups + group

    def send(value, pairs):
        return lax.ppermute(value, axes, pairs)

    pos, (x, xt, away, mine) = start(velocity, metric, True)

    def hops(sources):
        pairs = [(at(k, z, 0), at(k, (z + 1) % groups, 0)) for k in every for z in sources]
        return pairs + [(at(k, 3 - z, 1), at(k, (2 - z) % groups, 1)) for k in every for z in sources]

    near = send(x, hops(every))

    siblings = [(at(k, z, c), at(k, z, 1 - c)) for k in every for z in every for c in cores]
    mine = mine + send(away, siblings)
    others = [
        send(mine, [(at(k, z, c), at(k ^ m, z, c)) for k in every for z in every for c in cores])
        for m in range(1, groups)
    ]
    for other in others:
        mine = mine + other
    gram = gather_gram(pos, mine, send(mine, siblings))
    state = factor_part(0, 1, (gram,))
    near = passed(near, state[0])
    far = send(near, hops((1, 2)))

    def holder(k, z):
        return 0 if (z - k) % groups == 1 or z - k == 2 else 1

    homes = {(k, z): (k, z, holder(k, z)) for k in every for z in every if k != z}
    far_homes = {pair: home for pair, home in homes.items() if abs(pair[0] - pair[1]) == 2}
    near_homes = {pair: home for pair, home in homes.items() if pair not in far_homes}

    def gathered(block, group_homes):
        half = block.astype(jnp.float16)
        return [block] + [
            send(half, [(at(k ^ m, z, c), at(k, z, c)) for k, z, c in group_homes.values()]) for m in reversed(range(1, groups))
        ]

    def exchanged(packed, group_homes):
        received = send(packed, [(at(*home), at(*homes[z, k])) for (k, z), home in group_homes.items()])
        return received.astype(F32)

    near_block = pair_block(state[0], xt, near)
    near_parts = gathered(near_block, near_homes)
    state = factor_part(1, 1, state, (near_block,))
    far_block = pair_block(state[0], xt, far)
    far_parts = gathered(far_block, far_homes)
    state = factor_part(2, 1, state, (far_block,))
    near_own, packed = total(state[0], near_parts)
    near_cross = exchanged(packed, near_homes)
    far_own, packed = total(state[0], far_parts)
    far_cross = exchanged(packed, far_homes)
    w = factor_part(3, 1, state, (far_own, near_cross), True)
    near_pair, far_pair = (near_own, near_cross), (far_own, far_cross)
    top = first_rows(pos, w[0], near_pair, far_pair)
    mine, sib = merge(pos, top, near_pair, far_pair)
    sib = send(sib, [(at(k, z, c), at(k, z, 1 - c)) for k, z, c in homes.values()])
    top = send(top, [(at(k, z, c), at((k - 1) % groups, z, 1)) for k, z, c in homes.values()])
    return tiles(pos, w, gram, (mine, sib, top))


def general_body(velocity, metric):
    _, (x, xt, gram) = start(velocity, metric, False)
    w = inverse_factor(lax.psum(gram, "space"))
    count = lax.axis_size("tm")
    following = lax.ppermute(x[:, :1], "tm", [(i, (i - 1) % count) for i in range(count)])
    shifted = jnp.concatenate([x[:, 1:], following], axis=1)
    gathered = lax.all_gather(shifted, "tm", axis=1, tiled=True)
    partial = jnp.dot(xt, gathered, preferred_element_type=F32)
    summed = lax.psum_scatter(partial, "space", scatter_dimension=1, tiled=True)
    return mm(w, summed)


def solution(mesh):
    groups = mesh.shape["tm"]
    paired = groups == 4 and mesh.shape["space"] == 8
    return jax.shard_map(
        paired_body if paired else general_body,
        mesh=mesh,
        in_specs=(P(None, "space", "tm"), P("space")),
        out_specs=P("tm", "space"),
        check_vma=False,
    )
```
